256 devices in a mesh: wide: 32 (over x, z), narrow: 8 (over y, core).
Axes of the slice: x: 4, y: 4, z: 8, core: 2. Of those that a mesh axis runs over, the one named last changes fastest.
Arguments:
- embeddings: bfloat16 [131072, 1024], P('wide', 'narrow')
- centroids: bfloat16 [262144, 1024], P('wide', 'narrow')
- level2_cluster_index: int32 [512], P('wide'), may hold values from 0 to 16383, as said below
- child_lists: int32 [16384, 128], P('wide'), may hold values from 0 to 262143, as said below
Outputs:
- new_centroids: float32 [262144, 1024], P('wide', 'narrow')
The draws below stay inside these ranges and needn't reach their ends.
Inputs may be any that keep to these rules, and one draw needn't show every extreme that they name: `level2_cluster_index`: Level-2 cluster g belongs to group g // 512. Among the 16 blocks of one index of wide, at most 2 belong to clusters of one group. `child_lists`: the children of cluster g lie in (g // 512) * 8192 to (g // 512 + 1) * 8192 - 1; a list may name a centroid more than once.
All inputs are finite; a program needn't handle non-finite values.
Results may differ from the reference program's by a relative error of at most 0.0014.
Values may be sent and summed in bfloat16 or wider, within the bound.
A program may use at most 128 MiB of HBM per device.

```python
import math
import jax
import jax.numpy as jnp
from jax import lax

D = 1024
RB = 256
CH = 128
C1W = 8192
K2W = 512
BLK = 16
K1 = 262144
K2 = 16384
BLOCKS = 512
TOKENS = 131072
CAP = 2


def draw_centroids(key, part):
    key = jax.random.fold_in(key, 11)
    noise = jax.random.normal(key, (K1, D), jnp.float32)
    return noise.astype(jnp.bfloat16)


def draw_embeddings(key, part):
    key = jax.random.fold_in(key, 12)
    noise_key = jax.random.fold_in(key, 0)
    noise = jax.random.normal(noise_key, (TOKENS, D), jnp.float32)
    return noise.astype(jnp.bfloat16)


def draw_level2_cluster_index(key, part):
    key = jax.random.fold_in(key, 13)
    sources = BLOCKS // BLK
    hot_key, rest_key, cluster_key = jax.random.split(key, 3)
    hottest = jax.random.randint(hot_key, (), 0, sources)

    def one_source(source_key):
        perm_key, order_key = jax.random.split(source_key)
        others = (hottest + 1 + jnp.arange((sources - 1) * CAP, dtype=jnp.int32) // CAP) % sources
        others = jax.random.permutation(perm_key, others)
        owners = jnp.concatenate([jnp.full((CAP,), hottest, jnp.int32), others[:BLK - CAP]])
        return jax.random.permutation(order_key, owners)
    owners = jax.vmap(one_source)(jax.random.split(rest_key, sources)).reshape(-1)
    within = jax.random.randint(cluster_key, (BLOCKS,), 0, K2W)
    return (owners * K2W + within).astype(jnp.int32)


def draw_child_lists(key, part):
    key = jax.random.fold_in(key, 14)
    local = jax.random.randint(key, (K2, CH), 0, C1W)
    groups = jnp.arange(K2, dtype=jnp.int32)[:, None] // K2W
    return (groups * C1W + local).astype(jnp.int32)


def setup_inputs(seed: int = 0) -> dict:
    arg_keys = jax.random.split(jax.random.key(seed), 5)
    return {
        "embeddings": draw_embeddings(jax.random.fold_in(arg_keys[4], 71), 0),
        "centroids": draw_centroids(jax.random.fold_in(arg_keys[4], 71), 0),
        "level2_cluster_index": draw_level2_cluster_index(jax.random.fold_in(arg_keys[4], 71), 0),
        "child_lists": draw_child_lists(jax.random.fold_in(arg_keys[4], 71), 0),
    }


def block_terms(batch):
    rows, kids, embedding_table = batch
    cent = embedding_table.astype(jnp.float32)
    rows_f = rows.astype(jnp.float32)
    dot_products = jnp.einsum('grd,gcd->grc', rows_f, cent)
    lengths = lax.optimization_barrier(jnp.sum(cent * cent, axis=-1))
    score = (2.0 * dot_products - lengths[:, None, :]) * (1.0 / math.sqrt(D))
    soft_weight_matrix = jax.nn.softmax(score, axis=-1).astype(jnp.bfloat16)
    weights_f = soft_weight_matrix.astype(jnp.float32)
    block_weighted_totals = jnp.einsum('grc,grd->gcd', weights_f, rows_f)
    block_counts = lax.optimization_barrier(jnp.sum(weights_f, axis=1))
    return (block_weighted_totals, block_counts)

def reference(embeddings, centroids, level2_cluster_index, child_lists):
    group_size = 8
    batches = BLOCKS // group_size
    rows_all = embeddings.reshape(batches, group_size, RB, D)
    kids_all = child_lists[level2_cluster_index].astype(jnp.int32)

    def one_batch(index):
        rows = rows_all[index]
        kids = lax.dynamic_slice_in_dim(kids_all, index * group_size, group_size, 0)
        embedding_table = centroids[kids]
        return block_terms((rows, kids, embedding_table))
    block_weighted_totals, block_counts = lax.map(one_batch, jnp.arange(batches, dtype=jnp.int32))
    flat_kids = kids_all.reshape(-1)
    sums = jnp.zeros((K1, D), jnp.float32).at[flat_kids].add(block_weighted_totals.reshape(-1, D))
    counts = jnp.zeros((K1,), jnp.float32).at[flat_kids].add(block_counts.reshape(-1))
    return (sums + centroids.astype(jnp.float32)) / (counts + 1.0)[:, None]
```

```python
import functools
import math

import jax
import jax.numpy as jnp
from jax import lax
from jax.experimental import pallas as pl
from jax.experimental.pallas import tpu as pltpu
from jax.sharding import PartitionSpec as P

D = 1024
X, Z = 4, 8
W = X * Z
N = 8
RB = 256
CH = 128
F = 128
BLK = 16
GW = 512
CW = 8192
MESH = pl.DeviceIdType.MESH
NT = (((1,), (1,)), ((), ()))


def shifted(me, dx, dz):
    return lax.rem(me // Z + dx, X) * Z + lax.rem(lax.rem(me, Z) + dz, Z)


def shifted(me, dx, dz):
    return lax.rem(me // Z + dx, X) * Z + lax.rem(lax.rem(me, Z) + dz, Z)


def at_offset(me, k):
    return shifted(me, k // Z, lax.rem(k, Z))


def first_two(mask, lane):
    first = jnp.min(jnp.where(mask, lane, 127), axis=1, keepdims=True)
    rest = mask & (lane != first)
    second = jnp.min(jnp.where(rest, lane, 127), axis=1, keepdims=True)
    return first, second, rest


ROWS = 64
OWN_AT, MINE, PICK, LAST = W, W + 8, W + 16, W + 24


def exchange_kernel(
    ids_ref, child_ref, cent_ref, emb_ref,
    q_out, sc_out, kids_out, tab_out, dup_out, factor_out,
    ids_all, tab_s, kids_s, cent_b, child_v, cent_f, stage, counts_v, x_send,
    hop_send, hop_recv, xfull, csel, ctab, qsend, scs, qrecv, scr, pick, scu, swork,
    local_sem, ids_ss, ids_rs, e_ss, e_rs, d_ss, d_rs, h_ss, h_rs, c_ss, c_rs, s_ss, s_rs,
    t_ss, t_rs, v_ss, v_rs, g_ss, g_rs, u_ss, u_rs, own_sem, *many,
):
    x_recv, rings = many[:Z], (many[Z : Z + 4], many[Z + 4 :] + many[Z + 3 : Z + 4])
    me = lax.axis_index("wide")
    mn = lax.axis_index("narrow")
    mx, mz = me // Z, lax.rem(me, Z)

    def remote(src, dst, ss, rs, **where):
        return pltpu.make_async_remote_copy(
            src_ref=src, dst_ref=dst, send_sem=ss, recv_sem=rs,
            device_id=where, device_id_type=MESH,
        )

    def narrow_at(k):
        return lax.rem(mn + k, N)

    get_cent = pltpu.make_async_copy(cent_ref, cent_b, local_sem.at[0])
    get_child = pltpu.make_async_copy(child_ref, child_v, local_sem.at[1])
    get_cent.start()
    get_child.start()
    barrier = pltpu.get_barrier_semaphore()

    @pl.loop(1, W)
    def _(k):
        pl.semaphore_signal(
            barrier, inc=1, device_id={"wide": at_offset(me, k)}, device_id_type=MESH
        )

    @pl.loop(1, N)
    def _(k):
        pl.semaphore_signal(
            barrier, inc=1, device_id={"narrow": narrow_at(k)}, device_id_type=MESH
        )

    cols = pl.ds(pl.multiple_of(mn * F, F), F)
    own_rows = pl.ds(pl.multiple_of(mn * 2 * RB, 2 * RB), 2 * RB)
    pl.semaphore_wait(barrier, W - 1 + N - 1)

    def ids_copy(k):
        return remote(
            ids_ref, ids_all.at[me], ids_ss.at[k], ids_rs.at[k], wide=at_offset(me, k)
        )

    @pl.loop(1, W)
    def _(k):
        ids_copy(k).start()

    ids_all[me] = ids_ref[...]

    def e_copy(k):
        to = narrow_at(k)
        return remote(
            emb_ref.at[pl.ds(pl.multiple_of(to * 2 * RB, 2 * RB), 2 * RB)],
            xfull.at[:, cols], e_ss.at[k], e_rs.at[k], narrow=to,
        )

    @pl.loop(1, N)
    def _(k):
        e_copy(k).start()

    own_x = pltpu.make_async_copy(emb_ref.at[own_rows], xfull.at[:, cols], local_sem.at[2])
    own_x.start()
    get_cent.wait()

    @pl.loop(0, CW // 256)
    def _(i):
        rows = pl.ds(pl.multiple_of(i * 256, 256), 256)
        cent_f[rows, :] = cent_b[rows, :].astype(jnp.float32)

    @pl.loop(1, W)
    def _(k):
        ids_copy(k).wait()

    lane = lax.broadcasted_iota(jnp.int32, (W, 128), 1)
    asked = jnp.max(ids_all[...], axis=1)
    in0, in1, _ = first_two((asked >> 9) == me, lane)
    c0 = jnp.sum(jnp.where(lane == in0, asked - me * GW, 0), axis=1, keepdims=True)
    c1 = jnp.sum(jnp.where(lane == in1, asked - me * GW, 0), axis=1, keepdims=True)
    has0 = (in0 < BLK).astype(jnp.int32)
    has1 = (in1 < BLK).astype(jnp.int32)
    c0 = jnp.clip(c0 * has0, 0, GW - 1)
    c1 = jnp.clip(c1 * has1, 0, GW - 1)
    table = jnp.zeros((W, 128), jnp.int32)
    for i, column in ((0, c0), (1, c1), (4, has0), (5, has1)):
        table = jnp.where(lane == i, column, table)

    own_ids = jnp.broadcast_to(ids_ref[0:1, :], (W, 128))
    sub = lax.broadcasted_iota(jnp.int32, (W, 128), 0)
    b0, b1, _ = first_two((own_ids >> 9) == sub, lane)
    table = jnp.where(lane == 2, jnp.where(b0 < BLK, b0, 0), table)
    table = jnp.where(lane == 3, jnp.where(b1 < BLK, b1, 0), table)
    tab_out[0:W, :] = table

    lane8 = lax.broadcasted_iota(jnp.int32, (8, 128), 1)
    owner = jnp.max(ids_all[pl.ds(mx * Z, Z)], axis=1) >> 9
    owner = jnp.where(lane8 < BLK, owner, -1)
    position = jnp.zeros((8, 128), jnp.int32)
    for d in range(1, BLK):
        same = (owner == pltpu.roll(owner, d, 1)) & (lane8 >= d)
        position = jnp.where(same, 1, position)
    at = jnp.clip((owner >> 3) * 2 + position, 0, 2 * X - 1)
    tab_out[OWN_AT : OWN_AT + 8, :] = at
    tab_out[MINE : MINE + 8, :] = jnp.where((owner & 7) == mz, 1, 0)
    chosen = jnp.zeros((8, 128), jnp.int32)
    for x in range(X):
        b0, b1, _ = first_two(owner == x * Z + mz, lane8)
        chosen = jnp.where(lane8 == 2 * x, jnp.where(b0 < BLK, b0, 0), chosen)
        chosen = jnp.where(lane8 == 2 * x + 1, jnp.where(b1 < BLK, b1, 0), chosen)
    tab_out[PICK : PICK + 8, :] = chosen

    hops = (mz - (jnp.broadcast_to(ids_ref[0:1, :], (8, 128)) >> 9)) & 7
    way = jnp.where(hops < 4, 1, 2)
    way = jnp.where((hops == 4) & (lane8 < BLK // 2), 1, way)
    tab_out[LAST : LAST + 8, :] = jnp.where(hops == 0, 0, way)
    put_tab = pltpu.make_async_copy(tab_out, tab_s, local_sem.at[3])
    put_tab.start()
    put_tab.wait()
    get_child.wait()

    @pl.loop(0, W)
    def _(s):
        for j in range(2):
            row = jnp.clip(child_v[pl.ds(tab_s[s, j], 1), :] - me * CW, 0, CW - 1)
            kids_out[pl.ds(2 * s + j, 1), :] = row

    put_kids = pltpu.make_async_copy(kids_out, kids_s, local_sem.at[4])
    put_kids.start()
    put_kids.wait()

    def gather(p, dst):
        for j in range(2):

            @pl.loop(0, CH // 16)
            def _(g):
                base = pl.multiple_of(g * 16, 16)
                rows = [
                    cent_f[pl.ds(kids_s[2 * p + j, base + i], 1), :] for i in range(16)
                ]
                for i in range(16):
                    stage[j, pl.ds(base + i, 1), :] = rows[i]

        for j in range(2):
            dst[j] = stage[j].astype(jnp.bfloat16)

    def down_copy(dx, dz):
        return remote(
            x_send.at[dz, lax.rem(mx + dx, X)], x_recv[dz].at[pl.ds(2 * mx, 2)],
            d_ss.at[dx * Z + dz], d_rs.at[dx * Z + dz], wide=shifted(me, dx, 0),
        )

    def gather_for(dz):
        zs = lax.rem(mz + dz, Z)

        @pl.loop(1, X)
        def _(dx):
            xs = lax.rem(mx + dx, X)
            gather(xs * Z + zs, x_send.at[dz, xs])
            down_copy(dx, dz).start()

        gather(mx * Z + zs, x_recv[dz].at[pl.ds(2 * mx, 2)])

    def have_children(dz):
        @pl.loop(1, X)
        def _(dx):
            down_copy(dx, dz).wait()

    def down_hop(way, d, c):
        part = pl.ds(4 * c, 4)
        k = (way * 4 + d - 1) * 4 + c
        return remote(
            hop_send.at[way, d - 1, part], hop_recv.at[way, d - 1, part],
            h_ss.at[k], h_rs.at[k], wide=shifted(me, 0, 1 if way == 0 else Z - 1),
        )

    def down_parts(way, d):
        return range(4) if d < 4 else (0, 1) if way == 0 else (2, 3)

    def put_in(d):
        for dz in (d, Z - d) if d < 4 else (4,):
            have_children(dz)
        for c in range(4):
            for way in range(2):
                if c not in down_parts(way, d):
                    continue
                comes = d < 4 and c in down_parts(way, d + 1)
                if comes:
                    down_hop(way, d + 1, c).wait_recv()
                dz = d if way == 0 else Z - d
                zs = lax.rem(mz + dz, Z)

                @pl.loop(0, 4)
                def _(i):
                    b = 4 * c + i
                    value = x_recv[dz][tab_s[OWN_AT + zs, b]]
                    if comes:
                        came = hop_recv[way, d, b]
                        value = jnp.where(tab_s[MINE + zs, b] > 0, value, came)
                    hop_send[way, d - 1, b] = value

                down_hop(way, d, c).start()

    gather_for(4)
    gather_for(3)
    put_in(4)
    gather_for(5)
    gather_for(2)
    gather_for(6)
    put_in(3)
    gather_for(1)
    gather_for(7)
    put_in(2)
    gather_for(0)

    kids = kids_out[...]
    lane64 = lax.broadcasted_iota(jnp.int32, (2 * W, CH), 1)
    twice = jnp.zeros((2 * W, CH), jnp.int32)
    for d in range(1, 16):
        same = (kids == pltpu.roll(kids, d, 1)) & (lax.rem(lane64, 16) >= d)
        twice = jnp.where(same, 1, twice)
    any_twice = jnp.max(twice, axis=1, keepdims=True)
    for d in (1, 2, 4, 8):
        twice = jnp.maximum(twice, pltpu.roll(twice, CH - d, 1))
    dup_out[...] = jnp.where(lane64 == 1, any_twice, twice)

    put_in(1)
    have_children(0)
    own_x.wait()

    @pl.loop(1, N)
    def _(k):
        e_copy(k).wait()

    eye = lax.broadcasted_iota(jnp.int32, (CH, CH), 0) == lax.broadcasted_iota(
        jnp.int32, (CH, CH), 1
    )

    def as_row(column):
        return jnp.sum(jnp.where(eye, column, 0.0), axis=0, keepdims=True)

    row8 = lax.broadcasted_iota(jnp.int32, (8, CH), 0)

    def c_copy(to, sender):
        return remote(
            csel.at[pl.ds(2 * to, 2)], ctab.at[:, :, cols], c_ss.at[to], c_rs.at[sender],
            narrow=to,
        )

    def s_copy(to, sender):
        return remote(
            qsend.at[to], qrecv.at[pl.ds(2 * mn, 2)], s_ss.at[to], s_rs.at[sender], narrow=to
        )

    def t_copy(to, sender):
        return remote(
            scs.at[to], scr.at[pl.ds(2 * mn, 2)], t_ss.at[to], t_rs.at[sender], narrow=to
        )

    def weigh():
        for j in range(2):
            x = xfull[j * RB : (j + 1) * RB, :]
            squares = jnp.zeros((CH, F), jnp.float32)
            for n in range(N):
                part = ctab[j, :, n * F : (n + 1) * F].astype(jnp.float32)
                squares = squares + part * part
            lengths = as_row(jnp.sum(squares, axis=1, keepdims=True))
            dots = lax.dot_general(x, ctab[j], NT, preferred_element_type=jnp.float32)
            score = (2.0 * dots - lengths) * (1.0 / math.sqrt(D))
            e = jnp.exp(score - jnp.max(score, axis=1, keepdims=True))
            weights = (e / jnp.sum(e, axis=1, keepdims=True)).astype(jnp.bfloat16)
            weights_f = weights.astype(jnp.float32)
            counts = jnp.sum(weights_f, axis=0, keepdims=True)
            turned = weights_f.T.astype(jnp.bfloat16)
            swork[j] = jnp.dot(turned, x, preferred_element_type=jnp.float32)
            for n in range(N):
                part = swork[j, :, n * F : (n + 1) * F]
                top = jnp.maximum(jnp.max(jnp.abs(part), axis=1, keepdims=True), 1e-30)
                coded = jnp.round(part * (32767.0 / top)).astype(jnp.int32)
                qsend[n, j] = coded.astype(jnp.int16)
                scales = as_row(top * (1.0 / 32767.0))
                tile = jnp.where((row8 == 0) | (row8 == 4), scales, 0.0)
                scs[n, j] = jnp.where((row8 == 1) | (row8 == 5), counts, tile)

    @pl.loop(0, 4)
    def _(c):
        for way in range(2):
            down_hop(way, 1, c).wait_recv()

        @pl.loop(0, 4)
        def _(i):
            b = 4 * c + i
            comes = tab_s[LAST, b]
            value = jnp.where(comes == 1, hop_recv[0, 0, b], hop_recv[1, 0, b])
            csel[b] = jnp.where(comes == 0, x_recv[0][tab_s[OWN_AT + mz, b]], value)

        for i in range(2):
            to = 2 * c + i

            @pl.when(mn != to)
            def _():
                c_copy(to, mn).start()

            @pl.when(mn == to)
            def _():
                for j in range(2):
                    ctab[j, :, cols] = csel[2 * mn + j]

        @pl.when(mn // 2 == c)
        def _():
            @pl.loop(1, N)
            def _(k):
                c_copy(narrow_at(k), narrow_at(k)).wait_recv()

            weigh()

            @pl.loop(1, N)
            def _(k):
                s_copy(narrow_at(k), mn).start()
                t_copy(narrow_at(k), mn).start()

            for j in range(2):
                qrecv[2 * mn + j] = qsend[mn, j]
                scr[2 * mn + j] = scs[mn, j]

    def up_hop(way, t, c):
        part = pl.ds(4 * c, 4)
        k = (way * 4 + t - 1) * 4 + c
        src = (qrecv if t == 1 else rings[way][t - 2]).at[part]
        dst = rings[way][t - 1].at[part]
        return remote(
            src, dst, g_ss.at[k], g_rs.at[k], wide=shifted(me, 0, 1 if way == 0 else Z - 1)
        )

    def up_copy(dx, zs):
        return remote(
            pick.at[zs, lax.rem(mx + dx, X)], q_out.at[mx * Z + zs],
            u_ss.at[dx * Z + zs], u_rs.at[dx * Z + zs], wide=shifted(me, dx, 0),
        )

    def own_copy(zs):
        return pltpu.make_async_copy(pick.at[zs, mx], q_out.at[mx * Z + zs], own_sem.at[zs])

    def send_picked(zs, src):
        @pl.loop(1, X)
        def _(dx):
            xs = lax.rem(mx + dx, X)
            for j in range(2):
                pick[zs, xs, j] = src[tab_s[PICK + zs, 2 * xs + j]]
            up_copy(dx, zs).start()

        for j in range(2):
            pick[zs, mx, j] = src[tab_s[PICK + zs, 2 * mx + j]]
        own_copy(zs).start()

    @pl.loop(0, 4)
    def _(c):
        for i in range(2):
            sender = 2 * c + i

            @pl.when(mn != sender)
            def _():
                s_copy(sender, sender).wait_recv()
                t_copy(sender, sender).wait_recv()

        up_hop(0, 1, c).start()
        up_hop(1, 1, c).start()

    def scale_copy(k):
        to = at_offset(me, k)
        return remote(scu.at[to], sc_out.at[me], v_ss.at[k], v_rs.at[k], wide=to)

    def fill_scale(p):
        return jnp.where(row8 < 4, scr[tab_s[p, 2]], scr[tab_s[p, 3]])

    @pl.loop(1, W)
    def _(k):
        p = at_offset(me, k)
        scu[p] = fill_scale(p)
        scale_copy(k).start()

    sc_out[me] = fill_scale(me)
    send_picked(mz, qrecv)

    square_sub = lax.broadcasted_iota(jnp.int32, (CH, CH), 0)
    counts_v[...] = jnp.zeros_like(counts_v)

    def count(first, end):
        @pl.loop(first, end)
        def _(s):
            tile = sc_out[s]
            total = jnp.zeros((CH, CH), jnp.float32)
            for j in range(2):
                kid = kids_out[pl.ds(2 * s + j, 1), :]
                row = jnp.where(tab_s[s, 4 + j] > 0, tile[4 * j + 1 : 4 * j + 2, :], 0.0)
                low = ((kid & 127) == square_sub).astype(jnp.bfloat16)
                left = jnp.where((kid >> 7) == square_sub, row, 0.0)
                for _ in range(3):
                    piece = left.astype(jnp.bfloat16)
                    total = total + lax.dot_general(
                        low, piece, NT, preferred_element_type=jnp.float32
                    )
                    left = left - piece.astype(jnp.float32)
            counts_v[...] += total

    def pass_on(t):
        for c in range(4):
            for way in range(2):
                up_hop(way, t, c).wait_recv()
                if t < 3 or c in down_parts(way, 4):
                    up_hop(way, t + 1, c).start()
        for way in range(2):
            send_picked(lax.rem(mz + (Z - t if way == 0 else t), Z), rings[way][t - 1])

    pass_on(1)

    @pl.loop(1, W)
    def _(k):
        scale_copy(k).wait()

    count(0, W // 2)
    pass_on(2)
    count(W // 2, W)
    factor_out[...] = 1.0 / (counts_v[...] + 1.0)
    pass_on(3)
    for way in range(2):
        for c in down_parts(way, 4):
            up_hop(way, 4, c).wait_recv()
    send_picked(lax.rem(mz + 4, Z), rings[0][3])

    for way in range(2):
        for d in range(1, 5):
            for c in down_parts(way, d):
                down_hop(way, d, c).wait_send()
                up_hop(way, d, c).wait_send()

    @pl.loop(1, N)
    def _(k):
        c_copy(narrow_at(k), mn).wait_send()
        s_copy(narrow_at(k), mn).wait_send()
        t_copy(narrow_at(k), mn).wait_send()

    @pl.loop(0, Z)
    def _(zs):
        @pl.loop(1, X)
        def _(dx):
            up_copy(dx, zs).wait()

        own_copy(zs).wait()


def exchange(ids, children, centroids, embeddings):
    vm = pl.BlockSpec(memory_space=pltpu.VMEM)
    hbm = pl.BlockSpec(memory_space=pl.ANY)
    dma = pltpu.SemaphoreType.DMA
    bf, f32, i32, i16 = jnp.bfloat16, jnp.float32, jnp.int32, jnp.int16
    return pl.pallas_call(
        exchange_kernel,
        out_shape=(
            jax.ShapeDtypeStruct((W, 2, CH, F), i16),
            jax.ShapeDtypeStruct((W, 8, CH), f32),
            jax.ShapeDtypeStruct((2 * W, CH), i32),
            jax.ShapeDtypeStruct((ROWS, 128), i32),
            jax.ShapeDtypeStruct((2 * W, CH), i32),
            jax.ShapeDtypeStruct((CH, CH), f32),
        ),
        in_specs=[vm, hbm, hbm, hbm],
        out_specs=(hbm, vm, vm, vm, vm, vm),
        scratch_shapes=[
            pltpu.VMEM((W, 8, 128), i32),
            pltpu.SMEM((ROWS, 128), i32),
            pltpu.SMEM((2 * W, CH), i32),
            pltpu.VMEM((CW, F), bf),
            pltpu.VMEM((GW, CH), i32),
            pltpu.VMEM((CW, F), f32),
            pltpu.VMEM((2, CH, F), f32),
            pltpu.VMEM((CH, CH), f32),
            pltpu.VMEM((Z, X, 2, CH, F), bf),
            pltpu.VMEM((2, 4, BLK, CH, F), bf),
            pltpu.VMEM((2, 4, BLK, CH, F), bf),
            pltpu.VMEM((2 * RB, D), bf),
            pltpu.VMEM((BLK, CH, F), bf),
            pltpu.VMEM((2, CH, D), bf),
            pltpu.VMEM((N, 2, CH, F), i16),
            pltpu.VMEM((N, 2, 8, CH), f32),
            pltpu.VMEM((BLK, CH, F), i16),
            pltpu.VMEM((BLK, 8, CH), f32),
            pltpu.VMEM((Z, X, 2, CH, F), i16),
            pltpu.VMEM((W, 8, CH), f32),
            pltpu.VMEM((2, CH, D), f32),
            dma((5,)),
            dma((W,)), dma((W,)),
            dma((N,)), dma((N,)),
            dma((W,)), dma((W,)),
            dma((32,)), dma((32,)),
            dma((N,)), dma((N,)),
            dma((N,)), dma((N,)),
            dma((N,)), dma((N,)),
            dma((W,)), dma((W,)),
            dma((32,)), dma((32,)),
            dma((W,)), dma((W,)),
            dma((Z,)),
        ]
        + [pltpu.VMEM((2 * X, CH, F), bf)] * Z
        + [pltpu.VMEM((BLK, CH, F), i16)] * 7,
        compiler_params=pltpu.CompilerParams(
            collective_id=0, has_side_effects=True, vmem_limit_bytes=60 * 1024 * 1024
        ),
        name="exchange",
    )(ids, children, centroids, embeddings)


PARTS = 8
BATCH = 16


def scatter_kernel(
    kids_s, tab_s, dup_s, q_hbm, sc_ref, factor_ref, cent_hbm, out_hbm,
    q_ref, cent_b, slots, acc, cent_sem, q_sem, out_sem,
):
    lane = lax.broadcasted_iota(jnp.int32, (CH, CH), 1)
    eye = lane == lax.broadcasted_iota(jnp.int32, (CH, CH), 0)
    per, rows_per = W // PARTS, CW // PARTS

    def cent_copy(i):
        rows = pl.ds(pl.multiple_of(i * rows_per, rows_per), rows_per)
        return pltpu.make_async_copy(cent_hbm.at[rows], cent_b.at[rows], cent_sem.at[i])

    def q_copy(i):
        rows = pl.ds(i * per, per)
        return pltpu.make_async_copy(q_hbm.at[rows], q_ref.at[rows], q_sem.at[i])

    def out_copy(i):
        rows = pl.ds(pl.multiple_of(i * rows_per, rows_per), rows_per)
        return pltpu.make_async_copy(acc.at[rows], out_hbm.at[rows], out_sem.at[i])

    @pl.loop(0, PARTS)
    def _(i):
        cent_copy(i).start()

    @pl.loop(0, PARTS)
    def _(i):
        q_copy(i).start()

    @pl.loop(0, PARTS)
    def _(i):
        cent_copy(i).wait()
        for t in range(4):
            step = rows_per // 4
            rows = pl.ds(pl.multiple_of(i * rows_per + t * step, step), step)
            acc[rows, :] = cent_b[rows, :].astype(jnp.float32)

    def add_batch(slot, base):
        at = [pl.ds(kids_s[slot, base + i], 1) for i in range(BATCH)]
        sums = [acc[at[i], :] + slots[slot, pl.ds(base + i, 1), :] for i in range(BATCH)]
        for i in range(BATCH):
            acc[at[i], :] = sums[i]

    def decode(s):
        tile = sc_ref[s]
        for j in range(2):
            scale = jnp.sum(
                jnp.where(eye, tile[4 * j : 4 * j + 1, :], 0.0), axis=1, keepdims=True
            )
            slots[2 * s + j] = q_ref[s, j].astype(jnp.int32).astype(jnp.float32) * scale

    def add_slot(slot):
        @pl.when(dup_s[slot, 1] == 0)
        def _():
            for g in range(CH // BATCH):
                add_batch(slot, g * BATCH)

        @pl.when(dup_s[slot, 1] > 0)
        def _():
            @pl.loop(0, CH // BATCH)
            def _(g):
                base = pl.multiple_of(g * BATCH, BATCH)

                @pl.when(dup_s[slot, base] == 0)
                def _():
                    add_batch(slot, base)

                @pl.when(dup_s[slot, base] > 0)
                def _():
                    for i in range(BATCH):
                        at = pl.ds(kids_s[slot, base + i], 1)
                        acc[at, :] = acc[at, :] + slots[slot, pl.ds(base + i, 1), :]

    @pl.loop(0, PARTS)
    def _(i):
        q_copy(i).wait()

        @pl.loop(0, per)
        def _(t):
            decode(i * per + t)

    @pl.loop(0, W)
    def _(s):
        for j in range(2):

            @pl.when(tab_s[s, 4 + j] > 0)
            def _():
                add_slot(2 * s + j)

    factors = factor_ref[...]

    for i in range(PARTS):
        for h in range(i * (rows_per // CH), (i + 1) * (rows_per // CH)):
            rows = pl.ds(h * CH, CH)
            acc[rows, :] = acc[rows, :] * factors[:, h : h + 1]
        out_copy(i).start()

    @pl.loop(0, PARTS)
    def _(i):
        out_copy(i).wait()


def scatter(kids, table, twice, q, scales, factors, centroids):
    vm = pl.BlockSpec(memory_space=pltpu.VMEM)
    sm = pl.BlockSpec(memory_space=pltpu.SMEM)
    hbm = pl.BlockSpec(memory_space=pl.ANY)
    return pl.pallas_call(
        scatter_kernel,
        out_shape=jax.ShapeDtypeStruct((CW, F), jnp.float32),
        in_specs=[sm, sm, sm, hbm, vm, vm, hbm],
        out_specs=hbm,
        scratch_shapes=[
            pltpu.VMEM((W, 2, CH, F), jnp.int16),
            pltpu.VMEM((CW, F), jnp.bfloat16),
            pltpu.VMEM((2 * W, CH, F), jnp.float32),
            pltpu.VMEM((CW, F), jnp.float32),
            pltpu.SemaphoreType.DMA((PARTS,)),
            pltpu.SemaphoreType.DMA((PARTS,)),
            pltpu.SemaphoreType.DMA((PARTS,)),
        ],
        compiler_params=pltpu.CompilerParams(vmem_limit_bytes=60 * 1024 * 1024),
        name="scatter",
    )(kids, table, twice, q, scales, factors, centroids)


def body(embeddings, centroids, level2_cluster_index, child_lists):
    ids = jnp.pad(level2_cluster_index, (0, 128 - BLK), constant_values=-1)
    ids = jnp.broadcast_to(ids[None, :], (8, 128))
    q, scales, kids, table, twice, factors = exchange(ids, child_lists, centroids, embeddings)
    return scatter(kids, table, twice, q, scales, factors, centroids)


def solution(mesh):
    placed = (P("wide", "narrow"), P("wide", "narrow"), P("wide"), P("wide", None))
    return jax.shard_map(
        body, mesh=mesh, in_specs=placed, out_specs=P("wide", "narrow"), check_vma=False
    )
```

```python
import functools
import math

import jax
import jax.numpy as jnp
from jax import lax
from jax.experimental import pallas as pl
from jax.experimental.pallas import tpu as pltpu
from jax.sharding import PartitionSpec as P

D = 1024
X, Z = 4, 8
W = X * Z
N = 8
RB = 256
CH = 128
F = 128
BLK = 16
GW = 512
CW = 8192
MESH = pl.DeviceIdType.MESH
NT = (((1,), (1,)), ((), ()))


def shifted(me, dx, dz):
    return lax.rem(me // Z + dx, X) * Z + lax.rem(lax.rem(me, Z) + dz, Z)


def at_offset(me, k):
    return shifted(me, k // Z, lax.rem(k, Z))


def first_two(mask, lane):
    first = jnp.min(jnp.where(mask, lane, 127), axis=1, keepdims=True)
    rest = mask & (lane != first)
    second = jnp.min(jnp.where(rest, lane, 127), axis=1, keepdims=True)
    return first, second, rest


def exchange_kernel(
    ids_ref, child_ref, cent_ref, emb_ref,
    q_out, sc_out, kids_out, tab_out, dup_out, factor_out,
    ids_all, own_v, own_s, tab_s, kids_s, emb_v, cent_b, child_v, counts_v, cent_f, stage,
    e_send, x_in, c_send, ctab, q_send, t_send, swork,
    local_sem, ids_ss, ids_rs, e_ss, e_rs, c_ss, c_rs, q_ss, q_rs, t_ss, t_rs, own_sem,
):
    me = lax.axis_index("wide")
    mn = lax.axis_index("narrow")
    mx, mz, core = me // Z, lax.rem(me, Z), lax.rem(mn, 2)
    first = lax.rem(2 * mz + 4 - mn // 2, 4)

    def remote(src, dst, ss, rs, **where):
        return pltpu.make_async_remote_copy(
            src_ref=src, dst_ref=dst, send_sem=ss, recv_sem=rs,
            device_id=where, device_id_type=MESH,
        )

    def narrow_at(k):
        return lax.rem(mn + k, N)

    def lanes_of(n):
        return pl.ds(pl.multiple_of(n * F, F), F)

    def behind(dx, dz):
        return shifted(me, X - dx, Z - dz)

    get_emb = pltpu.make_async_copy(emb_ref, emb_v, local_sem.at[0])
    get_cent = pltpu.make_async_copy(cent_ref, cent_b, local_sem.at[1])
    get_child = pltpu.make_async_copy(child_ref, child_v, local_sem.at[2])
    get_emb.start()
    get_cent.start()
    get_child.start()
    barrier = pltpu.get_barrier_semaphore()

    @pl.loop(0, 2 * X)
    def _(i):
        dx, dz = i // 2, first + 4 * lax.rem(i, 2)

        @pl.when(dx + dz > 0)
        def _():
            @pl.loop(0, N)
            def _(n):
                pl.semaphore_signal(
                    barrier, inc=1, device_id={"wide": behind(dx, dz), "narrow": n},
                    device_id_type=MESH,
                )

    @pl.loop(1, W)
    def _(k):
        pl.semaphore_signal(
            barrier, inc=1, device_id={"wide": at_offset(me, k)}, device_id_type=MESH
        )

    @pl.loop(1, N)
    def _(k):
        pl.semaphore_signal(
            barrier, inc=1, device_id={"narrow": narrow_at(k)}, device_id_type=MESH
        )

    lane = lax.broadcasted_iota(jnp.int32, (W, 128), 1)
    sub = lax.broadcasted_iota(jnp.int32, (W, 128), 0)
    own_ids = jnp.broadcast_to(ids_ref[0:1, :], (W, 128))
    b0, b1, _ = first_two((own_ids >> 9) == sub, lane)
    b0 = jnp.where(b0 < BLK, b0, 0)
    b1 = jnp.where(b1 < BLK, b1, 0)
    own_v[...] = jnp.where(lane == 0, b0, jnp.where(lane == 1, b1, 0))
    put_own = pltpu.make_async_copy(own_v, own_s, local_sem.at[3])
    put_own.start()
    put_own.wait()
    get_emb.wait()
    pl.semaphore_wait(barrier, 2 * (W - 1) + W - 1 + N - 1)

    def ids_copy(k):
        return remote(
            ids_ref, ids_all.at[me], ids_ss.at[k], ids_rs.at[k], wide=at_offset(me, k)
        )

    @pl.loop(1, W)
    def _(k):
        ids_copy(k).start()

    ids_all[me] = ids_ref[...]

    def e_copy(dx, dz, j):
        to = shifted(me, dx, dz)
        k = dx * Z + dz
        return remote(
            e_send.at[to, j], x_in.at[dx, dz // 4, :, lanes_of(mn)],
            e_ss.at[2 * k + j], e_rs.at[(2 * dx + dz // 4) * N + mn],
            wide=to, narrow=2 * lax.rem(2 * mz + dz, 4) + j,
        )

    def stays(dx, dz, j):
        return (dx == 0) & (dz == 0) & (2 * lax.rem(2 * mz, 4) + j == mn)

    def send_blocks(dx):
        @pl.loop(0, Z)
        def _(m):
            u, v = m // 2 + 1, lax.rem(m, 2)
            dz = (u * (1 - v) + (Z - u) * v) * (1 - m // (Z - 1))
            to = shifted(me, dx, dz)
            for j in range(2):
                e_send[to, j] = emb_v[own_s[to, j]]

                @pl.when(jnp.logical_not(stays(dx, dz, j)))
                def _():
                    e_copy(dx, dz, j).start()

                @pl.when(stays(dx, dz, j))
                def _():
                    x_in[0, 0, :, lanes_of(mn)] = e_send[to, j]

    def blocks_left(dx):
        @pl.loop(0, Z)
        def _(dz):
            for j in range(2):

                @pl.when(jnp.logical_not(stays(dx, dz, j)))
                def _():
                    e_copy(dx, dz, j).wait_send()

    def have_blocks(dx):
        for h in range(2):
            stayed = (dx == 0) & (first == 0) & (h == 0)

            @pl.loop(0, N)
            def _(n):
                @pl.when(jnp.logical_not(stayed & (n == mn)))
                def _():
                    remote(
                        e_send.at[0, 0], x_in.at[dx, h, :, lanes_of(n)],
                        e_ss.at[0], e_rs.at[(2 * dx + h) * N + n], narrow=narrow_at(1),
                    ).wait_recv()

    send_blocks(0)
    send_blocks(1)

    get_cent.wait()

    @pl.loop(0, CW // 256)
    def _(i):
        rows = pl.ds(pl.multiple_of(i * 256, 256), 256)
        cent_f[rows, :] = cent_b[rows, :].astype(jnp.float32)

    @pl.loop(1, W)
    def _(k):
        ids_copy(k).wait()

    asked = jnp.max(ids_all[...], axis=1)
    in0, in1, _ = first_two((asked >> 9) == me, lane)
    c0 = jnp.sum(jnp.where(lane == in0, asked - me * GW, 0), axis=1, keepdims=True)
    c1 = jnp.sum(jnp.where(lane == in1, asked - me * GW, 0), axis=1, keepdims=True)
    has0 = (in0 < BLK).astype(jnp.int32)
    has1 = (in1 < BLK).astype(jnp.int32)
    c0 = jnp.clip(c0 * has0, 0, GW - 1)
    c1 = jnp.clip(c1 * has1, 0, GW - 1)
    table = jnp.zeros((W, 128), jnp.int32)
    for i, column in ((0, c0), (1, c1), (4, has0), (5, has1)):
        table = jnp.where(lane == i, column, table)
    tab_out[...] = table
    put_tab = pltpu.make_async_copy(tab_out, tab_s, local_sem.at[4])
    put_tab.start()
    put_tab.wait()
    get_child.wait()

    @pl.loop(0, W)
    def _(s):
        for j in range(2):
            row = jnp.clip(child_v[pl.ds(tab_s[s, j], 1), :] - me * CW, 0, CW - 1)
            kids_out[pl.ds(2 * s + j, 1), :] = row

    put_kids = pltpu.make_async_copy(kids_out, kids_s, local_sem.at[5])
    put_kids.start()
    put_kids.wait()

    def gather(slot, i, dst):
        @pl.loop(0, CH // 16)
        def _(g):
            base = pl.multiple_of(g * 16, 16)
            rows = [cent_f[pl.ds(kids_s[slot, base + r], 1), :] for r in range(16)]
            for r in range(16):
                stage[i, pl.ds(base + r, 1), :] = rows[r]

        dst[...] = stage[i].astype(jnp.bfloat16)

    def c_copy(half, to, sender):
        part = pl.ds(4 * half, 4)
        return remote(
            c_send.at[to, part], ctab.at[part, :, lanes_of(sender)],
            c_ss.at[half * N + to], c_rs.at[half * N + sender], narrow=to,
        )

    def own_children(half):
        part = pl.ds(4 * half, 4)
        return pltpu.make_async_copy(
            c_send.at[mn, part], ctab.at[part, :, lanes_of(mn)], local_sem.at[6 + half]
        )

    def send_children(half):
        @pl.loop(0, N)
        def _(k):
            to = narrow_at(k)
            far = lax.rem(2 * mz + 4 - to // 2, 4)

            @pl.loop(0, 2)
            def _(i):
                dx = 2 * half + i
                for h in range(2):
                    w = behind(dx, far + 4 * h)
                    gather(2 * w + lax.rem(to, 2), h, c_send.at[to, 2 * dx + h])

            @pl.when(k > 0)
            def _():
                c_copy(half, to, mn).start()

            @pl.when(k == 0)
            def _():
                own_children(half).start()

    send_children(0)
    send_children(1)

    kids = kids_out[...]
    lane64 = lax.broadcasted_iota(jnp.int32, (2 * W, CH), 1)
    twice = jnp.zeros((2 * W, CH), jnp.int32)
    for d in range(1, 16):
        same = (kids == pltpu.roll(kids, d, 1)) & (lax.rem(lane64, 16) >= d)
        twice = jnp.where(same, 1, twice)
    any_twice = jnp.max(twice, axis=1, keepdims=True)
    for d in (1, 2, 4, 8):
        twice = jnp.maximum(twice, pltpu.roll(twice, CH - d, 1))
    dup_out[...] = jnp.where(lane64 == 1, any_twice, twice)

    square_sub = lax.broadcasted_iota(jnp.int32, (CH, CH), 0)
    eye = square_sub == lax.broadcasted_iota(jnp.int32, (CH, CH), 1)

    def as_row(column):
        return jnp.sum(jnp.where(eye, column, 0.0), axis=0, keepdims=True)

    row8 = lax.broadcasted_iota(jnp.int32, (8, CH), 0)

    def weigh(dx, h):
        slot = 2 * dx + h
        x = x_in[dx, h]
        squares = jnp.zeros((CH, F), jnp.float32)
        for n in range(N):
            part = ctab[slot, :, n * F : (n + 1) * F].astype(jnp.float32)
            squares = squares + part * part
        lengths = as_row(jnp.sum(squares, axis=1, keepdims=True))
        dots = lax.dot_general(x, ctab[slot], NT, preferred_element_type=jnp.float32)
        score = (2.0 * dots - lengths) * (1.0 / math.sqrt(D))
        e = jnp.exp(score - jnp.max(score, axis=1, keepdims=True))
        weights = (e / jnp.sum(e, axis=1, keepdims=True)).astype(jnp.bfloat16)
        weights_f = weights.astype(jnp.float32)
        counts = jnp.sum(weights_f, axis=0, keepdims=True)
        turned = weights_f.T.astype(jnp.bfloat16)
        swork[h] = jnp.dot(turned, x, preferred_element_type=jnp.float32)
        for n in range(N):
            part = swork[h, :, n * F : (n + 1) * F]
            top = jnp.maximum(jnp.max(jnp.abs(part), axis=1, keepdims=True), 1e-30)
            coded = jnp.round(part * (32767.0 / top)).astype(jnp.int32)
            q_send[slot, n] = coded.astype(jnp.int16)
            scales = as_row(top * (1.0 / 32767.0))
            t_send[slot, n] = jnp.where(row8 == 0, scales, jnp.where(row8 == 1, counts, 0.0))

    def q_copy(slot, to, w, j):
        return remote(
            q_send.at[slot, to], q_out.at[w, j],
            q_ss.at[slot * N + to], q_rs.at[2 * w + j], narrow=to,
        )

    def t_copy(slot, to, w, j):
        return remote(
            t_send.at[slot, to], sc_out.at[w, j],
            t_ss.at[slot * N + to], t_rs.at[2 * w + j], narrow=to,
        )

    def own_sums(slot, w):
        return pltpu.make_async_copy(q_send.at[slot, mn], q_out.at[w, core], own_sem.at[slot])

    def send_sums(dx, h):
        slot, w = 2 * dx + h, behind(dx, first + 4 * h)

        @pl.loop(1, N)
        def _(k):
            q_copy(slot, narrow_at(k), w, core).start()
            t_copy(slot, narrow_at(k), w, core).start()

        own_sums(slot, w).start()
        sc_out[w, core] = t_send[slot, mn]

    counts_v[...] = jnp.zeros_like(counts_v)

    def take_sums(dx):
        @pl.loop(0, Z)
        def _(dz):
            w = behind(dx, dz)
            for j in range(2):
                sender = 2 * lax.rem(2 * mz + Z - dz, 4) + j

                @pl.when(sender != mn)
                def _():
                    q_copy(0, narrow_at(1), w, j).wait_recv()
                    t_copy(0, narrow_at(1), w, j).wait_recv()

            total = jnp.zeros((CH, CH), jnp.float32)
            for j in range(2):
                kid = kids_out[pl.ds(2 * w + j, 1), :]
                row = jnp.where(tab_s[w, 4 + j] > 0, sc_out[w, j][1:2, :], 0.0)
                low = ((kid & 127) == square_sub).astype(jnp.bfloat16)
                left = jnp.where((kid >> 7) == square_sub, row, 0.0)
                for _ in range(3):
                    piece = left.astype(jnp.bfloat16)
                    total = total + lax.dot_general(
                        low, piece, NT, preferred_element_type=jnp.float32
                    )
                    left = left - piece.astype(jnp.float32)
            counts_v[...] += total

    @pl.loop(0, X)
    def _(dx):
        blocks_left(dx)

        @pl.when(dx < X - 2)
        def _():
            send_blocks(dx + 2)

        @pl.when(lax.rem(dx, 2) == 0)
        def _():
            @pl.loop(1, N)
            def _(k):
                c_copy(dx // 2, narrow_at(k), narrow_at(k)).wait_recv()

            own_children(dx // 2).wait()

        have_blocks(dx)
        for h in range(2):
            weigh(dx, h)
            send_sums(dx, h)

        @pl.when(dx > 0)
        def _():
            take_sums(dx - 1)

    take_sums(X - 1)
    factor_out[...] = 1.0 / (counts_v[...] + 1.0)

    @pl.loop(1, N)
    def _(k):
        to = narrow_at(k)
        for half in range(2):
            c_copy(half, to, mn).wait_send()

        @pl.loop(0, 2 * X)
        def _(slot):
            q_copy(slot, to, 0, 0).wait_send()
            t_copy(slot, to, 0, 0).wait_send()

    @pl.loop(0, 2 * X)
    def _(slot):
        own_sums(slot, 0).wait()


def exchange(ids, children, centroids, embeddings):
    vm = pl.BlockSpec(memory_space=pltpu.VMEM)
    hbm = pl.BlockSpec(memory_space=pl.ANY)
    dma = pltpu.SemaphoreType.DMA
    bf, f32, i32, i16 = jnp.bfloat16, jnp.float32, jnp.int32, jnp.int16
    return pl.pallas_call(
        exchange_kernel,
        out_shape=(
            jax.ShapeDtypeStruct((W, 2, CH, F), i16),
            jax.ShapeDtypeStruct((W, 2, 8, CH), f32),
            jax.ShapeDtypeStruct((2 * W, CH), i32),
            jax.ShapeDtypeStruct((W, 128), i32),
            jax.ShapeDtypeStruct((2 * W, CH), i32),
            jax.ShapeDtypeStruct((CH, CH), f32),
        ),
        in_specs=[vm, hbm, hbm, hbm],
        out_specs=(hbm, vm, vm, vm, vm, vm),
        scratch_shapes=[
            pltpu.VMEM((W, 8, 128), i32),
            pltpu.VMEM((W, 128), i32),
            pltpu.SMEM((W, 128), i32),
            pltpu.SMEM((W, 128), i32),
            pltpu.SMEM((2 * W, CH), i32),
            pltpu.VMEM((BLK, RB, F), bf),
            pltpu.VMEM((CW, F), bf),
            pltpu.VMEM((GW, CH), i32),
            pltpu.VMEM((CH, CH), f32),
            pltpu.VMEM((CW, F), f32),
            pltpu.VMEM((2, CH, F), f32),
            pltpu.VMEM((W, 2, RB, F), bf),
            pltpu.VMEM((X, 2, RB, D), bf),
            pltpu.VMEM((N, 2 * X, CH, F), bf),
            pltpu.VMEM((2 * X, CH, D), bf),
            pltpu.VMEM((2 * X, N, CH, F), i16),
            pltpu.VMEM((2 * X, N, 8, CH), f32),
            pltpu.VMEM((2, CH, D), f32),
            dma((8,)),
            dma((W,)), dma((W,)),
            dma((2 * W,)), dma((2 * W,)),
            dma((2 * N,)), dma((2 * N,)),
            dma((2 * W,)), dma((2 * W,)),
            dma((2 * W,)), dma((2 * W,)),
            dma((2 * X,)),
        ],
        compiler_params=pltpu.CompilerParams(
            collective_id=0, has_side_effects=True, vmem_limit_bytes=60 * 1024 * 1024
        ),
        name="exchange",
    )(ids, children, centroids, embeddings)


PARTS = 8
BATCH = 16


def scatter_kernel(
    kids_s, tab_s, dup_s, q_hbm, sc_ref, factor_ref, cent_hbm, out_hbm,
    q_ref, cent_b, slots, acc, cent_sem, q_sem, out_sem,
):
    lane = lax.broadcasted_iota(jnp.int32, (CH, CH), 1)
    eye = lane == lax.broadcasted_iota(jnp.int32, (CH, CH), 0)
    per, rows_per = W // PARTS, CW // PARTS

    def cent_copy(i):
        rows = pl.ds(pl.multiple_of(i * rows_per, rows_per), rows_per)
        return pltpu.make_async_copy(cent_hbm.at[rows], cent_b.at[rows], cent_sem.at[i])

    def q_copy(i):
        rows = pl.ds(i * per, per)
        return pltpu.make_async_copy(q_hbm.at[rows], q_ref.at[rows], q_sem.at[i])

    def out_copy(i):
        rows = pl.ds(pl.multiple_of(i * rows_per, rows_per), rows_per)
        return pltpu.make_async_copy(acc.at[rows], out_hbm.at[rows], out_sem.at[i])

    @pl.loop(0, PARTS)
    def _(i):
        cent_copy(i).start()

    @pl.loop(0, PARTS)
    def _(i):
        q_copy(i).start()

    @pl.loop(0, PARTS)
    def _(i):
        cent_copy(i).wait()
        for t in range(4):
            step = rows_per // 4
            rows = pl.ds(pl.multiple_of(i * rows_per + t * step, step), step)
            acc[rows, :] = cent_b[rows, :].astype(jnp.float32)

    def add_batch(slot, base):
        at = [pl.ds(kids_s[slot, base + i], 1) for i in range(BATCH)]
        sums = [acc[at[i], :] + slots[slot, pl.ds(base + i, 1), :] for i in range(BATCH)]
        for i in range(BATCH):
            acc[at[i], :] = sums[i]

    def decode(s):
        for j in range(2):
            scale = jnp.sum(
                jnp.where(eye, sc_ref[s, j][0:1, :], 0.0), axis=1, keepdims=True
            )
            slots[2 * s + j] = q_ref[s, j].astype(jnp.int32).astype(jnp.float32) * scale

    def add_slot(slot):
        @pl.when(dup_s[slot, 1] == 0)
        def _():
            for g in range(CH // BATCH):
                add_batch(slot, g * BATCH)

        @pl.when(dup_s[slot, 1] > 0)
        def _():
            @pl.loop(0, CH // BATCH)
            def _(g):
                base = pl.multiple_of(g * BATCH, BATCH)

                @pl.when(dup_s[slot, base] == 0)
                def _():
                    add_batch(slot, base)

                @pl.when(dup_s[slot, base] > 0)
                def _():
                    for i in range(BATCH):
                        at = pl.ds(kids_s[slot, base + i], 1)
                        acc[at, :] = acc[at, :] + slots[slot, pl.ds(base + i, 1), :]

    @pl.loop(0, PARTS)
    def _(i):
        q_copy(i).wait()

        @pl.loop(0, per)
        def _(t):
            decode(i * per + t)

    @pl.loop(0, W)
    def _(s):
        for j in range(2):

            @pl.when(tab_s[s, 4 + j] > 0)
            def _():
                add_slot(2 * s + j)

    factors = factor_ref[...]

    for i in range(PARTS):
        for h in range(i * (rows_per // CH), (i + 1) * (rows_per // CH)):
            rows = pl.ds(h * CH, CH)
            acc[rows, :] = acc[rows, :] * factors[:, h : h + 1]
        out_copy(i).start()

    @pl.loop(0, PARTS)
    def _(i):
        out_copy(i).wait()


def scatter(kids, table, twice, q, scales, factors, centroids):
    vm = pl.BlockSpec(memory_space=pltpu.VMEM)
    sm = pl.BlockSpec(memory_space=pltpu.SMEM)
    hbm = pl.BlockSpec(memory_space=pl.ANY)
    return pl.pallas_call(
        scatter_kernel,
        out_shape=jax.ShapeDtypeStruct((CW, F), jnp.float32),
        in_specs=[sm, sm, sm, hbm, vm, vm, hbm],
        out_specs=hbm,
        scratch_shapes=[
            pltpu.VMEM((W, 2, CH, F), jnp.int16),
            pltpu.VMEM((CW, F), jnp.bfloat16),
            pltpu.VMEM((2 * W, CH, F), jnp.float32),
            pltpu.VMEM((CW, F), jnp.float32),
            pltpu.SemaphoreType.DMA((PARTS,)),
            pltpu.SemaphoreType.DMA((PARTS,)),
            pltpu.SemaphoreType.DMA((PARTS,)),
        ],
        compiler_params=pltpu.CompilerParams(vmem_limit_bytes=60 * 1024 * 1024),
        name="scatter",
    )(kids, table, twice, q, scales, factors, centroids)


def body(embeddings, centroids, level2_cluster_index, child_lists):
    ids = jnp.pad(level2_cluster_index, (0, 128 - BLK), constant_values=-1)
    ids = jnp.broadcast_to(ids[None, :], (8, 128))
    q, scales, kids, table, twice, factors = exchange(
        ids, child_lists, centroids, embeddings.reshape(BLK, RB, F)
    )
    return scatter(kids, table, twice, q, scales, factors, centroids)


def solution(mesh):
    placed = (P("wide", "narrow"), P("wide", "narrow"), P("wide"), P("wide", None))
    return jax.shard_map(
        body, mesh=mesh, in_specs=placed, out_specs=P("wide", "narrow"), check_vma=False
    )
```

```python
import functools
import math

import jax
import jax.numpy as jnp
from jax import lax
from jax.experimental import pallas as pl
from jax.experimental.pallas import tpu as pltpu
from jax.sharding import PartitionSpec as P

D = 1024
X, Z = 4, 8
W = X * Z
N = 8
RB = 256
CH = 128
F = 128
BLK = 16
GW = 512
CW = 8192
MESH = pl.DeviceIdType.MESH
NT = (((1,), (1,)), ((), ()))


def shifted(me, dx, dz):
    return lax.rem(me // Z + dx, X) * Z + lax.rem(lax.rem(me, Z) + dz, Z)


def at_offset(me, k):
    return shifted(me, k // Z, lax.rem(k, Z))


def first_two(mask, lane):
    first = jnp.min(jnp.where(mask, lane, 127), axis=1, keepdims=True)
    rest = mask & (lane != first)
    second = jnp.min(jnp.where(rest, lane, 127), axis=1, keepdims=True)
    return first, second, rest


def exchange_kernel(
    ids_ref, child_ref, cent_ref, emb_ref,
    q_out, sc_out, kids_out, tab_out, dup_out, factor_out,
    ids_all, own_v, own_s, tab_s, kids_s, emb_v, cent_b, child_v, counts_v, cent_f, stage,
    e_send, x_in, c_send, ctab, q_send, t_send, swork,
    local_sem, ids_ss, ids_rs, e_ss, e_rs, c_ss, c_rs, q_ss, q_rs, t_ss, t_rs, own_sem,
):
    me = lax.axis_index("wide")
    mn = lax.axis_index("narrow")
    mx, mz, core = me // Z, lax.rem(me, Z), lax.rem(mn, 2)
    first = lax.rem(2 * mz + 4 - mn // 2, 4)

    def remote(src, dst, ss, rs, **where):
        return pltpu.make_async_remote_copy(
            src_ref=src, dst_ref=dst, send_sem=ss, recv_sem=rs,
            device_id=where, device_id_type=MESH,
        )

    def narrow_at(k):
        return lax.rem(mn + k, N)

    def lanes_of(n):
        return pl.ds(pl.multiple_of(n * F, F), F)

    def behind(dx, dz):
        return shifted(me, X - dx, Z - dz)

    get_emb = pltpu.make_async_copy(emb_ref, emb_v, local_sem.at[0])
    get_cent = pltpu.make_async_copy(cent_ref, cent_b, local_sem.at[1])
    get_child = pltpu.make_async_copy(child_ref, child_v, local_sem.at[2])
    get_emb.start()
    get_cent.start()
    get_child.start()
    barrier = pltpu.get_barrier_semaphore()

    @pl.loop(0, 2 * X)
    def _(i):
        dx, dz = i // 2, first + 4 * lax.rem(i, 2)

        @pl.when(dx + dz > 0)
        def _():
            @pl.loop(0, N)
            def _(n):
                pl.semaphore_signal(
                    barrier, inc=1, device_id={"wide": behind(dx, dz), "narrow": n},
                    device_id_type=MESH,
                )

    @pl.loop(1, W)
    def _(k):
        pl.semaphore_signal(
            barrier, inc=1, device_id={"wide": at_offset(me, k)}, device_id_type=MESH
        )

    @pl.loop(1, N)
    def _(k):
        pl.semaphore_signal(
            barrier, inc=1, device_id={"narrow": narrow_at(k)}, device_id_type=MESH
        )

    lane = lax.broadcasted_iota(jnp.int32, (W, 128), 1)
    sub = lax.broadcasted_iota(jnp.int32, (W, 128), 0)
    own_ids = jnp.broadcast_to(ids_ref[0:1, :], (W, 128))
    b0, b1, _ = first_two((own_ids >> 9) == sub, lane)
    b0 = jnp.where(b0 < BLK, b0, 0)
    b1 = jnp.where(b1 < BLK, b1, 0)
    own_v[...] = jnp.where(lane == 0, b0, jnp.where(lane == 1, b1, 0))
    put_own = pltpu.make_async_copy(own_v, own_s, local_sem.at[3])
    put_own.start()
    put_own.wait()
    get_emb.wait()
    pl.semaphore_wait(barrier, 2 * (W - 1) + W - 1 + N - 1)

    def ids_copy(k):
        return remote(
            ids_ref, ids_all.at[me], ids_ss.at[k], ids_rs.at[k], wide=at_offset(me, k)
        )

    @pl.loop(1, W)
    def _(k):
        ids_copy(k).start()

    ids_all[me] = ids_ref[...]

    def e_copy(dx, dz, j):
        to = shifted(me, dx, dz)
        k = dx * Z + dz
        return remote(
            e_send.at[to, j], x_in.at[dx, dz // 4, :, lanes_of(mn)],
            e_ss.at[2 * k + j], e_rs.at[(2 * dx + dz // 4) * N + mn],
            wide=to, narrow=2 * lax.rem(2 * mz + dz, 4) + j,
        )

    def stays(dx, dz, j):
        return (dx == 0) & (dz == 0) & (2 * lax.rem(2 * mz, 4) + j == mn)

    def send_blocks(dx):
        @pl.loop(0, Z)
        def _(m):
            u, v = m // 2 + 1, lax.rem(m, 2)
            dz = (u * (1 - v) + (Z - u) * v) * (1 - m // (Z - 1))
            to = shifted(me, dx, dz)
            for j in range(2):
                e_send[to, j] = emb_v[own_s[to, j]]

                @pl.when(jnp.logical_not(stays(dx, dz, j)))
                def _():
                    e_copy(dx, dz, j).start()

                @pl.when(stays(dx, dz, j))
                def _():
                    x_in[0, 0, :, lanes_of(mn)] = e_send[to, j]

    def blocks_left(dx):
        @pl.loop(0, Z)
        def _(dz):
            for j in range(2):

                @pl.when(jnp.logical_not(stays(dx, dz, j)))
                def _():
                    e_copy(dx, dz, j).wait_send()

    def have_blocks(dx, h):
        stayed = (dx == 0) & (first == 0) & (h == 0)

        @pl.loop(0, N)
        def _(n):
            @pl.when(jnp.logical_not(stayed & (n == mn)))
            def _():
                remote(
                    e_send.at[0, 0], x_in.at[dx, h, :, lanes_of(n)],
                    e_ss.at[0], e_rs.at[(2 * dx + h) * N + n], narrow=narrow_at(1),
                ).wait_recv()

    send_blocks(0)
    send_blocks(1)

    get_cent.wait()

    @pl.loop(0, CW // 256)
    def _(i):
        rows = pl.ds(pl.multiple_of(i * 256, 256), 256)
        cent_f[rows, :] = cent_b[rows, :].astype(jnp.float32)

    @pl.loop(1, W)
    def _(k):
        ids_copy(k).wait()

    asked = jnp.max(ids_all[...], axis=1)
    in0, in1, _ = first_two((asked >> 9) == me, lane)
    c0 = jnp.sum(jnp.where(lane == in0, asked - me * GW, 0), axis=1, keepdims=True)
    c1 = jnp.sum(jnp.where(lane == in1, asked - me * GW, 0), axis=1, keepdims=True)
    has0 = (in0 < BLK).astype(jnp.int32)
    has1 = (in1 < BLK).astype(jnp.int32)
    c0 = jnp.clip(c0 * has0, 0, GW - 1)
    c1 = jnp.clip(c1 * has1, 0, GW - 1)
    table = jnp.zeros((W, 128), jnp.int32)
    for i, column in ((0, c0), (1, c1), (4, has0), (5, has1)):
        table = jnp.where(lane == i, column, table)
    tab_out[...] = table
    put_tab = pltpu.make_async_copy(tab_out, tab_s, local_sem.at[4])
    put_tab.start()
    put_tab.wait()
    get_child.wait()

    @pl.loop(0, W)
    def _(s):
        for j in range(2):
            row = jnp.clip(child_v[pl.ds(tab_s[s, j], 1), :] - me * CW, 0, CW - 1)
            kids_out[pl.ds(2 * s + j, 1), :] = row

    put_kids = pltpu.make_async_copy(kids_out, kids_s, local_sem.at[5])
    put_kids.start()
    put_kids.wait()

    def gather(slot, i, dst):
        @pl.loop(0, CH // 16)
        def _(g):
            base = pl.multiple_of(g * 16, 16)
            rows = [cent_f[pl.ds(kids_s[slot, base + r], 1), :] for r in range(16)]
            for r in range(16):
                stage[i, pl.ds(base + r, 1), :] = rows[r]

        dst[...] = stage[i].astype(jnp.bfloat16)

    def c_copy(half, to, sender):
        part = pl.ds(4 * half, 4)
        return remote(
            c_send.at[to, part], ctab.at[part, :, lanes_of(sender)],
            c_ss.at[half * N + to], c_rs.at[half * N + sender], narrow=to,
        )

    def own_children(half):
        part = pl.ds(4 * half, 4)
        return pltpu.make_async_copy(
            c_send.at[mn, part], ctab.at[part, :, lanes_of(mn)], local_sem.at[6 + half]
        )

    def send_children(half):
        @pl.loop(0, N)
        def _(k):
            to = narrow_at(k)
            far = lax.rem(2 * mz + 4 - to // 2, 4)

            @pl.loop(0, 2)
            def _(i):
                dx = 2 * half + i
                for h in range(2):
                    w = behind(dx, far + 4 * h)
                    gather(2 * w + lax.rem(to, 2), h, c_send.at[to, 2 * dx + h])

            @pl.when(k > 0)
            def _():
                c_copy(half, to, mn).start()

            @pl.when(k == 0)
            def _():
                own_children(half).start()

    send_children(0)
    send_children(1)

    kids = kids_out[...]
    lane64 = lax.broadcasted_iota(jnp.int32, (2 * W, CH), 1)
    twice = jnp.zeros((2 * W, CH), jnp.int32)
    for d in range(1, 16):
        same = (kids == pltpu.roll(kids, d, 1)) & (lax.rem(lane64, 16) >= d)
        twice = jnp.where(same, 1, twice)
    any_twice = jnp.max(twice, axis=1, keepdims=True)
    for d in (1, 2, 4, 8):
        twice = jnp.maximum(twice, pltpu.roll(twice, CH - d, 1))
    dup_out[...] = jnp.where(lane64 == 1, any_twice, twice)

    square_sub = lax.broadcasted_iota(jnp.int32, (CH, CH), 0)
    eye = square_sub == lax.broadcasted_iota(jnp.int32, (CH, CH), 1)

    def as_row(column):
        return jnp.sum(jnp.where(eye, column, 0.0), axis=0, keepdims=True)

    row8 = lax.broadcasted_iota(jnp.int32, (8, CH), 0)

    def weigh(dx, h):
        slot = 2 * dx + h
        x = x_in[dx, h]
        squares = jnp.zeros((CH, F), jnp.float32)
        for n in range(N):
            part = ctab[slot, :, n * F : (n + 1) * F].astype(jnp.float32)
            squares = squares + part * part
        lengths = jnp.sum(squares, axis=1, keepdims=True)
        dots = lax.dot_general(ctab[slot], x, NT, preferred_element_type=jnp.float32)
        score = (2.0 * dots - lengths) * (1.0 / math.sqrt(D))
        e = jnp.exp(score - jnp.max(score, axis=0, keepdims=True))
        weights = (e / jnp.sum(e, axis=0, keepdims=True)).astype(jnp.bfloat16)
        counts = as_row(jnp.sum(weights.astype(jnp.float32), axis=1, keepdims=True))
        swork[h] = jnp.dot(weights, x, preferred_element_type=jnp.float32)
        for n in range(N):
            part = swork[h, :, n * F : (n + 1) * F]
            top = jnp.maximum(jnp.max(jnp.abs(part), axis=1, keepdims=True), 1e-30)
            coded = jnp.round(part * (32767.0 / top)).astype(jnp.int32)
            q_send[slot, n] = coded.astype(jnp.int16)
            scales = as_row(top * (1.0 / 32767.0))
            t_send[slot, n] = jnp.where(row8 == 0, scales, jnp.where(row8 == 1, counts, 0.0))

    def q_copy(slot, to, w, j):
        return remote(
            q_send.at[slot, to], q_out.at[w, j],
            q_ss.at[slot * N + to], q_rs.at[2 * w + j], narrow=to,
        )

    def t_copy(slot, to, w, j):
        return remote(
            t_send.at[slot, to], sc_out.at[w, j],
            t_ss.at[slot * N + to], t_rs.at[2 * w + j], narrow=to,
        )

    def own_sums(slot, w):
        return pltpu.make_async_copy(q_send.at[slot, mn], q_out.at[w, core], own_sem.at[slot])

    def send_sums(dx, h):
        slot, w = 2 * dx + h, behind(dx, first + 4 * h)

        @pl.loop(1, N)
        def _(k):
            q_copy(slot, narrow_at(k), w, core).start()
            t_copy(slot, narrow_at(k), w, core).start()

        own_sums(slot, w).start()
        sc_out[w, core] = t_send[slot, mn]

    half_sub = lax.broadcasted_iota(jnp.int32, (CH // 2, CH), 0)
    counts_v[...] = jnp.zeros_like(counts_v)

    def take_sums(dx):
        @pl.loop(0, Z)
        def _(dz):
            w = behind(dx, dz)
            for j in range(2):
                sender = 2 * lax.rem(2 * mz + Z - dz, 4) + j

                @pl.when(sender != mn)
                def _():
                    q_copy(0, narrow_at(1), w, j).wait_recv()
                    t_copy(0, narrow_at(1), w, j).wait_recv()

            lows, lefts = [], []
            for j in range(2):
                kid = kids_out[pl.ds(2 * w + j, 1), :]
                row = jnp.where(tab_s[w, 4 + j] > 0, sc_out[w, j][1:2, :], 0.0)
                lows.append(((kid & 127) == square_sub).astype(jnp.bfloat16))
                left = jnp.where((kid >> 7) == half_sub, row, 0.0)
                pieces = []
                for _ in range(3):
                    pieces.append(left.astype(jnp.bfloat16))
                    left = left - pieces[-1].astype(jnp.float32)
                pieces.append(jnp.zeros((CH // 2, CH), jnp.bfloat16))
                lefts.append(jnp.concatenate(pieces, axis=0))
            total = lax.dot_general(
                jnp.concatenate(lows, axis=1), jnp.concatenate(lefts, axis=1), NT,
                preferred_element_type=jnp.float32,
            )
            counts_v[...] += total

    @pl.loop(0, X)
    def _(dx):
        @pl.when(dx < X - 2)
        def _():
            blocks_left(dx)
            send_blocks(dx + 2)

        @pl.when(lax.rem(dx, 2) == 0)
        def _():
            @pl.loop(1, N)
            def _(k):
                c_copy(dx // 2, narrow_at(k), narrow_at(k)).wait_recv()

            own_children(dx // 2).wait()

        for h in range(2):
            have_blocks(dx, h)
            weigh(dx, h)
            send_sums(dx, h)

        take_sums(dx)

    counts = counts_v[...]
    counts = counts[:, :CH] + pltpu.roll(counts[:, :CH], CH // 2, 1) + counts[:, CH:]
    factor_out[...] = 1.0 / (counts + 1.0)
    blocks_left(X - 2)
    blocks_left(X - 1)

    @pl.loop(1, N)
    def _(k):
        to = narrow_at(k)
        for half in range(2):
            c_copy(half, to, mn).wait_send()

        @pl.loop(0, 2 * X)
        def _(slot):
            q_copy(slot, to, 0, 0).wait_send()
            t_copy(slot, to, 0, 0).wait_send()

    @pl.loop(0, 2 * X)
    def _(slot):
        own_sums(slot, 0).wait()


def exchange(ids, children, centroids, embeddings):
    vm = pl.BlockSpec(memory_space=pltpu.VMEM)
    hbm = pl.BlockSpec(memory_space=pl.ANY)
    dma = pltpu.SemaphoreType.DMA
    bf, f32, i32, i16 = jnp.bfloat16, jnp.float32, jnp.int32, jnp.int16
    return pl.pallas_call(
        exchange_kernel,
        out_shape=(
            jax.ShapeDtypeStruct((W, 2, CH, F), i16),
            jax.ShapeDtypeStruct((W, 2, 8, CH), f32),
            jax.ShapeDtypeStruct((2 * W, CH), i32),
            jax.ShapeDtypeStruct((W, 128), i32),
            jax.ShapeDtypeStruct((2 * W, CH), i32),
            jax.ShapeDtypeStruct((CH, CH), f32),
        ),
        in_specs=[vm, hbm, hbm, hbm],
        out_specs=(hbm, vm, vm, vm, vm, vm),
        scratch_shapes=[
            pltpu.VMEM((W, 8, 128), i32),
            pltpu.VMEM((W, 128), i32),
            pltpu.SMEM((W, 128), i32),
            pltpu.SMEM((W, 128), i32),
            pltpu.SMEM((2 * W, CH), i32),
            pltpu.VMEM((BLK, RB, F), bf),
            pltpu.VMEM((CW, F), bf),
            pltpu.VMEM((GW, CH), i32),
            pltpu.VMEM((CH, 2 * CH), f32),
            pltpu.VMEM((CW, F), f32),
            pltpu.VMEM((2, CH, F), f32),
            pltpu.VMEM((W, 2, RB, F), bf),
            pltpu.VMEM((X, 2, RB, D), bf),
            pltpu.VMEM((N, 2 * X, CH, F), bf),
            pltpu.VMEM((2 * X, CH, D), bf),
            pltpu.VMEM((2 * X, N, CH, F), i16),
            pltpu.VMEM((2 * X, N, 8, CH), f32),
            pltpu.VMEM((2, CH, D), f32),
            dma((8,)),
            dma((W,)), dma((W,)),
            dma((2 * W,)), dma((2 * W,)),
            dma((2 * N,)), dma((2 * N,)),
            dma((2 * W,)), dma((2 * W,)),
            dma((2 * W,)), dma((2 * W,)),
            dma((2 * X,)),
        ],
        compiler_params=pltpu.CompilerParams(
            collective_id=0, has_side_effects=True, vmem_limit_bytes=60 * 1024 * 1024
        ),
        name="exchange",
    )(ids, children, centroids, embeddings)


PARTS = 8
BATCH = 16


def scatter_kernel(
    kids_s, tab_s, dup_s, q_hbm, sc_ref, factor_ref, cent_hbm, out_hbm,
    q_ref, cent_b, slots, acc, cent_sem, q_sem, out_sem,
):
    lane = lax.broadcasted_iota(jnp.int32, (CH, CH), 1)
    eye = lane == lax.broadcasted_iota(jnp.int32, (CH, CH), 0)
    per, rows_per = W // PARTS, CW // PARTS

    def cent_copy(i):
        rows = pl.ds(pl.multiple_of(i * rows_per, rows_per), rows_per)
        return pltpu.make_async_copy(cent_hbm.at[rows], cent_b.at[rows], cent_sem.at[i])

    def q_copy(i):
        rows = pl.ds(i * per, per)
        return pltpu.make_async_copy(q_hbm.at[rows], q_ref.at[rows], q_sem.at[i])

    def out_copy(i):
        rows = pl.ds(pl.multiple_of(i * rows_per, rows_per), rows_per)
        return pltpu.make_async_copy(acc.at[rows], out_hbm.at[rows], out_sem.at[i])

    @pl.loop(0, PARTS)
    def _(i):
        cent_copy(i).start()

    @pl.loop(0, PARTS)
    def _(i):
        q_copy(i).start()

    @pl.loop(0, PARTS)
    def _(i):
        cent_copy(i).wait()
        for t in range(4):
            step = rows_per // 4
            rows = pl.ds(pl.multiple_of(i * rows_per + t * step, step), step)
            acc[rows, :] = cent_b[rows, :].astype(jnp.float32)

    def add_batch(slot, base):
        at = [pl.ds(kids_s[slot, base + i], 1) for i in range(BATCH)]
        sums = [acc[at[i], :] + slots[slot, pl.ds(base + i, 1), :] for i in range(BATCH)]
        for i in range(BATCH):
            acc[at[i], :] = sums[i]

    def decode(s):
        for j in range(2):
            scale = jnp.sum(
                jnp.where(eye, sc_ref[s, j][0:1, :], 0.0), axis=1, keepdims=True
            )
            slots[2 * s + j] = q_ref[s, j].astype(jnp.int32).astype(jnp.float32) * scale

    def add_slot(slot):
        @pl.when(dup_s[slot, 1] == 0)
        def _():
            for g in range(CH // BATCH):
                add_batch(slot, g * BATCH)

        @pl.when(dup_s[slot, 1] > 0)
        def _():
            @pl.loop(0, CH // BATCH)
            def _(g):
                base = pl.multiple_of(g * BATCH, BATCH)

                @pl.when(dup_s[slot, base] == 0)
                def _():
                    add_batch(slot, base)

                @pl.when(dup_s[slot, base] > 0)
                def _():
                    for i in range(BATCH):
                        at = pl.ds(kids_s[slot, base + i], 1)
                        acc[at, :] = acc[at, :] + slots[slot, pl.ds(base + i, 1), :]

    @pl.loop(0, PARTS)
    def _(i):
        q_copy(i).wait()

        for t in range(per):
            decode(i * per + t)

    @pl.loop(0, W)
    def _(s):
        for j in range(2):

            @pl.when(tab_s[s, 4 + j] > 0)
            def _():
                add_slot(2 * s + j)

    factors = factor_ref[...]

    for i in range(PARTS):
        for h in range(i * (rows_per // CH), (i + 1) * (rows_per // CH)):
            rows = pl.ds(h * CH, CH)
            acc[rows, :] = acc[rows, :] * factors[:, h : h + 1]
        out_copy(i).start()

    @pl.loop(0, PARTS)
    def _(i):
        out_copy(i).wait()


def scatter(kids, table, twice, q, scales, factors, centroids):
    vm = pl.BlockSpec(memory_space=pltpu.VMEM)
    sm = pl.BlockSpec(memory_space=pltpu.SMEM)
    hbm = pl.BlockSpec(memory_space=pl.ANY)
    return pl.pallas_call(
        scatter_kernel,
        out_shape=jax.ShapeDtypeStruct((CW, F), jnp.float32),
        in_specs=[sm, sm, sm, hbm, vm, vm, hbm],
        out_specs=hbm,
        scratch_shapes=[
            pltpu.VMEM((W, 2, CH, F), jnp.int16),
            pltpu.VMEM((CW, F), jnp.bfloat16),
            pltpu.VMEM((2 * W, CH, F), jnp.float32),
            pltpu.VMEM((CW, F), jnp.float32),
            pltpu.SemaphoreType.DMA((PARTS,)),
            pltpu.SemaphoreType.DMA((PARTS,)),
            pltpu.SemaphoreType.DMA((PARTS,)),
        ],
        compiler_params=pltpu.CompilerParams(vmem_limit_bytes=60 * 1024 * 1024),
        name="scatter",
    )(kids, table, twice, q, scales, factors, centroids)


def body(embeddings, centroids, level2_cluster_index, child_lists):
    ids = jnp.pad(level2_cluster_index, (0, 128 - BLK), constant_values=-1)
    ids = jnp.broadcast_to(ids[None, :], (8, 128))
    q, scales, kids, table, twice, factors = exchange(
        ids, child_lists, centroids, embeddings.reshape(BLK, RB, F)
    )
    return scatter(kids, table, twice, q, scales, factors, centroids)


def solution(mesh):
    placed = (P("wide", "narrow"), P("wide", "narrow"), P("wide"), P("wide", None))
    return jax.shard_map(
        body, mesh=mesh, in_specs=placed, out_specs=P("wide", "narrow"), check_vma=False
    )
```

```python
import functools
import math

import jax
import jax.numpy as jnp
from jax import lax
from jax.experimental import pallas as pl
from jax.experimental.pallas import tpu as pltpu
from jax.sharding import PartitionSpec as P

D = 1024
X, Z = 4, 8
W = X * Z
N = 8
RB = 256
CH = 128
F = 128
BLK = 16
GW = 512
CW = 8192
MESH = pl.DeviceIdType.MESH
NT = (((1,), (1,)), ((), ()))


def shifted(me, dx, dz):
    return lax.rem(me // Z + dx, X) * Z + lax.rem(lax.rem(me, Z) + dz, Z)


def at_offset(me, k):
    return shifted(me, k // Z, lax.rem(k, Z))


def split_groups(owner, lane):
    here = lane < BLK
    earlier = jnp.zeros(owner.shape, jnp.int32)
    later = jnp.zeros(owner.shape, jnp.int32)
    for d in range(1, BLK):
        earlier = jnp.where((owner == pltpu.roll(owner, d, 1)) & (lane >= d), 1, earlier)
        later = jnp.where(
            (owner == pltpu.roll(owner, 128 - d, 1)) & (lane + d < BLK), 1, later
        )

    def before(flags):
        total = flags
        for d in (1, 2, 4, 8):
            total = total + jnp.where(lane >= d, pltpu.roll(total, d, 1), 0)
        return total - flags

    head = jnp.where(here & (earlier == 0) & (later == 1), 1, 0)
    single = jnp.where(here & (earlier == 0) & (later == 0), 1, 0)
    room = BLK // 2 - jnp.sum(head, axis=1, keepdims=True)
    one = jnp.where((single == 1) & (before(single) < room), 1, head)
    two = jnp.where(here, 1 - one, 0)
    return (one == 1, two == 1), (before(one), before(two))


def exchange_kernel(
    given_ref, child_ref, cent_ref, emb_ref,
    q_out, sc_out, kids_out, tab_out, dup_out, factor_out,
    ids_ref, ids_all, own_v, own_s, tab_s, kids_s, emb_v, cent_b, child_v, counts_v, cent_f, stage,
    e_send, xfull, d_send, c_send, ctab, q_send, t_send, u_send, scu, swork,
    local_sem, ids_ss, ids_rs, e_ss, e_rs, d_ss, d_rs, c_ss, c_rs, q_ss, q_rs, t_ss, t_rs,
    u_ss, u_rs, v_ss, v_rs, own_sem, d_one, d_two, q_one, q_two, t_one, t_two,
):
    me = lax.axis_index("wide")
    mn = lax.axis_index("narrow")
    d_recv, q_recv, t_recv = (d_one, d_two), (q_one, q_two), (t_one, t_two)

    def remote(src, dst, ss, rs, **where):
        return pltpu.make_async_remote_copy(
            src_ref=src, dst_ref=dst, send_sem=ss, recv_sem=rs,
            device_id=where, device_id_type=MESH,
        )

    def narrow_at(k):
        return lax.rem(mn + k, N)

    def lanes_of(n):
        return pl.ds(pl.multiple_of(n * F, F), F)

    def wide_at(i):
        m = lax.rem(i, Z)
        u, v = m // 2 + 1, lax.rem(m, 2)
        dz = (u * (1 - v) + (Z - u) * v) * (1 - m // (Z - 1))
        return shifted(me, lax.rem(i // Z + 1, X), dz)

    get_emb = pltpu.make_async_copy(emb_ref, emb_v, local_sem.at[0])
    get_cent = pltpu.make_async_copy(cent_ref, cent_b, local_sem.at[1])
    get_child = pltpu.make_async_copy(child_ref, child_v, local_sem.at[2])
    get_emb.start()
    get_cent.start()
    get_child.start()
    ids_ref[...] = jnp.full((1, 128), -1, jnp.int32)
    ids_ref[:, 0:BLK] = given_ref[...]
    barrier = pltpu.get_barrier_semaphore()

    @pl.loop(1, W)
    def _(k):
        pl.semaphore_signal(
            barrier, inc=1, device_id={"wide": at_offset(me, k)}, device_id_type=MESH
        )

    @pl.loop(1, N)
    def _(k):
        pl.semaphore_signal(
            barrier, inc=1, device_id={"narrow": narrow_at(k)}, device_id_type=MESH
        )

    lane = lax.broadcasted_iota(jnp.int32, (W, 128), 1)
    sub = lax.broadcasted_iota(jnp.int32, (W, 128), 0)
    owner = jnp.where(lane < BLK, jnp.broadcast_to(ids_ref[...], (W, 128)) >> 9, -1)
    groups, places = split_groups(owner, lane)
    own = jnp.zeros((W, 128), jnp.int32)
    ranks = jnp.zeros((W, 128), jnp.int32)
    for g in range(2):
        mine = groups[g] & (owner == sub)
        place = jnp.sum(jnp.where(mine, places[g], 0), axis=1, keepdims=True)
        own = jnp.where(lane == g, jnp.clip(place, 0, N - 1), own)
        this = groups[g] & (places[g] + N * g == sub)
        block = jnp.sum(jnp.where(this, lane, 0), axis=1, keepdims=True)
        its = jnp.sum(jnp.where(this, owner, 0), axis=1, keepdims=True)
        ranks = jnp.where(lane == 0, ranks + block, ranks)
        ranks = jnp.where(lane == 1, ranks + its, ranks)
    own_v[0:W, :] = own
    own_v[W : 2 * W, :] = jnp.clip(ranks, 0, W - 1)
    put_own = pltpu.make_async_copy(own_v, own_s, local_sem.at[3])
    put_own.start()
    pl.semaphore_wait(barrier, W - 1 + N - 1)

    def ids_copy(k):
        return remote(
            ids_ref, ids_all.at[me], ids_ss.at[k], ids_rs.at[k], wide=at_offset(me, k)
        )

    @pl.loop(1, W)
    def _(k):
        ids_copy(k).start()

    ids_all[me] = ids_ref[...]

    put_own.wait()
    get_emb.wait()

    @pl.loop(0, BLK)
    def _(r):
        e_send[lax.rem(r, N), r // N] = emb_v[lax.rem(own_s[W + r, 0], BLK)]

    def e_copy(k):
        to = narrow_at(k)
        return remote(
            e_send.at[to], xfull.at[:, :, lanes_of(mn)], e_ss.at[k], e_rs.at[k], narrow=to
        )

    @pl.loop(1, N)
    def _(k):
        e_copy(k).start()

    own_e = pltpu.make_async_copy(e_send.at[mn], xfull.at[:, :, lanes_of(mn)], local_sem.at[0])
    own_e.start()

    get_cent.wait()

    @pl.loop(0, CW // 256)
    def _(i):
        rows = pl.ds(pl.multiple_of(i * 256, 256), 256)
        cent_f[rows, :] = cent_b[rows, :].astype(jnp.float32)

    @pl.loop(1, W)
    def _(k):
        ids_copy(k).wait()

    asked = ids_all[:, 0, :]
    owner = jnp.where(lane < BLK, asked >> 9, -1)
    groups, _ = split_groups(owner, lane)
    table = jnp.zeros((W, 128), jnp.int32)
    for g in range(2):
        mine = groups[g] & (owner == me)
        has = jnp.sum(jnp.where(mine, 1, 0), axis=1, keepdims=True)
        cluster = jnp.sum(jnp.where(mine, asked - me * GW, 0), axis=1, keepdims=True)
        table = jnp.where(lane == g, jnp.clip(cluster, 0, GW - 1), table)
        table = jnp.where(lane == 4 + g, has, table)
    tab_out[...] = table
    put_tab = pltpu.make_async_copy(tab_out, tab_s, local_sem.at[4])
    put_tab.start()
    put_tab.wait()
    get_child.wait()

    @pl.loop(0, W)
    def _(s):
        for g in range(2):
            row = jnp.clip(child_v[pl.ds(tab_s[s, g], 1), :] - me * CW, 0, CW - 1)
            kids_out[pl.ds(2 * s + g, 1), :] = row

    put_kids = pltpu.make_async_copy(kids_out, kids_s, local_sem.at[5])
    put_kids.start()
    put_kids.wait()

    def gather(g, p, dst):
        @pl.loop(0, CH // 16)
        def _(i):
            base = pl.multiple_of(i * 16, 16)
            rows = [
                cent_f[pl.ds(kids_s[2 * p + g, base + r], 1), :] for r in range(16)
            ]
            for r in range(16):
                stage[g, pl.ds(base + r, 1), :] = rows[r]

        dst[...] = stage[g].astype(jnp.bfloat16)

    def down_copy(g, i):
        to = wide_at(i)
        return remote(
            d_send.at[g, to], d_recv[g].at[me], d_ss.at[g * W + i], d_rs.at[g * W + i], wide=to
        )

    @pl.loop(0, W - 1)
    def _(i):
        gather(0, wide_at(i), d_send.at[0, wide_at(i)])
        down_copy(0, i).start()

    gather(0, me, d_one.at[me])

    @pl.loop(0, W - 1)
    def _(i):
        gather(1, wide_at(i), d_send.at[1, wide_at(i)])
        down_copy(0, i).wait_send()
        down_copy(1, i).start()

    gather(1, me, d_two.at[me])

    kids = kids_out[...]
    lane64 = lax.broadcasted_iota(jnp.int32, (2 * W, CH), 1)
    twice = jnp.zeros((2 * W, CH), jnp.int32)
    for d in range(1, 16):
        same = (kids == pltpu.roll(kids, d, 1)) & (lax.rem(lane64, 16) >= d)
        twice = jnp.where(same, 1, twice)
    any_twice = jnp.max(twice, axis=1, keepdims=True)
    for d in (1, 2, 4, 8):
        twice = jnp.maximum(twice, pltpu.roll(twice, CH - d, 1))
    dup_out[...] = jnp.where(lane64 == 1, any_twice, twice)

    own_e.wait()

    @pl.loop(1, N)
    def _(k):
        e_copy(k).wait()

    square_sub = lax.broadcasted_iota(jnp.int32, (CH, CH), 0)
    eye = square_sub == lax.broadcasted_iota(jnp.int32, (CH, CH), 1)

    def as_row(column):
        return jnp.sum(jnp.where(eye, column, 0.0), axis=0, keepdims=True)

    row4 = lax.broadcasted_iota(jnp.int32, (4, CH), 0)

    def weigh(g):
        x = xfull[g]
        squares = jnp.zeros((CH, F), jnp.float32)
        for n in range(N):
            part = ctab[g, :, n * F : (n + 1) * F].astype(jnp.float32)
            squares = squares + part * part
        lengths = jnp.sum(squares, axis=1, keepdims=True)
        dots = lax.dot_general(ctab[g], x, NT, preferred_element_type=jnp.float32)
        score = (2.0 * dots - lengths) * (1.0 / math.sqrt(D))
        e = jnp.exp(score - jnp.max(score, axis=0, keepdims=True))
        weights = (e / jnp.sum(e, axis=0, keepdims=True)).astype(jnp.bfloat16)
        counts = as_row(jnp.sum(weights.astype(jnp.float32), axis=1, keepdims=True))
        swork[...] = jnp.dot(weights, x, preferred_element_type=jnp.float32)
        for n in range(N):
            part = swork[:, n * F : (n + 1) * F]
            top = jnp.maximum(jnp.max(jnp.abs(part), axis=1, keepdims=True), 1e-30)
            coded = jnp.round(part * (32767.0 / top)).astype(jnp.int32)
            q_send[g, n] = coded.astype(jnp.int16)
            scales = as_row(top * (1.0 / 32767.0))
            t_send[g, n] = jnp.where(lax.rem(row4, 2) == 0, scales, counts)

    def c_copy(g, k):
        to = narrow_at(k)
        return remote(
            c_send.at[g, to], ctab.at[g, :, lanes_of(mn)],
            c_ss.at[g * N + k], c_rs.at[g * N + k], narrow=to,
        )

    def q_copy(g, k):
        to = narrow_at(k)
        return remote(
            q_send.at[g, to], q_recv[g].at[mn],
            q_ss.at[g * N + k], q_rs.at[g * N + k], narrow=to,
        )

    def t_copy(g, k):
        to = narrow_at(k)
        return remote(
            t_send.at[g, to], t_recv[g].at[mn],
            t_ss.at[g * N + k], t_rs.at[g * N + k], narrow=to,
        )

    def up_copy(g, i):
        to = wide_at(i)
        return remote(
            u_send.at[g, to], q_out.at[me, g], u_ss.at[g * W + i], u_rs.at[g * W + i], wide=to
        )

    def own_sums(g):
        return pltpu.make_async_copy(u_send.at[g, me], q_out.at[me, g], own_sem.at[g])

    def scale_copy(k):
        to = at_offset(me, k)
        return remote(scu.at[to], sc_out.at[me], v_ss.at[k], v_rs.at[k], wide=to)

    def scales_for(p):
        return jnp.where(row4 < 2, t_one[own_s[p, 0]], t_two[own_s[p, 1]])

    for g in range(2):

        @pl.loop(0, W - 1)
        def _(i):
            down_copy(g, i).wait_recv()

        @pl.loop(0, N)
        def _(k):
            c_send[g, narrow_at(k)] = d_recv[g][own_s[W + N * g + narrow_at(k), 1]]

            @pl.when(k > 0)
            def _():
                c_copy(g, k).start()

        ctab[g, :, lanes_of(mn)] = c_send[g, mn]

        @pl.loop(1, N)
        def _(k):
            c_copy(g, k).wait()

        weigh(g)

        @pl.loop(1, N)
        def _(k):
            q_copy(g, k).start()
            t_copy(g, k).start()

        q_recv[g][mn] = q_send[g, mn]
        t_recv[g][mn] = t_send[g, mn]

        @pl.loop(1, N)
        def _(k):
            q_copy(g, k).wait()
            t_copy(g, k).wait()

        if g == 1:

            @pl.loop(1, W)
            def _(k):
                p = at_offset(me, k)
                scu[p] = scales_for(p)
                scale_copy(k).start()

            sc_out[me] = scales_for(me)

        @pl.loop(0, W - 1)
        def _(i):
            p = wide_at(i)
            u_send[g, p] = q_recv[g][own_s[p, g]]
            up_copy(g, i).start()

        u_send[g, me] = q_recv[g][own_s[me, g]]
        own_sums(g).start()

    @pl.loop(1, W)
    def _(k):
        scale_copy(k).wait()

    half_sub = lax.broadcasted_iota(jnp.int32, (CH // 2, CH), 0)
    counts_v[...] = jnp.zeros_like(counts_v)

    @pl.loop(0, W)
    def _(w):
        tile = sc_out[w]
        lows, lefts = [], []
        for g in range(2):
            kid = kids_out[pl.ds(2 * w + g, 1), :]
            row = jnp.where(tab_s[w, 4 + g] > 0, tile[2 * g + 1 : 2 * g + 2, :], 0.0)
            lows.append(((kid & 127) == square_sub).astype(jnp.bfloat16))
            left = jnp.where((kid >> 7) == half_sub, row, 0.0)
            pieces = []
            for _ in range(3):
                pieces.append(left.astype(jnp.bfloat16))
                left = left - pieces[-1].astype(jnp.float32)
            pieces.append(jnp.zeros((CH // 2, CH), jnp.bfloat16))
            lefts.append(jnp.concatenate(pieces, axis=0))
        counts_v[...] += lax.dot_general(
            jnp.concatenate(lows, axis=1), jnp.concatenate(lefts, axis=1), NT,
            preferred_element_type=jnp.float32,
        )

    counts = counts_v[...]
    counts = counts[:, :CH] + pltpu.roll(counts[:, :CH], CH // 2, 1) + counts[:, CH:]
    factor_out[...] = 1.0 / (counts + 1.0)

    @pl.loop(0, W - 1)
    def _(i):
        down_copy(1, i).wait_send()

    for g in range(2):
        own_sums(g).wait()

        @pl.loop(0, W - 1)
        def _(i):
            up_copy(g, i).wait()


def exchange(ids, children, centroids, embeddings):
    vm = pl.BlockSpec(memory_space=pltpu.VMEM)
    hbm = pl.BlockSpec(memory_space=pl.ANY)
    dma = pltpu.SemaphoreType.DMA
    bf, f32, i32, i16 = jnp.bfloat16, jnp.float32, jnp.int32, jnp.int16
    return pl.pallas_call(
        exchange_kernel,
        out_shape=(
            jax.ShapeDtypeStruct((W, 2, CH, F), i16),
            jax.ShapeDtypeStruct((W, 4, CH), f32),
            jax.ShapeDtypeStruct((2 * W, CH), i32),
            jax.ShapeDtypeStruct((W, 128), i32),
            jax.ShapeDtypeStruct((2 * W, CH), i32),
            jax.ShapeDtypeStruct((CH, CH), f32),
        ),
        in_specs=[vm, hbm, hbm, hbm],
        out_specs=(hbm, vm, vm, vm, vm, vm),
        scratch_shapes=[
            pltpu.VMEM((1, 128), i32),
            pltpu.VMEM((W, 1, 128), i32),
            pltpu.VMEM((2 * W, 128), i32),
            pltpu.SMEM((2 * W, 128), i32),
            pltpu.SMEM((W, 128), i32),
            pltpu.SMEM((2 * W, CH), i32),
            pltpu.VMEM((BLK, RB, F), bf),
            pltpu.VMEM((CW, F), bf),
            pltpu.VMEM((GW, CH), i32),
            pltpu.VMEM((CH, 2 * CH), f32),
            pltpu.VMEM((CW, F), f32),
            pltpu.VMEM((2, CH, F), f32),
            pltpu.VMEM((N, 2, RB, F), bf),
            pltpu.VMEM((2, RB, D), bf),
            pltpu.VMEM((2, W, CH, F), bf),
            pltpu.VMEM((2, N, CH, F), bf),
            pltpu.VMEM((2, CH, D), bf),
            pltpu.VMEM((2, N, CH, F), i16),
            pltpu.VMEM((2, N, 4, CH), f32),
            pltpu.VMEM((2, W, CH, F), i16),
            pltpu.VMEM((W, 4, CH), f32),
            pltpu.VMEM((CH, D), f32),
            dma((6,)),
            dma((W,)), dma((W,)),
            dma((N,)), dma((N,)),
            dma((2 * W,)), dma((2 * W,)),
            dma((2 * N,)), dma((2 * N,)),
            dma((2 * N,)), dma((2 * N,)),
            dma((2 * N,)), dma((2 * N,)),
            dma((2 * W,)), dma((2 * W,)),
            dma((W,)), dma((W,)),
            dma((2,)),
            pltpu.VMEM((W, CH, F), bf),
            pltpu.VMEM((W, CH, F), bf),
            pltpu.VMEM((N, CH, F), i16),
            pltpu.VMEM((N, CH, F), i16),
            pltpu.VMEM((N, 4, CH), f32),
            pltpu.VMEM((N, 4, CH), f32),
        ],
        compiler_params=pltpu.CompilerParams(
            collective_id=0, has_side_effects=True, vmem_limit_bytes=60 * 1024 * 1024
        ),
        name="exchange",
    )(ids, children, centroids, embeddings)


PARTS = 8
BATCH = 16


def scatter_kernel(
    kids_s, tab_s, dup_s, q_hbm, sc_ref, factor_ref, cent_hbm, out_hbm,
    q_ref, cent_b, slots, acc, acc_two, cent_sem, q_sem, out_sem,
):
    lane = lax.broadcasted_iota(jnp.int32, (CH, CH), 1)
    eye = lane == lax.broadcasted_iota(jnp.int32, (CH, CH), 0)
    per, rows_per = W // PARTS, CW // PARTS

    def cent_copy(i):
        rows = pl.ds(pl.multiple_of(i * rows_per, rows_per), rows_per)
        return pltpu.make_async_copy(cent_hbm.at[rows], cent_b.at[rows], cent_sem.at[i])

    def q_copy(i):
        rows = pl.ds(i * per, per)
        return pltpu.make_async_copy(q_hbm.at[rows], q_ref.at[rows], q_sem.at[i])

    def out_copy(i):
        rows = pl.ds(pl.multiple_of(i * rows_per, rows_per), rows_per)
        return pltpu.make_async_copy(acc.at[rows], out_hbm.at[rows], out_sem.at[i])

    @pl.loop(0, PARTS)
    def _(i):
        cent_copy(i).start()

    @pl.loop(0, PARTS)
    def _(i):
        q_copy(i).start()

    @pl.loop(0, PARTS)
    def _(i):
        cent_copy(i).wait()
        for t in range(4):
            step = rows_per // 4
            rows = pl.ds(pl.multiple_of(i * rows_per + t * step, step), step)
            acc[rows, :] = cent_b[rows, :].astype(jnp.float32)
            acc_two[rows, :] = jnp.zeros((step, F), jnp.float32)

    def add_batch(slot, base, *into):
        rows = [(to, base + BATCH * t + i) for t, to in enumerate(into) for i in range(BATCH)]
        at = [pl.ds(kids_s[slot, r], 1) for _, r in rows]
        sums = [
            to[at[i], :] + slots[slot, pl.ds(r, 1), :] for i, (to, r) in enumerate(rows)
        ]
        for i, (to, _) in enumerate(rows):
            to[at[i], :] = sums[i]

    def decode(s):
        for j in range(2):
            scale = jnp.sum(
                jnp.where(eye, sc_ref[s][2 * j : 2 * j + 1, :], 0.0), axis=1, keepdims=True
            )
            slots[2 * s + j] = q_ref[s, j].astype(jnp.int32).astype(jnp.float32) * scale

    def add_slot(slot):
        @pl.when(dup_s[slot, 1] == 0)
        def _():
            for g in range(CH // BATCH // 2):
                add_batch(slot, 2 * g * BATCH, acc, acc_two)

        @pl.when(dup_s[slot, 1] > 0)
        def _():
            @pl.loop(0, CH // BATCH)
            def _(g):
                base = pl.multiple_of(g * BATCH, BATCH)

                @pl.when(dup_s[slot, base] == 0)
                def _():
                    add_batch(slot, base, acc)

                @pl.when(dup_s[slot, base] > 0)
                def _():
                    for i in range(BATCH):
                        at = pl.ds(kids_s[slot, base + i], 1)
                        acc[at, :] = acc[at, :] + slots[slot, pl.ds(base + i, 1), :]

    @pl.loop(0, PARTS)
    def _(i):
        q_copy(i).wait()

        for t in range(per):
            decode(i * per + t)

    @pl.loop(0, W)
    def _(s):
        for j in range(2):

            @pl.when(tab_s[s, 4 + j] > 0)
            def _():
                add_slot(2 * s + j)

    factors = factor_ref[...]

    for i in range(PARTS):
        for h in range(i * (rows_per // CH), (i + 1) * (rows_per // CH)):
            rows = pl.ds(h * CH, CH)
            acc[rows, :] = (acc[rows, :] + acc_two[rows, :]) * factors[:, h : h + 1]
        out_copy(i).start()

    @pl.loop(0, PARTS)
    def _(i):
        out_copy(i).wait()


def scatter(kids, table, twice, q, scales, factors, centroids):
    vm = pl.BlockSpec(memory_space=pltpu.VMEM)
    sm = pl.BlockSpec(memory_space=pltpu.SMEM)
    hbm = pl.BlockSpec(memory_space=pl.ANY)
    return pl.pallas_call(
        scatter_kernel,
        out_shape=jax.ShapeDtypeStruct((CW, F), jnp.float32),
        in_specs=[sm, sm, sm, hbm, vm, vm, hbm],
        out_specs=hbm,
        scratch_shapes=[
            pltpu.VMEM((W, 2, CH, F), jnp.int16),
            pltpu.VMEM((CW, F), jnp.bfloat16),
            pltpu.VMEM((2 * W, CH, F), jnp.float32),
            pltpu.VMEM((CW, F), jnp.float32),
            pltpu.VMEM((CW, F), jnp.float32),
            pltpu.SemaphoreType.DMA((PARTS,)),
            pltpu.SemaphoreType.DMA((PARTS,)),
            pltpu.SemaphoreType.DMA((PARTS,)),
        ],
        compiler_params=pltpu.CompilerParams(vmem_limit_bytes=60 * 1024 * 1024),
        name="scatter",
    )(kids, table, twice, q, scales, factors, centroids)


def body(embeddings, centroids, level2_cluster_index, child_lists):
    ids = level2_cluster_index.reshape(1, BLK)
    q, scales, kids, table, twice, factors = exchange(
        ids, child_lists, centroids, embeddings.reshape(BLK, RB, F)
    )
    return scatter(kids, table, twice, q, scales, factors, centroids)


def solution(mesh):
    placed = (P("wide", "narrow"), P("wide", "narrow"), P("wide"), P("wide", None))
    return jax.shard_map(
        body, mesh=mesh, in_specs=placed, out_specs=P("wide", "narrow"), check_vma=False
    )
```

```python
import functools
import math

import jax
import jax.numpy as jnp
from jax import lax
from jax.experimental import pallas as pl
from jax.experimental.pallas import tpu as pltpu
from jax.sharding import PartitionSpec as P

D = 1024
X, Z = 4, 8
W = X * Z
N = 8
RB = 256
CH = 128
F = 128
BLK = 16
GW = 512
CW = 8192
MESH = pl.DeviceIdType.MESH
NT = (((1,), (1,)), ((), ()))


def shifted(me, dx, dz):
    return lax.rem(me // Z + dx, X) * Z + lax.rem(lax.rem(me, Z) + dz, Z)


def at_offset(me, k):
    return shifted(me, k // Z, lax.rem(k, Z))


def split_groups(owner, lane):
    here = lane < BLK
    earlier = jnp.zeros(owner.shape, jnp.int32)
    later = jnp.zeros(owner.shape, jnp.int32)
    for d in range(1, BLK):
        earlier = jnp.where((owner == pltpu.roll(owner, d, 1)) & (lane >= d), 1, earlier)
        later = jnp.where(
            (owner == pltpu.roll(owner, 128 - d, 1)) & (lane + d < BLK), 1, later
        )

    def before(flags):
        total = flags
        for d in (1, 2, 4, 8):
            total = total + jnp.where(lane >= d, pltpu.roll(total, d, 1), 0)
        return total - flags

    head = jnp.where(here & (earlier == 0) & (later == 1), 1, 0)
    single = jnp.where(here & (earlier == 0) & (later == 0), 1, 0)
    room = BLK // 2 - jnp.sum(head, axis=1, keepdims=True)
    one = jnp.where((single == 1) & (before(single) < room), 1, head)
    two = jnp.where(here, 1 - one, 0)
    return (one == 1, two == 1), (before(one), before(two))


def exchange_kernel(
    given_ref, child_ref, cent_ref, emb_ref,
    q_out, sc_out, kids_out, tab_out, factor_out,
    ids_ref, ids_all, own_v, own_s, tab_s, kids_s, emb_v, cent_b, child_v, counts_v, cent_f, stage,
    e_send, xfull, d_send, c_send, ctab, q_send, t_send, u_send, scu, swork,
    local_sem, ids_ss, ids_rs, e_ss, e_rs, d_ss, d_rs, c_ss, c_rs, q_ss, q_rs, t_ss, t_rs,
    u_ss, u_rs, v_ss, v_rs, own_sem, d_one, d_two, q_one, q_two, t_one, t_two,
):
    me = lax.axis_index("wide")
    mn = lax.axis_index("narrow")
    d_recv, q_recv, t_recv = (d_one, d_two), (q_one, q_two), (t_one, t_two)

    def remote(src, dst, ss, rs, **where):
        return pltpu.make_async_remote_copy(
            src_ref=src, dst_ref=dst, send_sem=ss, recv_sem=rs,
            device_id=where, device_id_type=MESH,
        )

    def narrow_at(k):
        return lax.rem(mn + k, N)

    def lanes_of(n):
        return pl.ds(pl.multiple_of(n * F, F), F)

    def wide_at(i):
        m = lax.rem(i, Z)
        u, v = m // 2 + 1, lax.rem(m, 2)
        dz = (u * (1 - v) + (Z - u) * v) * (1 - m // (Z - 1))
        return shifted(me, lax.rem(i // Z + 1, X), dz)

    get_emb = pltpu.make_async_copy(emb_ref, emb_v, local_sem.at[0])
    get_cent = pltpu.make_async_copy(cent_ref, cent_b, local_sem.at[1])
    get_child = pltpu.make_async_copy(child_ref, child_v, local_sem.at[2])
    get_emb.start()
    get_cent.start()
    get_child.start()
    ids_ref[...] = jnp.full((1, 128), -1, jnp.int32)
    ids_ref[:, 0:BLK] = given_ref[...]
    barrier = pltpu.get_barrier_semaphore()

    @pl.loop(1, W)
    def _(k):
        pl.semaphore_signal(
            barrier, inc=1, device_id={"wide": at_offset(me, k)}, device_id_type=MESH
        )

    @pl.loop(1, N)
    def _(k):
        pl.semaphore_signal(
            barrier, inc=1, device_id={"narrow": narrow_at(k)}, device_id_type=MESH
        )

    pl.semaphore_wait(barrier, W - 1 + N - 1)

    def ids_copy(k):
        return remote(
            ids_ref, ids_all.at[me], ids_ss.at[k], ids_rs.at[k], wide=at_offset(me, k)
        )

    @pl.loop(1, W)
    def _(k):
        ids_copy(k).start()

    ids_all[me] = ids_ref[...]

    get_cent.wait()

    @pl.loop(0, CW // 256)
    def _(i):
        rows = pl.ds(pl.multiple_of(i * 256, 256), 256)
        cent_f[rows, :] = cent_b[rows, :].astype(jnp.float32)

    @pl.loop(1, W)
    def _(k):
        ids_copy(k).wait_recv()

    lane = lax.broadcasted_iota(jnp.int32, (W, 128), 1)
    sub = lax.broadcasted_iota(jnp.int32, (W, 128), 0)
    asked = ids_all[:, 0, :]
    owner = jnp.where(lane < BLK, asked >> 9, -1)
    groups, _ = split_groups(owner, lane)
    table = jnp.zeros((W, 128), jnp.int32)
    for g in range(2):
        mine = groups[g] & (owner == me)
        has = jnp.sum(jnp.where(mine, 1, 0), axis=1, keepdims=True)
        cluster = jnp.sum(jnp.where(mine, asked - me * GW, 0), axis=1, keepdims=True)
        table = jnp.where(lane == g, jnp.clip(cluster, 0, GW - 1), table)
        table = jnp.where(lane == 4 + g, has, table)
    tab_out[...] = table
    put_tab = pltpu.make_async_copy(tab_out, tab_s, local_sem.at[4])
    put_tab.start()
    put_tab.wait()
    get_child.wait()

    @pl.loop(0, W // 4)
    def _(i):
        spots = [(g, 4 * i + t) for g in range(2) for t in range(4)]
        rows = [child_v[pl.ds(tab_s[w, g], 1), :] for g, w in spots]
        for (g, w), row in zip(spots, rows):
            kids_out[pl.ds(g * W + w, 1), :] = jnp.clip(row - me * CW, 0, CW - 1)

    put_kids = pltpu.make_async_copy(kids_out, kids_s, local_sem.at[5])
    put_kids.start()
    put_kids.wait()

    def gather(g, p, dst):
        @pl.loop(0, CH // 16)
        def _(i):
            base = pl.multiple_of(i * 16, 16)
            rows = [
                cent_f[pl.ds(kids_s[g * W + p, base + r], 1), :] for r in range(16)
            ]
            for r in range(16):
                stage[g, pl.ds(base + r, 1), :] = rows[r]

        dst[...] = stage[g].astype(jnp.bfloat16)

    def down_copy(g, i):
        to = wide_at(i)
        return remote(
            d_send.at[g, to], d_recv[g].at[me], d_ss.at[g * W + i], d_rs.at[g * W + i], wide=to
        )

    @pl.loop(0, W - 1)
    def _(i):
        gather(0, wide_at(i), d_send.at[0, wide_at(i)])
        down_copy(0, i).start()

    gather(0, me, d_one.at[me])

    owner = jnp.where(lane < BLK, jnp.broadcast_to(ids_ref[...], (W, 128)) >> 9, -1)
    groups, places = split_groups(owner, lane)
    own = jnp.zeros((W, 128), jnp.int32)
    ranks = jnp.zeros((W, 128), jnp.int32)
    for g in range(2):
        mine = groups[g] & (owner == sub)
        place = jnp.sum(jnp.where(mine, places[g], 0), axis=1, keepdims=True)
        own = jnp.where(lane == g, jnp.clip(place, 0, N - 1), own)
        this = groups[g] & (places[g] + N * g == sub)
        block = jnp.sum(jnp.where(this, lane, 0), axis=1, keepdims=True)
        its = jnp.sum(jnp.where(this, owner, 0), axis=1, keepdims=True)
        ranks = jnp.where(lane == 0, ranks + block, ranks)
        ranks = jnp.where(lane == 1, ranks + its, ranks)
    own_v[0:W, :] = own
    own_v[W : 2 * W, :] = jnp.clip(ranks, 0, W - 1)
    put_own = pltpu.make_async_copy(own_v, own_s, local_sem.at[3])
    put_own.start()
    put_own.wait()
    get_emb.wait()

    @pl.loop(0, BLK)
    def _(r):
        e_send[lax.rem(r, N), r // N] = emb_v[lax.rem(own_s[W + r, 0], BLK)]

    def e_copy(k):
        to = narrow_at(k)
        return remote(
            e_send.at[to], xfull.at[:, :, lanes_of(mn)], e_ss.at[k], e_rs.at[k], narrow=to
        )

    @pl.loop(1, N)
    def _(k):
        e_copy(k).start()

    own_e = pltpu.make_async_copy(e_send.at[mn], xfull.at[:, :, lanes_of(mn)], local_sem.at[0])
    own_e.start()

    @pl.loop(0, W - 1)
    def _(i):
        gather(1, wide_at(i), d_send.at[1, wide_at(i)])
        down_copy(0, i).wait_send()
        down_copy(1, i).start()

    gather(1, me, d_two.at[me])

    kids = kids_out[...]
    lane64 = lax.broadcasted_iota(jnp.int32, (2 * W, CH), 1)
    twice = jnp.zeros((2 * W, CH), jnp.int32)
    for d in range(1, 16):
        same = (kids == pltpu.roll(kids, d, 1)) & (lax.rem(lane64, 16) >= d)
        twice = jnp.where(same, 1, twice)
    for d in (1, 2, 4, 8):
        twice = jnp.maximum(twice, pltpu.roll(twice, CH - d, 1))
    bit = jnp.where(lax.rem(lane64, 16) == 0, 1 << (lane64 >> 4), 0)
    bits = jnp.sum(twice * bit, axis=1, keepdims=True)
    table = jnp.where(lane == 6, bits[0:W], table)
    tab_out[...] = jnp.where(lane == 7, bits[W : 2 * W], table)

    own_e.wait()

    @pl.loop(1, N)
    def _(k):
        e_copy(k).wait()

    square_sub = lax.broadcasted_iota(jnp.int32, (CH, CH), 0)
    eye = square_sub == lax.broadcasted_iota(jnp.int32, (CH, CH), 1)

    def as_row(column):
        return jnp.sum(jnp.where(eye, column, 0.0), axis=0, keepdims=True)

    row4 = lax.broadcasted_iota(jnp.int32, (4, CH), 0)

    def weigh(g):
        x = xfull[g]
        squares = jnp.zeros((CH, F), jnp.float32)
        for n in range(N):
            part = ctab[g, :, n * F : (n + 1) * F].astype(jnp.float32)
            squares = squares + part * part
        lengths = jnp.sum(squares, axis=1, keepdims=True)
        dots = lax.dot_general(ctab[g], x, NT, preferred_element_type=jnp.float32)
        score = (2.0 * dots - lengths) * (1.0 / math.sqrt(D))
        e = jnp.exp(score - jnp.max(score, axis=0, keepdims=True))
        weights = (e / jnp.sum(e, axis=0, keepdims=True)).astype(jnp.bfloat16)
        counts = as_row(jnp.sum(weights.astype(jnp.float32), axis=1, keepdims=True))
        swork[...] = jnp.dot(weights, x, preferred_element_type=jnp.float32)
        for n in range(N):
            part = swork[:, n * F : (n + 1) * F]
            top = jnp.maximum(jnp.max(jnp.abs(part), axis=1, keepdims=True), 1e-30)
            coded = jnp.round(part * (32767.0 / top)).astype(jnp.int32)
            q_send[g, n] = coded.astype(jnp.int16)
            scales = as_row(top * (1.0 / 32767.0))
            t_send[g, n] = jnp.where(lax.rem(row4, 2) == 0, scales, counts)

    def c_copy(g, k):
        to = narrow_at(k)
        return remote(
            c_send.at[g, to], ctab.at[g, :, lanes_of(mn)],
            c_ss.at[g * N + k], c_rs.at[g * N + k], narrow=to,
        )

    def q_copy(g, k):
        to = narrow_at(k)
        return remote(
            q_send.at[g, to], q_recv[g].at[mn],
            q_ss.at[g * N + k], q_rs.at[g * N + k], narrow=to,
        )

    def t_copy(g, k):
        to = narrow_at(k)
        return remote(
            t_send.at[g, to], t_recv[g].at[mn],
            t_ss.at[g * N + k], t_rs.at[g * N + k], narrow=to,
        )

    def up_copy(g, i):
        to = wide_at(i)
        return remote(
            u_send.at[g, to], q_out.at[me, g], u_ss.at[g * W + i], u_rs.at[g * W + i], wide=to
        )

    def own_sums(g):
        return pltpu.make_async_copy(u_send.at[g, me], q_out.at[me, g], own_sem.at[g])

    def scale_copy(k):
        to = at_offset(me, k)
        return remote(scu.at[to], sc_out.at[me], v_ss.at[k], v_rs.at[k], wide=to)

    def scales_for(p):
        return jnp.where(row4 < 2, t_one[own_s[p, 0]], t_two[own_s[p, 1]])

    for g in range(2):

        @pl.loop(0, W - 1)
        def _(i):
            down_copy(g, i).wait_recv()

        @pl.loop(0, N)
        def _(k):
            c_send[g, narrow_at(k)] = d_recv[g][own_s[W + N * g + narrow_at(k), 1]]

            @pl.when(k > 0)
            def _():
                c_copy(g, k).start()

        ctab[g, :, lanes_of(mn)] = c_send[g, mn]

        @pl.loop(1, N)
        def _(k):
            c_copy(g, k).wait()

        weigh(g)

        @pl.loop(1, N)
        def _(k):
            q_copy(g, k).start()
            t_copy(g, k).start()

        q_recv[g][mn] = q_send[g, mn]
        t_recv[g][mn] = t_send[g, mn]

        @pl.loop(1, N)
        def _(k):
            q_copy(g, k).wait()
            t_copy(g, k).wait()

        if g == 1:

            @pl.loop(1, W)
            def _(k):
                p = at_offset(me, k)
                scu[p] = scales_for(p)
                scale_copy(k).start()

            sc_out[me] = scales_for(me)

        @pl.loop(0, W - 1)
        def _(i):
            p = wide_at(i)
            u_send[g, p] = q_recv[g][own_s[p, g]]
            up_copy(g, i).start()

        u_send[g, me] = q_recv[g][own_s[me, g]]
        own_sums(g).start()

    @pl.loop(1, W)
    def _(k):
        scale_copy(k).wait()

    half_sub = lax.broadcasted_iota(jnp.int32, (CH // 2, CH), 0)
    counts_v[...] = jnp.zeros_like(counts_v)

    @pl.loop(0, W)
    def _(w):
        tile = sc_out[w]
        lows, lefts = [], []
        for g in range(2):
            kid = kids_out[pl.ds(g * W + w, 1), :]
            row = jnp.where(tab_s[w, 4 + g] > 0, tile[2 * g + 1 : 2 * g + 2, :], 0.0)
            lows.append(((kid & 127) == square_sub).astype(jnp.bfloat16))
            left = jnp.where((kid >> 7) == half_sub, row, 0.0)
            pieces = []
            for _ in range(3):
                pieces.append(left.astype(jnp.bfloat16))
                left = left - pieces[-1].astype(jnp.float32)
            pieces.append(jnp.zeros((CH // 2, CH), jnp.bfloat16))
            lefts.append(jnp.concatenate(pieces, axis=0))
        counts_v[...] += lax.dot_general(
            jnp.concatenate(lows, axis=1), jnp.concatenate(lefts, axis=1), NT,
            preferred_element_type=jnp.float32,
        )

    counts = counts_v[...]
    counts = counts[:, :CH] + pltpu.roll(counts[:, :CH], CH // 2, 1) + counts[:, CH:]
    factor_out[...] = 1.0 / (counts + 1.0)

    @pl.loop(1, W)
    def _(k):
        ids_copy(k).wait_send()

    @pl.loop(0, W - 1)
    def _(i):
        down_copy(1, i).wait_send()

    for g in range(2):
        own_sums(g).wait()

        @pl.loop(0, W - 1)
        def _(i):
            up_copy(g, i).wait()


def exchange(ids, children, centroids, embeddings):
    vm = pl.BlockSpec(memory_space=pltpu.VMEM)
    hbm = pl.BlockSpec(memory_space=pl.ANY)
    dma = pltpu.SemaphoreType.DMA
    bf, f32, i32, i16 = jnp.bfloat16, jnp.float32, jnp.int32, jnp.int16
    return pl.pallas_call(
        exchange_kernel,
        out_shape=(
            jax.ShapeDtypeStruct((W, 2, CH, F), i16),
            jax.ShapeDtypeStruct((W, 4, CH), f32),
            jax.ShapeDtypeStruct((2 * W, CH), i32),
            jax.ShapeDtypeStruct((W, 128), i32),
            jax.ShapeDtypeStruct((CH, CH), f32),
        ),
        in_specs=[vm, hbm, hbm, hbm],
        out_specs=(hbm, vm, vm, vm, vm),
        scratch_shapes=[
            pltpu.VMEM((1, 128), i32),
            pltpu.VMEM((W, 1, 128), i32),
            pltpu.VMEM((2 * W, 128), i32),
            pltpu.SMEM((2 * W, 128), i32),
            pltpu.SMEM((W, 128), i32),
            pltpu.SMEM((2 * W, CH), i32),
            pltpu.VMEM((BLK, RB, F), bf),
            pltpu.VMEM((CW, F), bf),
            pltpu.VMEM((GW, CH), i32),
            pltpu.VMEM((CH, 2 * CH), f32),
            pltpu.VMEM((CW, F), f32),
            pltpu.VMEM((2, CH, F), f32),
            pltpu.VMEM((N, 2, RB, F), bf),
            pltpu.VMEM((2, RB, D), bf),
            pltpu.VMEM((2, W, CH, F), bf),
            pltpu.VMEM((2, N, CH, F), bf),
            pltpu.VMEM((2, CH, D), bf),
            pltpu.VMEM((2, N, CH, F), i16),
            pltpu.VMEM((2, N, 4, CH), f32),
            pltpu.VMEM((2, W, CH, F), i16),
            pltpu.VMEM((W, 4, CH), f32),
            pltpu.VMEM((CH, D), f32),
            dma((6,)),
            dma((W,)), dma((W,)),
            dma((N,)), dma((N,)),
            dma((2 * W,)), dma((2 * W,)),
            dma((2 * N,)), dma((2 * N,)),
            dma((2 * N,)), dma((2 * N,)),
            dma((2 * N,)), dma((2 * N,)),
            dma((2 * W,)), dma((2 * W,)),
            dma((W,)), dma((W,)),
            dma((2,)),
            pltpu.VMEM((W, CH, F), bf),
            pltpu.VMEM((W, CH, F), bf),
            pltpu.VMEM((N, CH, F), i16),
            pltpu.VMEM((N, CH, F), i16),
            pltpu.VMEM((N, 4, CH), f32),
            pltpu.VMEM((N, 4, CH), f32),
        ],
        compiler_params=pltpu.CompilerParams(
            collective_id=0, has_side_effects=True, vmem_limit_bytes=60 * 1024 * 1024
        ),
        name="exchange",
    )(ids, children, centroids, embeddings)


PARTS = 8
BATCH = 16


def scatter_kernel(
    kids_s, tab_s, q_hbm, sc_ref, factor_ref, cent_hbm, out_hbm,
    q_ref, cent_b, slots, acc, cent_sem, q_sem, out_sem,
):
    lane = lax.broadcasted_iota(jnp.int32, (CH, CH), 1)
    eye = lane == lax.broadcasted_iota(jnp.int32, (CH, CH), 0)
    per, rows_per = W // PARTS, CW // PARTS

    def cent_copy(i):
        rows = pl.ds(pl.multiple_of(i * rows_per, rows_per), rows_per)
        return pltpu.make_async_copy(cent_hbm.at[rows], cent_b.at[rows], cent_sem.at[i])

    def q_copy(i):
        rows = pl.ds(i * per, per)
        return pltpu.make_async_copy(q_hbm.at[rows], q_ref.at[rows], q_sem.at[i])

    def out_copy(i):
        rows = pl.ds(pl.multiple_of(i * rows_per, rows_per), rows_per)
        return pltpu.make_async_copy(acc.at[rows], out_hbm.at[rows], out_sem.at[i])

    @pl.loop(0, PARTS)
    def _(i):
        cent_copy(i).start()

    @pl.loop(0, PARTS)
    def _(i):
        q_copy(i).start()

    @pl.loop(0, PARTS)
    def _(i):
        cent_copy(i).wait()
        for t in range(4):
            step = rows_per // 4
            rows = pl.ds(pl.multiple_of(i * rows_per + t * step, step), step)
            acc[rows, :] = cent_b[rows, :].astype(jnp.float32)

    def add_batch(slot, base):
        at = [pl.ds(kids_s[slot, base + i], 1) for i in range(BATCH)]
        sums = [acc[at[i], :] + slots[slot, pl.ds(base + i, 1), :] for i in range(BATCH)]
        for i in range(BATCH):
            acc[at[i], :] = sums[i]

    def decode(s):
        for j in range(2):
            scale = jnp.sum(
                jnp.where(eye, sc_ref[s][2 * j : 2 * j + 1, :], 0.0), axis=1, keepdims=True
            )
            slots[j * W + s] = q_ref[s, j].astype(jnp.int32).astype(jnp.float32) * scale

    def add_slot(s, j):
        slot, twice = j * W + s, tab_s[s, 6 + j]

        @pl.when(twice == 0)
        def _():
            for g in range(CH // BATCH):
                add_batch(slot, g * BATCH)

        @pl.when(twice > 0)
        def _():
            @pl.loop(0, CH // BATCH)
            def _(g):
                base = pl.multiple_of(g * BATCH, BATCH)

                @pl.when(((twice >> g) & 1) == 0)
                def _():
                    add_batch(slot, base)

                @pl.when(((twice >> g) & 1) > 0)
                def _():
                    for i in range(BATCH):
                        at = pl.ds(kids_s[slot, base + i], 1)
                        acc[at, :] = acc[at, :] + slots[slot, pl.ds(base + i, 1), :]

    @pl.loop(0, PARTS)
    def _(i):
        q_copy(i).wait()

        for t in range(per):
            decode(i * per + t)

    @pl.loop(0, W)
    def _(s):
        for j in range(2):

            @pl.when(tab_s[s, 4 + j] > 0)
            def _():
                add_slot(s, j)

    factors = factor_ref[...]

    for i in range(PARTS):
        for h in range(i * (rows_per // CH), (i + 1) * (rows_per // CH)):
            rows = pl.ds(h * CH, CH)
            acc[rows, :] = acc[rows, :] * factors[:, h : h + 1]
        out_copy(i).start()

    @pl.loop(0, PARTS)
    def _(i):
        out_copy(i).wait()


def scatter(kids, table, q, scales, factors, centroids):
    vm = pl.BlockSpec(memory_space=pltpu.VMEM)
    sm = pl.BlockSpec(memory_space=pltpu.SMEM)
    hbm = pl.BlockSpec(memory_space=pl.ANY)
    return pl.pallas_call(
        scatter_kernel,
        out_shape=jax.ShapeDtypeStruct((CW, F), jnp.float32),
        in_specs=[sm, sm, hbm, vm, vm, hbm],
        out_specs=hbm,
        scratch_shapes=[
            pltpu.VMEM((W, 2, CH, F), jnp.int16),
            pltpu.VMEM((CW, F), jnp.bfloat16),
            pltpu.VMEM((2 * W, CH, F), jnp.float32),
            pltpu.VMEM((CW, F), jnp.float32),
            pltpu.SemaphoreType.DMA((PARTS,)),
            pltpu.SemaphoreType.DMA((PARTS,)),
            pltpu.SemaphoreType.DMA((PARTS,)),
        ],
        compiler_params=pltpu.CompilerParams(vmem_limit_bytes=60 * 1024 * 1024),
        name="scatter",
    )(kids, table, q, scales, factors, centroids)


def body(embeddings, centroids, level2_cluster_index, child_lists):
    ids = level2_cluster_index.reshape(1, BLK)
    q, scales, kids, table, factors = exchange(
        ids, child_lists, centroids, embeddings.reshape(BLK, RB, F)
    )
    return scatter(kids, table, q, scales, factors, centroids)


def solution(mesh):
    placed = (P("wide", "narrow"), P("wide", "narrow"), P("wide"), P("wide", None))
    return jax.shard_map(
        body, mesh=mesh, in_specs=placed, out_specs=P("wide", "narrow"), check_vma=False
    )
```

```python
import functools
import math

import jax
import jax.numpy as jnp
from jax import lax
from jax.experimental import pallas as pl
from jax.experimental.pallas import tpu as pltpu
from jax.sharding import PartitionSpec as P

D = 1024
X, Z = 4, 8
W = X * Z
N = 8
RB = 256
CH = 128
F = 128
BLK = 16
GW = 512
CW = 8192
MESH = pl.DeviceIdType.MESH
NT = (((1,), (1,)), ((), ()))


def shifted(me, dx, dz):
    return lax.rem(me // Z + dx, X) * Z + lax.rem(lax.rem(me, Z) + dz, Z)


def at_offset(me, k):
    return shifted(me, k // Z, lax.rem(k, Z))


def split_groups(owner, lane):
    here = lane < BLK
    earlier = jnp.zeros(owner.shape, jnp.int32)
    later = jnp.zeros(owner.shape, jnp.int32)
    for d in range(1, BLK):
        earlier = jnp.where((owner == pltpu.roll(owner, d, 1)) & (lane >= d), 1, earlier)
        later = jnp.where(
            (owner == pltpu.roll(owner, 128 - d, 1)) & (lane + d < BLK), 1, later
        )

    def before(flags):
        total = flags
        for d in (1, 2, 4, 8):
            total = total + jnp.where(lane >= d, pltpu.roll(total, d, 1), 0)
        return total - flags

    head = jnp.where(here & (earlier == 0) & (later == 1), 1, 0)
    single = jnp.where(here & (earlier == 0) & (later == 0), 1, 0)
    room = BLK // 2 - jnp.sum(head, axis=1, keepdims=True)
    one = jnp.where((single == 1) & (before(single) < room), 1, head)
    two = jnp.where(here, 1 - one, 0)
    return (one == 1, two == 1), (before(one), before(two))


def exchange_kernel(
    given_ref, child_ref, cent_ref, emb_ref,
    q_out, f_out, col_out, kids_out, tab_out, factor_out,
    ids_ref, ids_all, own_v, own_s, tab_s, kids_s, emb_v, cent_b, child_v, counts_v, cent_f, stage,
    e_send, xfull, d_send, c_send, ctab, q_send, t_send, u_send, scu, swork,
    local_sem, ids_ss, ids_rs, e_ss, e_rs, d_ss, d_rs, c_ss, c_rs, q_ss, q_rs, t_ss, t_rs,
    u_ss, u_rs, v_ss, v_rs, own_sem, d_one, d_two, q_one, q_two, t_one, t_two,
    sc_all, u_one, decoded,
):
    me = lax.axis_index("wide")
    mn = lax.axis_index("narrow")
    d_recv, q_recv, t_recv = (d_one, d_two), (q_one, q_two), (t_one, t_two)

    def remote(src, dst, ss, rs, **where):
        return pltpu.make_async_remote_copy(
            src_ref=src, dst_ref=dst, send_sem=ss, recv_sem=rs,
            device_id=where, device_id_type=MESH,
        )

    def narrow_at(k):
        return lax.rem(mn + k, N)

    def lanes_of(n):
        return pl.ds(pl.multiple_of(n * F, F), F)

    def wide_at(i):
        m = lax.rem(i, Z)
        u, v = m // 2 + 1, lax.rem(m, 2)
        dz = (u * (1 - v) + (Z - u) * v) * (1 - m // (Z - 1))
        return shifted(me, lax.rem(i // Z + 1, X), dz)

    get_emb = pltpu.make_async_copy(emb_ref, emb_v, local_sem.at[0])
    get_cent = pltpu.make_async_copy(cent_ref, cent_b, local_sem.at[1])
    get_child = pltpu.make_async_copy(child_ref, child_v, local_sem.at[2])
    get_emb.start()
    get_cent.start()
    get_child.start()
    ids_ref[...] = jnp.full((1, 128), -1, jnp.int32)
    ids_ref[:, 0:BLK] = given_ref[...]
    barrier = pltpu.get_barrier_semaphore()

    @pl.loop(1, W)
    def _(k):
        pl.semaphore_signal(
            barrier, inc=1, device_id={"wide": at_offset(me, k)}, device_id_type=MESH
        )

    @pl.loop(1, N)
    def _(k):
        pl.semaphore_signal(
            barrier, inc=1, device_id={"narrow": narrow_at(k)}, device_id_type=MESH
        )

    pl.semaphore_wait(barrier, W - 1 + N - 1)

    def ids_copy(k):
        return remote(
            ids_ref, ids_all.at[me], ids_ss.at[k], ids_rs.at[k], wide=at_offset(me, k)
        )

    @pl.loop(1, W)
    def _(k):
        ids_copy(k).start()

    ids_all[me] = ids_ref[...]

    get_cent.wait()

    @pl.loop(0, CW // 256)
    def _(i):
        rows = pl.ds(pl.multiple_of(i * 256, 256), 256)
        cent_f[rows, :] = cent_b[rows, :].astype(jnp.float32)

    @pl.loop(1, W)
    def _(k):
        ids_copy(k).wait_recv()

    lane = lax.broadcasted_iota(jnp.int32, (W, 128), 1)
    sub = lax.broadcasted_iota(jnp.int32, (W, 128), 0)
    asked = ids_all[:, 0, :]
    owner = jnp.where(lane < BLK, asked >> 9, -1)
    groups, _ = split_groups(owner, lane)
    table = jnp.zeros((W, 128), jnp.int32)
    for g in range(2):
        mine = groups[g] & (owner == me)
        has = jnp.sum(jnp.where(mine, 1, 0), axis=1, keepdims=True)
        cluster = jnp.sum(jnp.where(mine, asked - me * GW, 0), axis=1, keepdims=True)
        table = jnp.where(lane == g, jnp.clip(cluster, 0, GW - 1), table)
        table = jnp.where(lane == 4 + g, has, table)
    tab_out[...] = table
    put_tab = pltpu.make_async_copy(tab_out, tab_s, local_sem.at[4])
    put_tab.start()
    put_tab.wait()
    get_child.wait()

    @pl.loop(0, W // 4)
    def _(i):
        spots = [(g, 4 * i + t) for g in range(2) for t in range(4)]
        rows = [child_v[pl.ds(tab_s[w, g], 1), :] for g, w in spots]
        for (g, w), row in zip(spots, rows):
            kids_out[pl.ds(g * W + w, 1), :] = jnp.clip(row - me * CW, 0, CW - 1)

    put_kids = pltpu.make_async_copy(kids_out, kids_s, local_sem.at[5])
    put_kids.start()
    put_kids.wait()

    def gather(g, p, dst):
        @pl.loop(0, CH // 16)
        def _(i):
            base = pl.multiple_of(i * 16, 16)
            rows = [
                cent_f[pl.ds(kids_s[g * W + p, base + r], 1), :] for r in range(16)
            ]
            for r in range(16):
                stage[g, pl.ds(base + r, 1), :] = rows[r]

        dst[...] = stage[g].astype(jnp.bfloat16)

    def down_copy(g, i):
        to = wide_at(i)
        return remote(
            d_send.at[g, to], d_recv[g].at[me], d_ss.at[g * W + i], d_rs.at[g * W + i], wide=to
        )

    @pl.loop(0, W - 1)
    def _(i):
        gather(0, wide_at(i), d_send.at[0, wide_at(i)])
        down_copy(0, i).start()

    gather(0, me, d_one.at[me])

    owner = jnp.where(lane < BLK, jnp.broadcast_to(ids_ref[...], (W, 128)) >> 9, -1)
    groups, places = split_groups(owner, lane)
    own = jnp.zeros((W, 128), jnp.int32)
    ranks = jnp.zeros((W, 128), jnp.int32)
    for g in range(2):
        mine = groups[g] & (owner == sub)
        place = jnp.sum(jnp.where(mine, places[g], 0), axis=1, keepdims=True)
        own = jnp.where(lane == g, jnp.clip(place, 0, N - 1), own)
        this = groups[g] & (places[g] + N * g == sub)
        block = jnp.sum(jnp.where(this, lane, 0), axis=1, keepdims=True)
        its = jnp.sum(jnp.where(this, owner, 0), axis=1, keepdims=True)
        ranks = jnp.where(lane == 0, ranks + block, ranks)
        ranks = jnp.where(lane == 1, ranks + its, ranks)
    own_v[0:W, :] = own
    own_v[W : 2 * W, :] = jnp.clip(ranks, 0, W - 1)
    put_own = pltpu.make_async_copy(own_v, own_s, local_sem.at[3])
    put_own.start()
    put_own.wait()
    get_emb.wait()

    @pl.loop(0, BLK)
    def _(r):
        e_send[lax.rem(r, N), r // N] = emb_v[lax.rem(own_s[W + r, 0], BLK)]

    def e_copy(k):
        to = narrow_at(k)
        return remote(
            e_send.at[to], xfull.at[:, :, lanes_of(mn)], e_ss.at[k], e_rs.at[k], narrow=to
        )

    @pl.loop(1, N)
    def _(k):
        e_copy(k).start()

    own_e = pltpu.make_async_copy(e_send.at[mn], xfull.at[:, :, lanes_of(mn)], local_sem.at[0])
    own_e.start()

    @pl.loop(0, W - 1)
    def _(i):
        gather(1, wide_at(i), d_send.at[1, wide_at(i)])
        down_copy(0, i).wait_send()
        down_copy(1, i).start()

    gather(1, me, d_two.at[me])

    kids = kids_out[...]
    lane64 = lax.broadcasted_iota(jnp.int32, (2 * W, CH), 1)
    twice = jnp.zeros((2 * W, CH), jnp.int32)
    for d in range(1, 16):
        same = (kids == pltpu.roll(kids, d, 1)) & (lax.rem(lane64, 16) >= d)
        twice = jnp.where(same, 1, twice)
    for d in (1, 2, 4, 8):
        twice = jnp.maximum(twice, pltpu.roll(twice, CH - d, 1))
    bit = jnp.where(lax.rem(lane64, 16) == 0, 1 << (lane64 >> 4), 0)
    bits = jnp.sum(twice * bit, axis=1, keepdims=True)
    table = jnp.where(lane == 6, bits[0:W], table)
    tab_out[...] = jnp.where(lane == 7, bits[W : 2 * W], table)

    own_e.wait()

    @pl.loop(1, N)
    def _(k):
        e_copy(k).wait()

    square_sub = lax.broadcasted_iota(jnp.int32, (CH, CH), 0)
    eye = square_sub == lax.broadcasted_iota(jnp.int32, (CH, CH), 1)

    def as_row(column):
        return jnp.sum(jnp.where(eye, column, 0.0), axis=0, keepdims=True)

    row4 = lax.broadcasted_iota(jnp.int32, (4, CH), 0)

    def weigh(g):
        x = xfull[g]
        squares = jnp.zeros((CH, F), jnp.float32)
        for n in range(N):
            part = ctab[g, :, n * F : (n + 1) * F].astype(jnp.float32)
            squares = squares + part * part
        lengths = jnp.sum(squares, axis=1, keepdims=True)
        dots = lax.dot_general(ctab[g], x, NT, preferred_element_type=jnp.float32)
        score = (2.0 * dots - lengths) * (1.0 / math.sqrt(D))
        e = jnp.exp(score - jnp.max(score, axis=0, keepdims=True))
        weights = (e / jnp.sum(e, axis=0, keepdims=True)).astype(jnp.bfloat16)
        counts = as_row(jnp.sum(weights.astype(jnp.float32), axis=1, keepdims=True))
        swork[...] = jnp.dot(weights, x, preferred_element_type=jnp.float32)
        for n in range(N):
            part = swork[:, n * F : (n + 1) * F]
            top = jnp.maximum(jnp.max(jnp.abs(part), axis=1, keepdims=True), 1e-30)
            coded = jnp.round(part * (32767.0 / top)).astype(jnp.int32)
            q_send[g, n] = coded.astype(jnp.int16)
            scales = as_row(top * (1.0 / 32767.0))
            t_send[g, n] = jnp.where(lax.rem(row4, 2) == 0, scales, counts)

    def c_copy(g, k):
        to = narrow_at(k)
        return remote(
            c_send.at[g, to], ctab.at[g, :, lanes_of(mn)],
            c_ss.at[g * N + k], c_rs.at[g * N + k], narrow=to,
        )

    def q_copy(g, k):
        to = narrow_at(k)
        return remote(
            q_send.at[g, to], q_recv[g].at[mn],
            q_ss.at[g * N + k], q_rs.at[g * N + k], narrow=to,
        )

    def t_copy(g, k):
        to = narrow_at(k)
        return remote(
            t_send.at[g, to], t_recv[g].at[mn],
            t_ss.at[g * N + k], t_rs.at[g * N + k], narrow=to,
        )

    def up_copy(g, i):
        to = wide_at(i)
        return remote(
            u_send.at[g, to], (u_one, q_out)[g].at[me],
            u_ss.at[g * W + i], u_rs.at[g * W + i], wide=to,
        )

    def own_sums(g):
        return pltpu.make_async_copy(u_send.at[g, me], (u_one, q_out)[g].at[me], own_sem.at[g])

    def scale_copy(k):
        to = at_offset(me, k)
        return remote(scu.at[to], sc_all.at[me], v_ss.at[k], v_rs.at[k], wide=to)

    def scales_for(p):
        return jnp.where(row4 < 2, t_one[own_s[p, 0]], t_two[own_s[p, 1]])

    for g in range(2):

        @pl.loop(0, W - 1)
        def _(i):
            down_copy(g, i).wait_recv()

        @pl.loop(0, N)
        def _(k):
            c_send[g, narrow_at(k)] = d_recv[g][own_s[W + N * g + narrow_at(k), 1]]

            @pl.when(k > 0)
            def _():
                c_copy(g, k).start()

        ctab[g, :, lanes_of(mn)] = c_send[g, mn]

        @pl.loop(1, N)
        def _(k):
            c_copy(g, k).wait()

        weigh(g)

        @pl.loop(1, N)
        def _(k):
            q_copy(g, k).start()
            t_copy(g, k).start()

        q_recv[g][mn] = q_send[g, mn]
        t_recv[g][mn] = t_send[g, mn]

        @pl.loop(1, N)
        def _(k):
            q_copy(g, k).wait()
            t_copy(g, k).wait()

        if g == 1:

            @pl.loop(1, W)
            def _(k):
                p = at_offset(me, k)
                scu[p] = scales_for(p)
                scale_copy(k).start()

            sc_all[me] = scales_for(me)

        @pl.loop(0, W - 1)
        def _(i):
            p = wide_at(i)
            u_send[g, p] = q_recv[g][own_s[p, g]]
            up_copy(g, i).start()

        u_send[g, me] = q_recv[g][own_s[me, g]]
        own_sums(g).start()

    @pl.loop(1, W)
    def _(k):
        scale_copy(k).wait()

    half_sub = lax.broadcasted_iota(jnp.int32, (CH // 2, CH), 0)
    counts_v[...] = jnp.zeros_like(counts_v)

    @pl.loop(0, W)
    def _(w):
        tile = sc_all[w]
        lows, lefts = [], []
        for g in range(2):
            kid = kids_out[pl.ds(g * W + w, 1), :]
            row = jnp.where(tab_s[w, 4 + g] > 0, tile[2 * g + 1 : 2 * g + 2, :], 0.0)
            lows.append(((kid & 127) == square_sub).astype(jnp.bfloat16))
            left = jnp.where((kid >> 7) == half_sub, row, 0.0)
            pieces = []
            for _ in range(3):
                pieces.append(left.astype(jnp.bfloat16))
                left = left - pieces[-1].astype(jnp.float32)
            pieces.append(jnp.zeros((CH // 2, CH), jnp.bfloat16))
            lefts.append(jnp.concatenate(pieces, axis=0))
        counts_v[...] += lax.dot_general(
            jnp.concatenate(lows, axis=1), jnp.concatenate(lefts, axis=1), NT,
            preferred_element_type=jnp.float32,
        )

    counts = counts_v[...]
    counts = counts[:, :CH] + pltpu.roll(counts[:, :CH], CH // 2, 1) + counts[:, CH:]
    factor_out[...] = 1.0 / (counts + 1.0)

    scales = jnp.concatenate(
        [sc_all[:, 0, :], sc_all[:, 2, :], jnp.zeros((CH - 2 * W, CH), jnp.float32)], axis=0
    ).T
    col_out[...] = scales
    own_sums(0).wait()

    @pl.loop(0, W - 1)
    def _(i):
        up_copy(0, i).wait()

    for w in range(W):
        decoded[w] = u_one[w].astype(jnp.int32).astype(jnp.float32) * scales[:, w : w + 1]
    put_decoded = pltpu.make_async_copy(decoded, f_out, local_sem.at[1])
    put_decoded.start()

    @pl.loop(1, W)
    def _(k):
        ids_copy(k).wait_send()

    @pl.loop(0, W - 1)
    def _(i):
        down_copy(1, i).wait_send()

    own_sums(1).wait()

    @pl.loop(0, W - 1)
    def _(i):
        up_copy(1, i).wait()

    put_decoded.wait()


def exchange(ids, children, centroids, embeddings):
    vm = pl.BlockSpec(memory_space=pltpu.VMEM)
    hbm = pl.BlockSpec(memory_space=pl.ANY)
    dma = pltpu.SemaphoreType.DMA
    bf, f32, i32, i16 = jnp.bfloat16, jnp.float32, jnp.int32, jnp.int16
    return pl.pallas_call(
        exchange_kernel,
        out_shape=(
            jax.ShapeDtypeStruct((W, CH, F), i16),
            jax.ShapeDtypeStruct((W, CH, F), f32),
            jax.ShapeDtypeStruct((CH, CH), f32),
            jax.ShapeDtypeStruct((2 * W, CH), i32),
            jax.ShapeDtypeStruct((W, 128), i32),
            jax.ShapeDtypeStruct((CH, CH), f32),
        ),
        in_specs=[vm, hbm, hbm, hbm],
        out_specs=(hbm, hbm, vm, vm, vm, vm),
        scratch_shapes=[
            pltpu.VMEM((1, 128), i32),
            pltpu.VMEM((W, 1, 128), i32),
            pltpu.VMEM((2 * W, 128), i32),
            pltpu.SMEM((2 * W, 128), i32),
            pltpu.SMEM((W, 128), i32),
            pltpu.SMEM((2 * W, CH), i32),
            pltpu.VMEM((BLK, RB, F), bf),
            pltpu.VMEM((CW, F), bf),
            pltpu.VMEM((GW, CH), i32),
            pltpu.VMEM((CH, 2 * CH), f32),
            pltpu.VMEM((CW, F), f32),
            pltpu.VMEM((2, CH, F), f32),
            pltpu.VMEM((N, 2, RB, F), bf),
            pltpu.VMEM((2, RB, D), bf),
            pltpu.VMEM((2, W, CH, F), bf),
            pltpu.VMEM((2, N, CH, F), bf),
            pltpu.VMEM((2, CH, D), bf),
            pltpu.VMEM((2, N, CH, F), i16),
            pltpu.VMEM((2, N, 4, CH), f32),
            pltpu.VMEM((2, W, CH, F), i16),
            pltpu.VMEM((W, 4, CH), f32),
            pltpu.VMEM((CH, D), f32),
            dma((6,)),
            dma((W,)), dma((W,)),
            dma((N,)), dma((N,)),
            dma((2 * W,)), dma((2 * W,)),
            dma((2 * N,)), dma((2 * N,)),
            dma((2 * N,)), dma((2 * N,)),
            dma((2 * N,)), dma((2 * N,)),
            dma((2 * W,)), dma((2 * W,)),
            dma((W,)), dma((W,)),
            dma((2,)),
            pltpu.VMEM((W, CH, F), bf),
            pltpu.VMEM((W, CH, F), bf),
            pltpu.VMEM((N, CH, F), i16),
            pltpu.VMEM((N, CH, F), i16),
            pltpu.VMEM((N, 4, CH), f32),
            pltpu.VMEM((N, 4, CH), f32),
            pltpu.VMEM((W, 4, CH), f32),
            pltpu.VMEM((W, CH, F), i16),
            pltpu.VMEM((W, CH, F), f32),
        ],
        compiler_params=pltpu.CompilerParams(
            collective_id=0, has_side_effects=True, vmem_limit_bytes=60 * 1024 * 1024
        ),
        name="exchange",
    )(ids, children, centroids, embeddings)


PARTS = 8
BATCH = 16


def scatter_kernel(
    kids_s, tab_s, q_hbm, f_hbm, col_ref, factor_ref, cent_hbm, out_hbm,
    q_ref, cent_b, slots, acc, cent_sem, q_sem, out_sem, f_sem,
):
    per, rows_per = W // PARTS, CW // PARTS

    def cent_copy(i):
        rows = pl.ds(pl.multiple_of(i * rows_per, rows_per), rows_per)
        return pltpu.make_async_copy(cent_hbm.at[rows], cent_b.at[rows], cent_sem.at[i])

    def q_copy(i):
        rows = pl.ds(i * per, per)
        return pltpu.make_async_copy(q_hbm.at[rows], q_ref.at[rows], q_sem.at[i])

    def out_copy(i):
        rows = pl.ds(pl.multiple_of(i * rows_per, rows_per), rows_per)
        return pltpu.make_async_copy(acc.at[rows], out_hbm.at[rows], out_sem.at[i])

    @pl.loop(0, PARTS)
    def _(i):
        cent_copy(i).start()

    @pl.loop(0, PARTS)
    def _(i):
        q_copy(i).start()

    get_f = pltpu.make_async_copy(f_hbm, slots.at[pl.ds(0, W)], f_sem.at[0])
    get_f.start()

    @pl.loop(0, PARTS)
    def _(i):
        cent_copy(i).wait()
        for t in range(4):
            step = rows_per // 4
            rows = pl.ds(pl.multiple_of(i * rows_per + t * step, step), step)
            acc[rows, :] = cent_b[rows, :].astype(jnp.float32)

    def add_batch(slot, base):
        at = [pl.ds(kids_s[slot, base + i], 1) for i in range(BATCH)]
        sums = [acc[at[i], :] + slots[slot, pl.ds(base + i, 1), :] for i in range(BATCH)]
        for i in range(BATCH):
            acc[at[i], :] = sums[i]

    def add_slot(s, j):
        slot, twice = j * W + s, tab_s[s, 6 + j]

        @pl.when(twice == 0)
        def _():
            for g in range(CH // BATCH):
                add_batch(slot, g * BATCH)

        @pl.when(twice > 0)
        def _():
            @pl.loop(0, CH // BATCH)
            def _(g):
                base = pl.multiple_of(g * BATCH, BATCH)

                @pl.when(((twice >> g) & 1) == 0)
                def _():
                    add_batch(slot, base)

                @pl.when(((twice >> g) & 1) > 0)
                def _():
                    for i in range(BATCH):
                        at = pl.ds(kids_s[slot, base + i], 1)
                        acc[at, :] = acc[at, :] + slots[slot, pl.ds(base + i, 1), :]

    columns = col_ref[...]
    for i in range(PARTS):
        q_copy(i).wait()
        for w in range(i * per, (i + 1) * per):
            scale = columns[:, W + w : W + w + 1]
            slots[W + w] = q_ref[w].astype(jnp.int32).astype(jnp.float32) * scale

    get_f.wait()

    @pl.loop(0, W)
    def _(s):
        for j in range(2):

            @pl.when(tab_s[s, 4 + j] > 0)
            def _():
                add_slot(s, j)

    factors = factor_ref[...]

    for i in range(PARTS):
        for h in range(i * (rows_per // CH), (i + 1) * (rows_per // CH)):
            rows = pl.ds(h * CH, CH)
            acc[rows, :] = acc[rows, :] * factors[:, h : h + 1]
        out_copy(i).start()

    @pl.loop(0, PARTS)
    def _(i):
        out_copy(i).wait()


def scatter(kids, table, q, decoded, columns, factors, centroids):
    vm = pl.BlockSpec(memory_space=pltpu.VMEM)
    sm = pl.BlockSpec(memory_space=pltpu.SMEM)
    hbm = pl.BlockSpec(memory_space=pl.ANY)
    return pl.pallas_call(
        scatter_kernel,
        out_shape=jax.ShapeDtypeStruct((CW, F), jnp.float32),
        in_specs=[sm, sm, hbm, hbm, vm, vm, hbm],
        out_specs=hbm,
        scratch_shapes=[
            pltpu.VMEM((W, CH, F), jnp.int16),
            pltpu.VMEM((CW, F), jnp.bfloat16),
            pltpu.VMEM((2 * W, CH, F), jnp.float32),
            pltpu.VMEM((CW, F), jnp.float32),
            pltpu.SemaphoreType.DMA((PARTS,)),
            pltpu.SemaphoreType.DMA((PARTS,)),
            pltpu.SemaphoreType.DMA((PARTS,)),
            pltpu.SemaphoreType.DMA((1,)),
        ],
        compiler_params=pltpu.CompilerParams(vmem_limit_bytes=60 * 1024 * 1024),
        name="scatter",
    )(kids, table, q, decoded, columns, factors, centroids)


def body(embeddings, centroids, level2_cluster_index, child_lists):
    ids = level2_cluster_index.reshape(1, BLK)
    q, decoded, columns, kids, table, factors = exchange(
        ids, child_lists, centroids, embeddings.reshape(BLK, RB, F)
    )
    return scatter(kids, table, q, decoded, columns, factors, centroids)


def solution(mesh):
    placed = (P("wide", "narrow"), P("wide", "narrow"), P("wide"), P("wide", None))
    return jax.shard_map(
        body, mesh=mesh, in_specs=placed, out_specs=P("wide", "narrow"), check_vma=False
    )
```

```python
import functools
import math

import jax
import jax.numpy as jnp
from jax import lax
from jax.experimental import pallas as pl
from jax.experimental.pallas import tpu as pltpu
from jax.sharding import PartitionSpec as P

D = 1024
X, Z = 4, 8
W = X * Z
N = 8
RB = 256
CH = 128
F = 128
BLK = 16
GW = 512
CW = 8192
MESH = pl.DeviceIdType.MESH
NT = (((1,), (1,)), ((), ()))


def shifted(me, dx, dz):
    return lax.rem(me // Z + dx, X) * Z + lax.rem(lax.rem(me, Z) + dz, Z)


def at_offset(me, k):
    return shifted(me, k // Z, lax.rem(k, Z))


def split_groups(owner, lane):
    here = lane < BLK
    earlier = jnp.zeros(owner.shape, jnp.int32)
    later = jnp.zeros(owner.shape, jnp.int32)
    for d in range(1, BLK):
        earlier = jnp.where((owner == pltpu.roll(owner, d, 1)) & (lane >= d), 1, earlier)
        later = jnp.where(
            (owner == pltpu.roll(owner, 128 - d, 1)) & (lane + d < BLK), 1, later
        )

    def before(flags):
        total = flags
        for d in (1, 2, 4, 8):
            total = total + jnp.where(lane >= d, pltpu.roll(total, d, 1), 0)
        return total - flags

    head = jnp.where(here & (earlier == 0) & (later == 1), 1, 0)
    single = jnp.where(here & (earlier == 0) & (later == 0), 1, 0)
    room = BLK // 2 - jnp.sum(head, axis=1, keepdims=True)
    one = jnp.where((single == 1) & (before(single) < room), 1, head)
    two = jnp.where(here, 1 - one, 0)
    return (one == 1, two == 1), (before(one), before(two))


def exchange_kernel(
    given_ref, child_ref, cent_ref, emb_ref,
    q_out, sc_out, kids_out, tab_out, factor_out,
    ids_ref, ids_all, own_v, own_s, tab_s, kids_s, emb_v, cent_b, child_v, counts_v, cent_f, stage,
    e_send, xfull, d_send, c_send, ctab, q_send, t_send, u_send, scu, swork,
    local_sem, ids_ss, ids_rs, e_ss, e_rs, d_ss, d_rs, c_ss, c_rs, q_ss, q_rs, t_ss, t_rs,
    u_ss, u_rs, v_ss, v_rs, own_sem, d_one, d_two, q_one, q_two, t_one, t_two,
):
    me = lax.axis_index("wide")
    mn = lax.axis_index("narrow")
    d_recv, q_recv, t_recv = (d_one, d_two), (q_one, q_two), (t_one, t_two)

    def remote(src, dst, ss, rs, **where):
        return pltpu.make_async_remote_copy(
            src_ref=src, dst_ref=dst, send_sem=ss, recv_sem=rs,
            device_id=where, device_id_type=MESH,
        )

    def narrow_at(k):
        return lax.rem(mn + k, N)

    def lanes_of(n):
        return pl.ds(pl.multiple_of(n * F, F), F)

    def wide_at(i):
        m = lax.rem(i, Z)
        u, v = m // 2 + 1, lax.rem(m, 2)
        dz = (u * (1 - v) + (Z - u) * v) * (1 - m // (Z - 1))
        return shifted(me, lax.rem(i // Z + 1, X), dz)

    get_emb = pltpu.make_async_copy(emb_ref, emb_v, local_sem.at[0])
    get_cent = pltpu.make_async_copy(cent_ref, cent_b, local_sem.at[1])
    get_child = pltpu.make_async_copy(child_ref, child_v, local_sem.at[2])
    get_emb.start()
    get_cent.start()
    get_child.start()
    ids_ref[...] = jnp.full((1, 128), -1, jnp.int32)
    ids_ref[:, 0:BLK] = given_ref[...]
    barrier = pltpu.get_barrier_semaphore()

    @pl.loop(1, W)
    def _(k):
        pl.semaphore_signal(
            barrier, inc=1, device_id={"wide": at_offset(me, k)}, device_id_type=MESH
        )

    @pl.loop(1, N)
    def _(k):
        pl.semaphore_signal(
            barrier, inc=1, device_id={"narrow": narrow_at(k)}, device_id_type=MESH
        )

    pl.semaphore_wait(barrier, W - 1 + N - 1)

    def ids_copy(k):
        return remote(
            ids_ref, ids_all.at[me], ids_ss.at[k], ids_rs.at[k], wide=at_offset(me, k)
        )

    @pl.loop(1, W)
    def _(k):
        ids_copy(k).start()

    ids_all[me] = ids_ref[...]

    get_cent.wait()

    @pl.loop(0, CW // 256)
    def _(i):
        rows = pl.ds(pl.multiple_of(i * 256, 256), 256)
        cent_f[rows, :] = cent_b[rows, :].astype(jnp.float32)

    @pl.loop(1, W)
    def _(k):
        ids_copy(k).wait_recv()

    lane = lax.broadcasted_iota(jnp.int32, (W, 128), 1)
    sub = lax.broadcasted_iota(jnp.int32, (W, 128), 0)
    asked = ids_all[:, 0, :]
    owner = jnp.where(lane < BLK, asked >> 9, -1)
    groups, _ = split_groups(owner, lane)
    table = jnp.zeros((W, 128), jnp.int32)
    for g in range(2):
        mine = groups[g] & (owner == me)
        has = jnp.sum(jnp.where(mine, 1, 0), axis=1, keepdims=True)
        cluster = jnp.sum(jnp.where(mine, asked - me * GW, 0), axis=1, keepdims=True)
        table = jnp.where(lane == g, jnp.clip(cluster, 0, GW - 1), table)
        table = jnp.where(lane == 4 + g, has, table)
    tab_out[...] = table
    put_tab = pltpu.make_async_copy(tab_out, tab_s, local_sem.at[4])
    put_tab.start()
    put_tab.wait()
    get_child.wait()

    @pl.loop(0, W // 4)
    def _(i):
        spots = [(g, 4 * i + t) for g in range(2) for t in range(4)]
        rows = [child_v[pl.ds(tab_s[w, g], 1), :] for g, w in spots]
        for (g, w), row in zip(spots, rows):
            kids_out[pl.ds(g * W + w, 1), :] = jnp.clip(row - me * CW, 0, CW - 1)

    put_kids = pltpu.make_async_copy(kids_out, kids_s, local_sem.at[5])
    put_kids.start()
    put_kids.wait()

    def gather(g, p, dst):
        @pl.loop(0, CH // 16)
        def _(i):
            base = pl.multiple_of(i * 16, 16)
            rows = [
                cent_f[pl.ds(kids_s[g * W + p, base + r], 1), :] for r in range(16)
            ]
            for r in range(16):
                stage[g, pl.ds(base + r, 1), :] = rows[r]

        dst[...] = stage[g].astype(jnp.bfloat16)

    def down_copy(g, i):
        to = wide_at(i)
        return remote(
            d_send.at[g, to], d_recv[g].at[me], d_ss.at[g * W + i], d_rs.at[g * W + i], wide=to
        )

    @pl.loop(0, W - 1)
    def _(i):
        gather(0, wide_at(i), d_send.at[0, wide_at(i)])
        down_copy(0, i).start()

    gather(0, me, d_one.at[me])

    owner = jnp.where(lane < BLK, jnp.broadcast_to(ids_ref[...], (W, 128)) >> 9, -1)
    groups, places = split_groups(owner, lane)
    own = jnp.zeros((W, 128), jnp.int32)
    ranks = jnp.zeros((W, 128), jnp.int32)
    for g in range(2):
        mine = groups[g] & (owner == sub)
        place = jnp.sum(jnp.where(mine, places[g], 0), axis=1, keepdims=True)
        own = jnp.where(lane == g, jnp.clip(place, 0, N - 1), own)
        this = groups[g] & (places[g] + N * g == sub)
        block = jnp.sum(jnp.where(this, lane, 0), axis=1, keepdims=True)
        its = jnp.sum(jnp.where(this, owner, 0), axis=1, keepdims=True)
        ranks = jnp.where(lane == 0, ranks + block, ranks)
        ranks = jnp.where(lane == 1, ranks + its, ranks)
    own_v[0:W, :] = own
    own_v[W : 2 * W, :] = jnp.clip(ranks, 0, W - 1)
    put_own = pltpu.make_async_copy(own_v, own_s, local_sem.at[3])
    put_own.start()
    put_own.wait()
    get_emb.wait()

    @pl.loop(0, BLK)
    def _(r):
        e_send[lax.rem(r, N), r // N] = emb_v[lax.rem(own_s[W + r, 0], BLK)]

    def e_copy(k):
        to = narrow_at(k)
        return remote(
            e_send.at[to], xfull.at[:, :, lanes_of(mn)], e_ss.at[k], e_rs.at[k], narrow=to
        )

    @pl.loop(1, N)
    def _(k):
        e_copy(k).start()

    own_e = pltpu.make_async_copy(e_send.at[mn], xfull.at[:, :, lanes_of(mn)], local_sem.at[0])
    own_e.start()

    @pl.loop(0, W - 1)
    def _(i):
        gather(1, wide_at(i), d_send.at[1, wide_at(i)])

    gather(1, me, d_two.at[me])

    thirds = ((0, W // 3), (W // 3, 2 * W // 3), (2 * W // 3, W - 1))

    def start_down(g, third):
        @pl.loop(*thirds[third])
        def _(i):
            down_copy(g, i).start()

    @pl.loop(0, thirds[1][1])
    def _(i):
        down_copy(0, i).wait_send()

    start_down(1, 0)

    @pl.loop(thirds[1][1], W - 1)
    def _(i):
        down_copy(0, i).wait_send()

    kids = kids_out[...]
    lane64 = lax.broadcasted_iota(jnp.int32, (2 * W, CH), 1)
    twice = jnp.zeros((2 * W, CH), jnp.int32)
    for d in range(1, 16):
        same = (kids == pltpu.roll(kids, d, 1)) & (lax.rem(lane64, 16) >= d)
        twice = jnp.where(same, 1, twice)
    for d in (1, 2, 4, 8):
        twice = jnp.maximum(twice, pltpu.roll(twice, CH - d, 1))
    bit = jnp.where(lax.rem(lane64, 16) == 0, 1 << (lane64 >> 4), 0)
    bits = jnp.sum(twice * bit, axis=1, keepdims=True)
    table = jnp.where(lane == 6, bits[0:W], table)
    tab_out[...] = jnp.where(lane == 7, bits[W : 2 * W], table)

    own_e.wait()

    @pl.loop(1, N)
    def _(k):
        e_copy(k).wait()

    square_sub = lax.broadcasted_iota(jnp.int32, (CH, CH), 0)
    eye = square_sub == lax.broadcasted_iota(jnp.int32, (CH, CH), 1)

    def as_row(column):
        return jnp.sum(jnp.where(eye, column, 0.0), axis=0, keepdims=True)

    row4 = lax.broadcasted_iota(jnp.int32, (4, CH), 0)

    def weigh(g):
        x = xfull[g]
        squares = jnp.zeros((CH, F), jnp.float32)
        for n in range(N):
            part = ctab[g, :, n * F : (n + 1) * F].astype(jnp.float32)
            squares = squares + part * part
        lengths = jnp.sum(squares, axis=1, keepdims=True)
        dots = lax.dot_general(ctab[g], x, NT, preferred_element_type=jnp.float32)
        score = (2.0 * dots - lengths) * (1.0 / math.sqrt(D))
        e = jnp.exp(score - jnp.max(score, axis=0, keepdims=True))
        weights = (e / jnp.sum(e, axis=0, keepdims=True)).astype(jnp.bfloat16)
        counts = as_row(jnp.sum(weights.astype(jnp.float32), axis=1, keepdims=True))
        swork[...] = jnp.dot(weights, x, preferred_element_type=jnp.float32)
        for n in range(N):
            part = swork[:, n * F : (n + 1) * F]
            top = jnp.maximum(jnp.max(jnp.abs(part), axis=1, keepdims=True), 1e-30)
            coded = jnp.round(part * (32767.0 / top)).astype(jnp.int32)
            q_send[g, n] = coded.astype(jnp.int16)
            scales = as_row(top * (1.0 / 32767.0))
            t_send[g, n] = jnp.where(lax.rem(row4, 2) == 0, scales, counts)

    def c_copy(g, k):
        to = narrow_at(k)
        return remote(
            c_send.at[g, to], ctab.at[g, :, lanes_of(mn)],
            c_ss.at[g * N + k], c_rs.at[g * N + k], narrow=to,
        )

    def q_copy(g, k):
        to = narrow_at(k)
        return remote(
            q_send.at[g, to], q_recv[g].at[mn],
            q_ss.at[g * N + k], q_rs.at[g * N + k], narrow=to,
        )

    def t_copy(g, k):
        to = narrow_at(k)
        return remote(
            t_send.at[g, to], t_recv[g].at[mn],
            t_ss.at[g * N + k], t_rs.at[g * N + k], narrow=to,
        )

    def up_copy(g, i):
        to = wide_at(i)
        return remote(
            u_send.at[g, to], q_out.at[me, g], u_ss.at[g * W + i], u_rs.at[g * W + i], wide=to
        )

    def own_sums(g):
        return pltpu.make_async_copy(u_send.at[g, me], q_out.at[me, g], own_sem.at[g])

    def scale_copy(k):
        to = at_offset(me, k)
        return remote(scu.at[to], sc_out.at[me], v_ss.at[k], v_rs.at[k], wide=to)

    def scales_for(p):
        return jnp.where(row4 < 2, t_one[own_s[p, 0]], t_two[own_s[p, 1]])

    def start_up(g, third):
        @pl.loop(*thirds[third])
        def _(i):
            p = wide_at(i)
            u_send[g, p] = q_recv[g][own_s[p, g]]
            up_copy(g, i).start()

    def start_other(g, third):
        if g == 0:
            start_down(1, third)
        else:
            start_up(0, third)

    for g in range(2):

        @pl.loop(0, W - 1)
        def _(i):
            down_copy(g, i).wait_recv()

        @pl.loop(0, N)
        def _(k):
            c_send[g, narrow_at(k)] = d_recv[g][own_s[W + N * g + narrow_at(k), 1]]

            @pl.when(k > 0)
            def _():
                c_copy(g, k).start()

        ctab[g, :, lanes_of(mn)] = c_send[g, mn]
        start_other(g, 1)

        @pl.loop(1, N)
        def _(k):
            c_copy(g, k).wait()

        weigh(g)

        @pl.loop(1, N)
        def _(k):
            q_copy(g, k).start()
            t_copy(g, k).start()

        start_other(g, 2)
        q_recv[g][mn] = q_send[g, mn]
        t_recv[g][mn] = t_send[g, mn]

        @pl.loop(1, N)
        def _(k):
            q_copy(g, k).wait()
            t_copy(g, k).wait()

        start_up(g, 0)
        u_send[g, me] = q_recv[g][own_s[me, g]]
        own_sums(g).start()

    @pl.loop(1, W)
    def _(k):
        p = at_offset(me, k)
        scu[p] = scales_for(p)
        scale_copy(k).start()

    sc_out[me] = scales_for(me)
    start_up(1, 1)
    start_up(1, 2)

    @pl.loop(1, W)
    def _(k):
        scale_copy(k).wait()

    half_sub = lax.broadcasted_iota(jnp.int32, (CH // 2, CH), 0)
    counts_v[...] = jnp.zeros_like(counts_v)

    @pl.loop(0, W)
    def _(w):
        tile = sc_out[w]
        lows, lefts = [], []
        for g in range(2):
            kid = kids_out[pl.ds(g * W + w, 1), :]
            row = jnp.where(tab_s[w, 4 + g] > 0, tile[2 * g + 1 : 2 * g + 2, :], 0.0)
            lows.append(((kid & 127) == square_sub).astype(jnp.bfloat16))
            left = jnp.where((kid >> 7) == half_sub, row, 0.0)
            pieces = []
            for _ in range(3):
                pieces.append(left.astype(jnp.bfloat16))
                left = left - pieces[-1].astype(jnp.float32)
            pieces.append(jnp.zeros((CH // 2, CH), jnp.bfloat16))
            lefts.append(jnp.concatenate(pieces, axis=0))
        counts_v[...] += lax.dot_general(
            jnp.concatenate(lows, axis=1), jnp.concatenate(lefts, axis=1), NT,
            preferred_element_type=jnp.float32,
        )

    counts = counts_v[...]
    counts = counts[:, :CH] + pltpu.roll(counts[:, :CH], CH // 2, 1) + counts[:, CH:]
    factor_out[...] = 1.0 / (counts + 1.0)

    @pl.loop(1, W)
    def _(k):
        ids_copy(k).wait_send()

    @pl.loop(0, W - 1)
    def _(i):
        down_copy(1, i).wait_send()

    for g in range(2):
        own_sums(g).wait()

        @pl.loop(0, W - 1)
        def _(i):
            up_copy(g, i).wait()


def exchange(ids, children, centroids, embeddings):
    vm = pl.BlockSpec(memory_space=pltpu.VMEM)
    hbm = pl.BlockSpec(memory_space=pl.ANY)
    dma = pltpu.SemaphoreType.DMA
    bf, f32, i32, i16 = jnp.bfloat16, jnp.float32, jnp.int32, jnp.int16
    return pl.pallas_call(
        exchange_kernel,
        out_shape=(
            jax.ShapeDtypeStruct((W, 2, CH, F), i16),
            jax.ShapeDtypeStruct((W, 4, CH), f32),
            jax.ShapeDtypeStruct((2 * W, CH), i32),
            jax.ShapeDtypeStruct((W, 128), i32),
            jax.ShapeDtypeStruct((CH, CH), f32),
        ),
        in_specs=[vm, hbm, hbm, hbm],
        out_specs=(hbm, vm, vm, vm, vm),
        scratch_shapes=[
            pltpu.VMEM((1, 128), i32),
            pltpu.VMEM((W, 1, 128), i32),
            pltpu.VMEM((2 * W, 128), i32),
            pltpu.SMEM((2 * W, 128), i32),
            pltpu.SMEM((W, 128), i32),
            pltpu.SMEM((2 * W, CH), i32),
            pltpu.VMEM((BLK, RB, F), bf),
            pltpu.VMEM((CW, F), bf),
            pltpu.VMEM((GW, CH), i32),
            pltpu.VMEM((CH, 2 * CH), f32),
            pltpu.VMEM((CW, F), f32),
            pltpu.VMEM((2, CH, F), f32),
            pltpu.VMEM((N, 2, RB, F), bf),
            pltpu.VMEM((2, RB, D), bf),
            pltpu.VMEM((2, W, CH, F), bf),
            pltpu.VMEM((2, N, CH, F), bf),
            pltpu.VMEM((2, CH, D), bf),
            pltpu.VMEM((2, N, CH, F), i16),
            pltpu.VMEM((2, N, 4, CH), f32),
            pltpu.VMEM((2, W, CH, F), i16),
            pltpu.VMEM((W, 4, CH), f32),
            pltpu.VMEM((CH, D), f32),
            dma((6,)),
            dma((W,)), dma((W,)),
            dma((N,)), dma((N,)),
            dma((2 * W,)), dma((2 * W,)),
            dma((2 * N,)), dma((2 * N,)),
            dma((2 * N,)), dma((2 * N,)),
            dma((2 * N,)), dma((2 * N,)),
            dma((2 * W,)), dma((2 * W,)),
            dma((W,)), dma((W,)),
            dma((2,)),
            pltpu.VMEM((W, CH, F), bf),
            pltpu.VMEM((W, CH, F), bf),
            pltpu.VMEM((N, CH, F), i16),
            pltpu.VMEM((N, CH, F), i16),
            pltpu.VMEM((N, 4, CH), f32),
            pltpu.VMEM((N, 4, CH), f32),
        ],
        compiler_params=pltpu.CompilerParams(
            collective_id=0, has_side_effects=True, vmem_limit_bytes=60 * 1024 * 1024
        ),
        name="exchange",
    )(ids, children, centroids, embeddings)


PARTS = 8
BATCH = 16


def scatter_kernel(
    kids_s, tab_s, q_hbm, sc_ref, factor_ref, cent_hbm, out_hbm,
    q_ref, cent_b, slots, acc, cent_sem, q_sem, out_sem,
):
    lane = lax.broadcasted_iota(jnp.int32, (CH, CH), 1)
    eye = lane == lax.broadcasted_iota(jnp.int32, (CH, CH), 0)
    per, rows_per = W // PARTS, CW // PARTS

    def cent_copy(i):
        rows = pl.ds(pl.multiple_of(i * rows_per, rows_per), rows_per)
        return pltpu.make_async_copy(cent_hbm.at[rows], cent_b.at[rows], cent_sem.at[i])

    def q_copy(i):
        rows = pl.ds(i * per, per)
        return pltpu.make_async_copy(q_hbm.at[rows], q_ref.at[rows], q_sem.at[i])

    def out_copy(i):
        rows = pl.ds(pl.multiple_of(i * rows_per, rows_per), rows_per)
        return pltpu.make_async_copy(acc.at[rows], out_hbm.at[rows], out_sem.at[i])

    @pl.loop(0, PARTS)
    def _(i):
        cent_copy(i).start()

    @pl.loop(0, PARTS)
    def _(i):
        q_copy(i).start()

    @pl.loop(0, PARTS)
    def _(i):
        cent_copy(i).wait()
        for t in range(4):
            step = rows_per // 4
            rows = pl.ds(pl.multiple_of(i * rows_per + t * step, step), step)
            acc[rows, :] = cent_b[rows, :].astype(jnp.float32)

    def add_batch(slot, base):
        at = [pl.ds(kids_s[slot, base + i], 1) for i in range(BATCH)]
        sums = [acc[at[i], :] + slots[slot, pl.ds(base + i, 1), :] for i in range(BATCH)]
        for i in range(BATCH):
            acc[at[i], :] = sums[i]

    def decode(s):
        for j in range(2):
            scale = jnp.sum(
                jnp.where(eye, sc_ref[s][2 * j : 2 * j + 1, :], 0.0), axis=1, keepdims=True
            )
            slots[j * W + s] = q_ref[s, j].astype(jnp.int32).astype(jnp.float32) * scale

    def add_slot(s, j):
        slot, twice = j * W + s, tab_s[s, 6 + j]

        @pl.when(twice == 0)
        def _():
            for g in range(CH // BATCH):
                add_batch(slot, g * BATCH)

        @pl.when(twice > 0)
        def _():
            @pl.loop(0, CH // BATCH)
            def _(g):
                base = pl.multiple_of(g * BATCH, BATCH)

                @pl.when(((twice >> g) & 1) == 0)
                def _():
                    add_batch(slot, base)

                @pl.when(((twice >> g) & 1) > 0)
                def _():
                    for i in range(BATCH):
                        at = pl.ds(kids_s[slot, base + i], 1)
                        acc[at, :] = acc[at, :] + slots[slot, pl.ds(base + i, 1), :]

    @pl.loop(0, PARTS)
    def _(i):
        q_copy(i).wait()

        for t in range(per):
            decode(i * per + t)

    @pl.loop(0, W)
    def _(s):
        for j in range(2):

            @pl.when(tab_s[s, 4 + j] > 0)
            def _():
                add_slot(s, j)

    factors = factor_ref[...]

    for i in range(PARTS):
        for h in range(i * (rows_per // CH), (i + 1) * (rows_per // CH)):
            rows = pl.ds(h * CH, CH)
            acc[rows, :] = acc[rows, :] * factors[:, h : h + 1]
        out_copy(i).start()

    @pl.loop(0, PARTS)
    def _(i):
        out_copy(i).wait()


def scatter(kids, table, q, scales, factors, centroids):
    vm = pl.BlockSpec(memory_space=pltpu.VMEM)
    sm = pl.BlockSpec(memory_space=pltpu.SMEM)
    hbm = pl.BlockSpec(memory_space=pl.ANY)
    return pl.pallas_call(
        scatter_kernel,
        out_shape=jax.ShapeDtypeStruct((CW, F), jnp.float32),
        in_specs=[sm, sm, hbm, vm, vm, hbm],
        out_specs=hbm,
        scratch_shapes=[
            pltpu.VMEM((W, 2, CH, F), jnp.int16),
            pltpu.VMEM((CW, F), jnp.bfloat16),
            pltpu.VMEM((2 * W, CH, F), jnp.float32),
            pltpu.VMEM((CW, F), jnp.float32),
            pltpu.SemaphoreType.DMA((PARTS,)),
            pltpu.SemaphoreType.DMA((PARTS,)),
            pltpu.SemaphoreType.DMA((PARTS,)),
        ],
        compiler_params=pltpu.CompilerParams(vmem_limit_bytes=60 * 1024 * 1024),
        name="scatter",
    )(kids, table, q, scales, factors, centroids)


def body(embeddings, centroids, level2_cluster_index, child_lists):
    ids = level2_cluster_index.reshape(1, BLK)
    q, scales, kids, table, factors = exchange(
        ids, child_lists, centroids, embeddings.reshape(BLK, RB, F)
    )
    return scatter(kids, table, q, scales, factors, centroids)


def solution(mesh):
    placed = (P("wide", "narrow"), P("wide", "narrow"), P("wide"), P("wide", None))
    return jax.shard_map(
        body, mesh=mesh, in_specs=placed, out_specs=P("wide", "narrow"), check_vma=False
    )
```

```python
import functools
import math

import jax
import jax.numpy as jnp
from jax import lax
from jax.experimental import pallas as pl
from jax.experimental.pallas import tpu as pltpu
from jax.sharding import PartitionSpec as P

D = 1024
X, Z = 4, 8
W = X * Z
N = 8
RB = 256
CH = 128
F = 128
BLK = 16
GW = 512
CW = 8192
MESH = pl.DeviceIdType.MESH
NT = (((1,), (1,)), ((), ()))


def shifted(me, dx, dz):
    return lax.rem(me // Z + dx, X) * Z + lax.rem(lax.rem(me, Z) + dz, Z)


def at_offset(me, k):
    return shifted(me, k // Z, lax.rem(k, Z))


def split_groups(owner, lane):
    here = lane < BLK
    earlier = jnp.zeros(owner.shape, jnp.int32)
    later = jnp.zeros(owner.shape, jnp.int32)
    for d in range(1, BLK):
        earlier = jnp.where((owner == pltpu.roll(owner, d, 1)) & (lane >= d), 1, earlier)
        later = jnp.where(
            (owner == pltpu.roll(owner, 128 - d, 1)) & (lane + d < BLK), 1, later
        )

    def before(flags):
        total = flags
        for d in (1, 2, 4, 8):
            total = total + jnp.where(lane >= d, pltpu.roll(total, d, 1), 0)
        return total - flags

    head = jnp.where(here & (earlier == 0) & (later == 1), 1, 0)
    single = jnp.where(here & (earlier == 0) & (later == 0), 1, 0)
    room = BLK // 2 - jnp.sum(head, axis=1, keepdims=True)
    one = jnp.where((single == 1) & (before(single) < room), 1, head)
    two = jnp.where(here, 1 - one, 0)
    return (one == 1, two == 1), (before(one), before(two))


def exchange_kernel(
    given_ref, child_ref, cent_ref, emb_ref,
    q_out, sc_out, kids_out, tab_out, factor_out,
    ids_ref, ids_all, own_v, own_s, tab_s, kids_s, emb_v, cent_b, child_v, counts_v, cent_f, stage,
    e_send, xfull, d_send, c_send, ctab, q_send, t_send, u_send, scu, swork,
    local_sem, ids_ss, ids_rs, e_ss, e_rs, d_ss, d_rs, c_ss, c_rs, q_ss, q_rs, t_ss, t_rs,
    u_ss, u_rs, v_ss, v_rs, own_sem, d_one, d_two, q_one, q_two, t_one, t_two,
):
    me = lax.axis_index("wide")
    mn = lax.axis_index("narrow")
    d_recv, q_recv, t_recv = (d_one, d_two), (q_one, q_two), (t_one, t_two)

    def remote(src, dst, ss, rs, **where):
        return pltpu.make_async_remote_copy(
            src_ref=src, dst_ref=dst, send_sem=ss, recv_sem=rs,
            device_id=where, device_id_type=MESH,
        )

    def narrow_at(k):
        return lax.rem(mn + k, N)

    def lanes_of(n):
        return pl.ds(pl.multiple_of(n * F, F), F)

    def wide_at(i):
        t = lax.rem(i + W - X + 1, W)
        dx = lax.rem(t, X)
        m = lax.rem(t // X + 3 * dx, Z)
        u, v = m // 2 + 1, lax.rem(m, 2)
        dz = (u * (1 - v) + (Z - u) * v) * (1 - m // (Z - 1))
        return shifted(me, dx, dz)

    get_emb = pltpu.make_async_copy(emb_ref, emb_v, local_sem.at[0])
    get_cent = pltpu.make_async_copy(cent_ref, cent_b, local_sem.at[1])
    get_child = pltpu.make_async_copy(child_ref, child_v, local_sem.at[2])
    get_emb.start()
    get_cent.start()
    get_child.start()
    ids_ref[...] = jnp.full((1, 128), -1, jnp.int32)
    ids_ref[:, 0:BLK] = given_ref[...]
    barrier = pltpu.get_barrier_semaphore()

    @pl.loop(1, W)
    def _(k):
        pl.semaphore_signal(
            barrier, inc=1, device_id={"wide": at_offset(me, k)}, device_id_type=MESH
        )

    @pl.loop(1, N)
    def _(k):
        pl.semaphore_signal(
            barrier, inc=1, device_id={"narrow": narrow_at(k)}, device_id_type=MESH
        )

    pl.semaphore_wait(barrier, W - 1 + N - 1)

    def ids_copy(k):
        return remote(
            ids_ref, ids_all.at[me], ids_ss.at[k], ids_rs.at[k], wide=at_offset(me, k)
        )

    @pl.loop(1, W)
    def _(k):
        ids_copy(k).start()

    ids_all[me] = ids_ref[...]

    get_cent.wait()

    @pl.loop(0, CW // 256)
    def _(i):
        rows = pl.ds(pl.multiple_of(i * 256, 256), 256)
        cent_f[rows, :] = cent_b[rows, :].astype(jnp.float32)

    @pl.loop(1, W)
    def _(k):
        ids_copy(k).wait_recv()

    lane = lax.broadcasted_iota(jnp.int32, (W, 128), 1)
    sub = lax.broadcasted_iota(jnp.int32, (W, 128), 0)
    asked = ids_all[:, 0, :]
    owner = jnp.where(lane < BLK, asked >> 9, -1)
    groups, _ = split_groups(owner, lane)
    table = jnp.zeros((W, 128), jnp.int32)
    for g in range(2):
        mine = groups[g] & (owner == me)
        has = jnp.sum(jnp.where(mine, 1, 0), axis=1, keepdims=True)
        cluster = jnp.sum(jnp.where(mine, asked - me * GW, 0), axis=1, keepdims=True)
        table = jnp.where(lane == g, jnp.clip(cluster, 0, GW - 1), table)
        table = jnp.where(lane == 4 + g, has, table)
    tab_out[...] = table
    put_tab = pltpu.make_async_copy(tab_out, tab_s, local_sem.at[4])
    put_tab.start()
    put_tab.wait()
    get_child.wait()

    @pl.loop(0, W // 4)
    def _(i):
        spots = [(g, 4 * i + t) for g in range(2) for t in range(4)]
        rows = [child_v[pl.ds(tab_s[w, g], 1), :] for g, w in spots]
        for (g, w), row in zip(spots, rows):
            kids_out[pl.ds(g * W + w, 1), :] = jnp.clip(row - me * CW, 0, CW - 1)

    put_kids = pltpu.make_async_copy(kids_out, kids_s, local_sem.at[5])
    put_kids.start()
    put_kids.wait()

    def gather(g, p, dst):
        @pl.loop(0, CH // 16)
        def _(i):
            base = pl.multiple_of(i * 16, 16)
            rows = [
                cent_f[pl.ds(kids_s[g * W + p, base + r], 1), :] for r in range(16)
            ]
            for r in range(16):
                stage[g, pl.ds(base + r, 1), :] = rows[r]

        dst[...] = stage[g].astype(jnp.bfloat16)

    def down_copy(g, i):
        to = wide_at(i)
        return remote(
            d_send.at[g, to], d_recv[g].at[me], d_ss.at[g * W + i], d_rs.at[g * W + i], wide=to
        )

    @pl.loop(0, W - 1)
    def _(i):
        gather(0, wide_at(i), d_send.at[0, wide_at(i)])
        down_copy(0, i).start()

    gather(0, me, d_one.at[me])

    owner = jnp.where(lane < BLK, jnp.broadcast_to(ids_ref[...], (W, 128)) >> 9, -1)
    groups, places = split_groups(owner, lane)
    own = jnp.zeros((W, 128), jnp.int32)
    ranks = jnp.zeros((W, 128), jnp.int32)
    for g in range(2):
        mine = groups[g] & (owner == sub)
        place = jnp.sum(jnp.where(mine, places[g], 0), axis=1, keepdims=True)
        own = jnp.where(lane == g, jnp.clip(place, 0, N - 1), own)
        this = groups[g] & (places[g] + N * g == sub)
        block = jnp.sum(jnp.where(this, lane, 0), axis=1, keepdims=True)
        its = jnp.sum(jnp.where(this, owner, 0), axis=1, keepdims=True)
        ranks = jnp.where(lane == 0, ranks + block, ranks)
        ranks = jnp.where(lane == 1, ranks + its, ranks)
    own_v[0:W, :] = own
    own_v[W : 2 * W, :] = jnp.clip(ranks, 0, W - 1)
    put_own = pltpu.make_async_copy(own_v, own_s, local_sem.at[3])
    put_own.start()
    put_own.wait()
    get_emb.wait()

    @pl.loop(0, BLK)
    def _(r):
        e_send[lax.rem(r, N), r // N] = emb_v[lax.rem(own_s[W + r, 0], BLK)]

    def e_copy(k):
        to = narrow_at(k)
        return remote(
            e_send.at[to], xfull.at[:, :, lanes_of(mn)], e_ss.at[k], e_rs.at[k], narrow=to
        )

    @pl.loop(1, N)
    def _(k):
        e_copy(k).start()

    own_e = pltpu.make_async_copy(e_send.at[mn], xfull.at[:, :, lanes_of(mn)], local_sem.at[0])
    own_e.start()

    @pl.loop(0, W - 1)
    def _(i):
        gather(1, wide_at(i), d_send.at[1, wide_at(i)])
        down_copy(0, i).wait_send()
        down_copy(1, i).start()

    gather(1, me, d_two.at[me])

    kids = kids_out[...]
    lane64 = lax.broadcasted_iota(jnp.int32, (2 * W, CH), 1)
    twice = jnp.zeros((2 * W, CH), jnp.int32)
    for d in range(1, 16):
        same = (kids == pltpu.roll(kids, d, 1)) & (lax.rem(lane64, 16) >= d)
        twice = jnp.where(same, 1, twice)
    for d in (1, 2, 4, 8):
        twice = jnp.maximum(twice, pltpu.roll(twice, CH - d, 1))
    bit = jnp.where(lax.rem(lane64, 16) == 0, 1 << (lane64 >> 4), 0)
    bits = jnp.sum(twice * bit, axis=1, keepdims=True)
    table = jnp.where(lane == 6, bits[0:W], table)
    tab_out[...] = jnp.where(lane == 7, bits[W : 2 * W], table)

    own_e.wait()

    @pl.loop(1, N)
    def _(k):
        e_copy(k).wait()

    square_sub = lax.broadcasted_iota(jnp.int32, (CH, CH), 0)
    eye = square_sub == lax.broadcasted_iota(jnp.int32, (CH, CH), 1)

    def as_row(column):
        return jnp.sum(jnp.where(eye, column, 0.0), axis=0, keepdims=True)

    row4 = lax.broadcasted_iota(jnp.int32, (4, CH), 0)

    def weigh(g):
        x = xfull[g]
        squares = jnp.zeros((CH, F), jnp.float32)
        for n in range(N):
            part = ctab[g, :, n * F : (n + 1) * F].astype(jnp.float32)
            squares = squares + part * part
        lengths = jnp.sum(squares, axis=1, keepdims=True)
        dots = lax.dot_general(ctab[g], x, NT, preferred_element_type=jnp.float32)
        score = (2.0 * dots - lengths) * (1.0 / math.sqrt(D))
        e = jnp.exp(score - jnp.max(score, axis=0, keepdims=True))
        weights = (e / jnp.sum(e, axis=0, keepdims=True)).astype(jnp.bfloat16)
        counts = as_row(jnp.sum(weights.astype(jnp.float32), axis=1, keepdims=True))
        swork[...] = jnp.dot(weights, x, preferred_element_type=jnp.float32)
        for n in range(N):
            part = swork[:, n * F : (n + 1) * F]
            top = jnp.maximum(jnp.max(jnp.abs(part), axis=1, keepdims=True), 1e-30)
            coded = jnp.round(part * (32767.0 / top)).astype(jnp.int32)
            q_send[g, n] = coded.astype(jnp.int16)
            scales = as_row(top * (1.0 / 32767.0))
            t_send[g, n] = jnp.where(lax.rem(row4, 2) == 0, scales, counts)

    def c_copy(g, k):
        to = narrow_at(k)
        return remote(
            c_send.at[g, to], ctab.at[g, :, lanes_of(mn)],
            c_ss.at[g * N + k], c_rs.at[g * N + k], narrow=to,
        )

    def q_copy(g, k):
        to = narrow_at(k)
        return remote(
            q_send.at[g, to], q_recv[g].at[mn],
            q_ss.at[g * N + k], q_rs.at[g * N + k], narrow=to,
        )

    def t_copy(g, k):
        to = narrow_at(k)
        return remote(
            t_send.at[g, to], t_recv[g].at[mn],
            t_ss.at[g * N + k], t_rs.at[g * N + k], narrow=to,
        )

    def up_copy(g, i):
        to = wide_at(i)
        return remote(
            u_send.at[g, to], q_out.at[me, g], u_ss.at[g * W + i], u_rs.at[g * W + i], wide=to
        )

    def own_sums(g):
        return pltpu.make_async_copy(u_send.at[g, me], q_out.at[me, g], own_sem.at[g])

    def scale_copy(k):
        to = at_offset(me, k)
        return remote(scu.at[to], sc_out.at[me], v_ss.at[k], v_rs.at[k], wide=to)

    def scales_for(p):
        return jnp.where(row4 < 2, t_one[own_s[p, 0]], t_two[own_s[p, 1]])

    for g in range(2):

        @pl.loop(0, W - 1)
        def _(i):
            down_copy(g, i).wait_recv()

        @pl.loop(0, N)
        def _(k):
            c_send[g, narrow_at(k)] = d_recv[g][own_s[W + N * g + narrow_at(k), 1]]

            @pl.when(k > 0)
            def _():
                c_copy(g, k).start()

        ctab[g, :, lanes_of(mn)] = c_send[g, mn]

        @pl.loop(1, N)
        def _(k):
            c_copy(g, k).wait()

        weigh(g)

        @pl.loop(1, N)
        def _(k):
            q_copy(g, k).start()
            t_copy(g, k).start()

        q_recv[g][mn] = q_send[g, mn]
        t_recv[g][mn] = t_send[g, mn]

        @pl.loop(1, N)
        def _(k):
            q_copy(g, k).wait()
            t_copy(g, k).wait()

        if g == 1:

            @pl.loop(1, W)
            def _(k):
                p = at_offset(me, k)
                scu[p] = scales_for(p)
                scale_copy(k).start()

            sc_out[me] = scales_for(me)

        @pl.loop(0, W - 1)
        def _(i):
            p = wide_at(i)
            u_send[g, p] = q_recv[g][own_s[p, g]]
            up_copy(g, i).start()

        u_send[g, me] = q_recv[g][own_s[me, g]]
        own_sums(g).start()

    @pl.loop(1, W)
    def _(k):
        scale_copy(k).wait()

    half_sub = lax.broadcasted_iota(jnp.int32, (CH // 2, CH), 0)
    counts_v[...] = jnp.zeros_like(counts_v)

    @pl.loop(0, W)
    def _(w):
        tile = sc_out[w]
        lows, lefts = [], []
        for g in range(2):
            kid = kids_out[pl.ds(g * W + w, 1), :]
            row = jnp.where(tab_s[w, 4 + g] > 0, tile[2 * g + 1 : 2 * g + 2, :], 0.0)
            lows.append(((kid & 127) == square_sub).astype(jnp.bfloat16))
            left = jnp.where((kid >> 7) == half_sub, row, 0.0)
            pieces = []
            for _ in range(3):
                pieces.append(left.astype(jnp.bfloat16))
                left = left - pieces[-1].astype(jnp.float32)
            pieces.append(jnp.zeros((CH // 2, CH), jnp.bfloat16))
            lefts.append(jnp.concatenate(pieces, axis=0))
        counts_v[...] += lax.dot_general(
            jnp.concatenate(lows, axis=1), jnp.concatenate(lefts, axis=1), NT,
            preferred_element_type=jnp.float32,
        )

    counts = counts_v[...]
    counts = counts[:, :CH] + pltpu.roll(counts[:, :CH], CH // 2, 1) + counts[:, CH:]
    factor_out[...] = 1.0 / (counts + 1.0)

    @pl.loop(1, W)
    def _(k):
        ids_copy(k).wait_send()

    @pl.loop(0, W - 1)
    def _(i):
        down_copy(1, i).wait_send()

    for g in range(2):
        own_sums(g).wait()

        @pl.loop(0, W - 1)
        def _(i):
            up_copy(g, i).wait()


def exchange(ids, children, centroids, embeddings):
    vm = pl.BlockSpec(memory_space=pltpu.VMEM)
    hbm = pl.BlockSpec(memory_space=pl.ANY)
    dma = pltpu.SemaphoreType.DMA
    bf, f32, i32, i16 = jnp.bfloat16, jnp.float32, jnp.int32, jnp.int16
    return pl.pallas_call(
        exchange_kernel,
        out_shape=(
            jax.ShapeDtypeStruct((W, 2, CH, F), i16),
            jax.ShapeDtypeStruct((W, 4, CH), f32),
            jax.ShapeDtypeStruct((2 * W, CH), i32),
            jax.ShapeDtypeStruct((W, 128), i32),
            jax.ShapeDtypeStruct((CH, CH), f32),
        ),
        in_specs=[vm, hbm, hbm, hbm],
        out_specs=(hbm, vm, vm, vm, vm),
        scratch_shapes=[
            pltpu.VMEM((1, 128), i32),
            pltpu.VMEM((W, 1, 128), i32),
            pltpu.VMEM((2 * W, 128), i32),
            pltpu.SMEM((2 * W, 128), i32),
            pltpu.SMEM((W, 128), i32),
            pltpu.SMEM((2 * W, CH), i32),
            pltpu.VMEM((BLK, RB, F), bf),
            pltpu.VMEM((CW, F), bf),
            pltpu.VMEM((GW, CH), i32),
            pltpu.VMEM((CH, 2 * CH), f32),
            pltpu.VMEM((CW, F), f32),
            pltpu.VMEM((2, CH, F), f32),
            pltpu.VMEM((N, 2, RB, F), bf),
            pltpu.VMEM((2, RB, D), bf),
            pltpu.VMEM((2, W, CH, F), bf),
            pltpu.VMEM((2, N, CH, F), bf),
            pltpu.VMEM((2, CH, D), bf),
            pltpu.VMEM((2, N, CH, F), i16),
            pltpu.VMEM((2, N, 4, CH), f32),
            pltpu.VMEM((2, W, CH, F), i16),
            pltpu.VMEM((W, 4, CH), f32),
            pltpu.VMEM((CH, D), f32),
            dma((6,)),
            dma((W,)), dma((W,)),
            dma((N,)), dma((N,)),
            dma((2 * W,)), dma((2 * W,)),
            dma((2 * N,)), dma((2 * N,)),
            dma((2 * N,)), dma((2 * N,)),
            dma((2 * N,)), dma((2 * N,)),
            dma((2 * W,)), dma((2 * W,)),
            dma((W,)), dma((W,)),
            dma((2,)),
            pltpu.VMEM((W, CH, F), bf),
            pltpu.VMEM((W, CH, F), bf),
            pltpu.VMEM((N, CH, F), i16),
            pltpu.VMEM((N, CH, F), i16),
            pltpu.VMEM((N, 4, CH), f32),
            pltpu.VMEM((N, 4, CH), f32),
        ],
        compiler_params=pltpu.CompilerParams(
            collective_id=0, has_side_effects=True, vmem_limit_bytes=60 * 1024 * 1024
        ),
        name="exchange",
    )(ids, children, centroids, embeddings)


PARTS = 8
BATCH = 16


def scatter_kernel(
    kids_s, tab_s, q_hbm, sc_ref, factor_ref, cent_hbm, out_hbm,
    q_ref, cent_b, slots, acc, cent_sem, q_sem, out_sem,
):
    lane = lax.broadcasted_iota(jnp.int32, (CH, CH), 1)
    eye = lane == lax.broadcasted_iota(jnp.int32, (CH, CH), 0)
    per, rows_per = W // PARTS, CW // PARTS

    def cent_copy(i):
        rows = pl.ds(pl.multiple_of(i * rows_per, rows_per), rows_per)
        return pltpu.make_async_copy(cent_hbm.at[rows], cent_b.at[rows], cent_sem.at[i])

    def q_copy(i):
        rows = pl.ds(i * per, per)
        return pltpu.make_async_copy(q_hbm.at[rows], q_ref.at[rows], q_sem.at[i])

    def out_copy(i):
        rows = pl.ds(pl.multiple_of(i * rows_per, rows_per), rows_per)
        return pltpu.make_async_copy(acc.at[rows], out_hbm.at[rows], out_sem.at[i])

    @pl.loop(0, PARTS)
    def _(i):
        cent_copy(i).start()

    @pl.loop(0, PARTS)
    def _(i):
        q_copy(i).start()

    @pl.loop(0, PARTS)
    def _(i):
        cent_copy(i).wait()
        for t in range(4):
            step = rows_per // 4
            rows = pl.ds(pl.multiple_of(i * rows_per + t * step, step), step)
            acc[rows, :] = cent_b[rows, :].astype(jnp.float32)

    def add_batch(slot, base):
        at = [pl.ds(kids_s[slot, base + i], 1) for i in range(BATCH)]
        sums = [acc[at[i], :] + slots[slot, pl.ds(base + i, 1), :] for i in range(BATCH)]
        for i in range(BATCH):
            acc[at[i], :] = sums[i]

    def decode(s):
        for j in range(2):
            scale = jnp.sum(
                jnp.where(eye, sc_ref[s][2 * j : 2 * j + 1, :], 0.0), axis=1, keepdims=True
            )
            slots[j * W + s] = q_ref[s, j].astype(jnp.int32).astype(jnp.float32) * scale

    def add_slot(s, j):
        slot, twice = j * W + s, tab_s[s, 6 + j]

        @pl.when(twice == 0)
        def _():
            for g in range(CH // BATCH):
                add_batch(slot, g * BATCH)

        @pl.when(twice > 0)
        def _():
            @pl.loop(0, CH // BATCH)
            def _(g):
                base = pl.multiple_of(g * BATCH, BATCH)

                @pl.when(((twice >> g) & 1) == 0)
                def _():
                    add_batch(slot, base)

                @pl.when(((twice >> g) & 1) > 0)
                def _():
                    for i in range(BATCH):
                        at = pl.ds(kids_s[slot, base + i], 1)
                        acc[at, :] = acc[at, :] + slots[slot, pl.ds(base + i, 1), :]

    @pl.loop(0, PARTS)
    def _(i):
        q_copy(i).wait()

        for t in range(per):
            decode(i * per + t)

    @pl.loop(0, W)
    def _(s):
        for j in range(2):

            @pl.when(tab_s[s, 4 + j] > 0)
            def _():
                add_slot(s, j)

    factors = factor_ref[...]

    for i in range(PARTS):
        for h in range(i * (rows_per // CH), (i + 1) * (rows_per // CH)):
            rows = pl.ds(h * CH, CH)
            acc[rows, :] = acc[rows, :] * factors[:, h : h + 1]
        out_copy(i).start()

    @pl.loop(0, PARTS)
    def _(i):
        out_copy(i).wait()


def scatter(kids, table, q, scales, factors, centroids):
    vm = pl.BlockSpec(memory_space=pltpu.VMEM)
    sm = pl.BlockSpec(memory_space=pltpu.SMEM)
    hbm = pl.BlockSpec(memory_space=pl.ANY)
    return pl.pallas_call(
        scatter_kernel,
        out_shape=jax.ShapeDtypeStruct((CW, F), jnp.float32),
        in_specs=[sm, sm, hbm, vm, vm, hbm],
        out_specs=hbm,
        scratch_shapes=[
            pltpu.VMEM((W, 2, CH, F), jnp.int16),
            pltpu.VMEM((CW, F), jnp.bfloat16),
            pltpu.VMEM((2 * W, CH, F), jnp.float32),
            pltpu.VMEM((CW, F), jnp.float32),
            pltpu.SemaphoreType.DMA((PARTS,)),
            pltpu.SemaphoreType.DMA((PARTS,)),
            pltpu.SemaphoreType.DMA((PARTS,)),
        ],
        compiler_params=pltpu.CompilerParams(vmem_limit_bytes=60 * 1024 * 1024),
        name="scatter",
    )(kids, table, q, scales, factors, centroids)


def body(embeddings, centroids, level2_cluster_index, child_lists):
    ids = level2_cluster_index.reshape(1, BLK)
    q, scales, kids, table, factors = exchange(
        ids, child_lists, centroids, embeddings.reshape(BLK, RB, F)
    )
    return scatter(kids, table, q, scales, factors, centroids)


def solution(mesh):
    placed = (P("wide", "narrow"), P("wide", "narrow"), P("wide"), P("wide", None))
    return jax.shard_map(
        body, mesh=mesh, in_specs=placed, out_specs=P("wide", "narrow"), check_vma=False
    )
```
